32 devices in a mesh: tm: 2 (over core), height: 16 (over z, y, x).
Axes of the slice: x: 2, y: 2, z: 4, core: 2. Of those that a mesh axis runs over, the one named last changes fastest.
Arguments:
- features: bfloat16 [4, 64, 32, 192], P('tm', 'height'), may hold values from -6 to 6
- weight_one: bfloat16 [3, 3, 3, 192, 192], replicated, may hold values from -0.078125 to 0.078125
- bias_one: float32 [192], replicated, may hold values from -3 to 3
- gain_one: float32 [192], replicated, may hold values from 0.1 to 1.9
- weight_two: bfloat16 [3, 3, 3, 192, 192], replicated, may hold values from -0.078125 to 0.078125
- bias_two: float32 [192], replicated, may hold values from -3 to 3
- gain_two: float32 [192], replicated, may hold values from 0.1 to 1.9
- cotangent: bfloat16 [4, 64, 32, 192], P('tm', 'height'), may hold values from -6 to 6
Outputs:
- block_out: bfloat16 [4, 64, 32, 192], P('tm', 'height')
- grad_input: bfloat16 [4, 64, 32, 192], P('tm', 'height')
- grad_weight_one: bfloat16 [3, 3, 3, 192, 192], replicated
- grad_weight_two: bfloat16 [3, 3, 3, 192, 192], replicated
- grad_bias_one: bfloat16 [192], replicated
- grad_bias_two: bfloat16 [192], replicated
- grad_gain_one: bfloat16 [192], replicated
- grad_gain_two: bfloat16 [192], replicated
The draws below stay inside these ranges and needn't reach their ends.
All inputs are finite; a program needn't handle non-finite values.
Results may differ from the reference program's by a relative error of at most 0.013.
Values may be sent and summed in bfloat16 or wider, within the bound.
No kernel may reach another device: no remote copies, remote signals or barrier semaphores. Data moves between devices by JAX's collectives and lax.ppermute only.
A program may use at most 128 MiB of HBM per device.

```python
import jax
import jax.numpy as jnp
from jax import lax

C = 192
WIDTH = 32
FRAMES = 4
ROWS = 64


def block_levels(rng, extent, cuts, low, high):
    factor_of, own = 1.0, jax.random.fold_in(rng, 6)
    for axis_at, shards_of in cuts:
        heights = jnp.exp(jax.random.uniform(jax.random.fold_in(own, axis_at), (shards_of,), jnp.float32, low / len(cuts), high / len(cuts)))
        factor_of = factor_of * jnp.repeat(heights, extent[axis_at] // shards_of).reshape([-1 if axis == axis_at else 1 for axis in range(len(extent))])
    return factor_of


def scatter_about(own_key, dims, spread, reach, pieces=(), dtype=jnp.bfloat16):
    entries = spread * jax.random.normal(own_key, dims, jnp.float32)
    if pieces:
        entries = entries * block_levels(own_key, dims, pieces, -0.22, 0.18)
    return jnp.clip(entries, -reach, reach).astype(dtype)


def setup_inputs(seed: int = 0) -> dict:
    arg_keys = jax.random.split(jax.random.key(seed), 9)
    return {
        "features": scatter_about(arg_keys[0], (FRAMES, ROWS, WIDTH, C), 1.0, 6.0, ((0, 2), (1, 16))),
        "weight_one": scatter_about(arg_keys[1], (3, 3, 3, C, C), (27 * C) ** -0.5, 0.078125),
        "bias_one": scatter_about(arg_keys[2], (C,), 0.5, 3.0, (), jnp.float32),
        "gain_one": jnp.clip(1.0 + 0.18 * jax.random.normal(arg_keys[3], (C,), jnp.float32), 0.1, 1.9),
        "weight_two": scatter_about(arg_keys[4], (3, 3, 3, C, C), (27 * C) ** -0.5, 0.078125),
        "bias_two": scatter_about(arg_keys[5], (C,), 0.5, 3.0, (), jnp.float32),
        "gain_two": jnp.clip(1.0 + 0.18 * jax.random.normal(arg_keys[6], (C,), jnp.float32), 0.1, 1.9),
        "cotangent": scatter_about(arg_keys[7], (FRAMES, ROWS, WIDTH, C), 1.0, 6.0, ((0, 2), (1, 16))),
    }


epsilon = 1e-06

def norm_silu(values, gain):
    vals = values.astype(jnp.float32)
    scale = lax.rsqrt(lax.optimization_barrier(jnp.mean(vals * vals, axis=-1, keepdims=True)) + epsilon)
    normed = vals * scale
    lifted = normed * gain
    return lifted * jax.nn.sigmoid(lifted)

def norm_silu_back(grad, values, gain):
    vals = values.astype(jnp.float32)
    scale = lax.rsqrt(lax.optimization_barrier(jnp.mean(vals * vals, axis=-1, keepdims=True)) + epsilon)
    normed = vals * scale
    lifted = normed * gain
    sig = jax.nn.sigmoid(lifted)
    d_lift = grad * sig * (1.0 + lifted * (1.0 - sig))
    d_gain = lax.optimization_barrier(jnp.sum(d_lift * normed, axis=(0, 1, 2)))
    d_norm = d_lift * gain
    d_vals = scale * (d_norm - normed * lax.optimization_barrier(jnp.mean(d_norm * normed, axis=-1, keepdims=True)))
    return (d_vals, d_gain)

def taps_forward(padded, weight):
    frames = padded.shape[0] - 2
    rows = padded.shape[1] - 2
    cols = padded.shape[2] - 2
    chans = padded.shape[3]
    total = jnp.zeros((frames * rows * cols, weight.shape[4]), jnp.float32)
    for step_t in range(3):
        for step_h in range(3):
            for step_w in range(3):
                piece = padded[step_t:step_t + frames, step_h:step_h + rows, step_w:step_w + cols].reshape(-1, chans)
                total = total + jnp.dot(piece, weight[step_t, step_h, step_w], preferred_element_type=jnp.float32)
    return total.reshape(frames, rows, cols, weight.shape[4])

def taps_back(padded, weight):
    frames = padded.shape[0] - 2
    rows = padded.shape[1] - 2
    cols = padded.shape[2] - 2
    chans = padded.shape[3]
    total = jnp.zeros((frames * rows * cols, weight.shape[3]), jnp.float32)
    for step_t in range(3):
        for step_h in range(3):
            for step_w in range(3):
                piece = padded[2 - step_t:2 - step_t + frames, 2 - step_h:2 - step_h + rows, 2 - step_w:2 - step_w + cols].reshape(-1, chans)
                total = total + jnp.dot(piece, weight[step_t, step_h, step_w].T, preferred_element_type=jnp.float32)
    return total.reshape(frames, rows, cols, weight.shape[3])

def weight_grads(padded, grad):
    frames, rows, cols, chans = grad.shape
    flat_grad = grad.reshape(-1, chans)
    results = []
    for step_t in range(3):
        for step_h in range(3):
            for step_w in range(3):
                piece = padded[step_t:step_t + frames, step_h:step_h + rows, step_w:step_w + cols].reshape(-1, padded.shape[3])
                results.append(lax.dot_general(piece, flat_grad, (((0,), (0,)), ((), ())), preferred_element_type=jnp.float32))
    return jnp.stack(results).reshape(3, 3, 3, padded.shape[3], chans)

def pad_ahead(values):
    return jnp.pad(values, ((2, 0), (1, 1), (1, 1), (0, 0)))

def pad_behind(values):
    return jnp.pad(values, ((0, 2), (1, 1), (1, 1), (0, 0)))

def reference(features, weight_one, bias_one, gain_one, weight_two, bias_two, gain_two, cotangent):
    act_one = norm_silu(features, gain_one).astype(jnp.bfloat16)
    padded_one = pad_ahead(act_one)
    middle = (taps_forward(padded_one, weight_one) + bias_one).astype(jnp.bfloat16)
    act_two = norm_silu(middle, gain_two).astype(jnp.bfloat16)
    padded_two = pad_ahead(act_two)
    block_out = (features.astype(jnp.float32) + taps_forward(padded_two, weight_two) + bias_two).astype(jnp.bfloat16)
    grad_w_two = weight_grads(padded_two, cotangent)
    grad_b_two = lax.optimization_barrier(jnp.sum(cotangent.astype(jnp.float32), axis=(0, 1, 2)))
    grad_act_two = taps_back(pad_behind(cotangent), weight_two)
    grad_mid, grad_g_two = norm_silu_back(grad_act_two, middle, gain_two)
    grad_mid = grad_mid.astype(jnp.bfloat16)
    grad_b_one = lax.optimization_barrier(jnp.sum(grad_mid.astype(jnp.float32), axis=(0, 1, 2)))
    grad_w_one = weight_grads(padded_one, grad_mid)
    grad_act_one = taps_back(pad_behind(grad_mid), weight_one)
    grad_feat, grad_g_one = norm_silu_back(grad_act_one, features, gain_one)
    grad_input = (grad_feat + cotangent.astype(jnp.float32)).astype(jnp.bfloat16)
    return (block_out, grad_input, grad_w_one.astype(jnp.bfloat16), grad_w_two.astype(jnp.bfloat16), grad_b_one.astype(jnp.bfloat16), grad_b_two.astype(jnp.bfloat16), grad_g_one.astype(jnp.bfloat16), grad_g_two.astype(jnp.bfloat16))
```

```python
import functools

import jax
import jax.numpy as jnp
from jax import lax
from jax.experimental import pallas as pl
from jax.experimental.pallas import tpu as pltpu
from jax.sharding import PartitionSpec as P

epsilon = 1e-06
bf16 = jnp.bfloat16
f32 = jnp.float32


def shift_cols(value, by):
    zero = jnp.zeros_like(value[:, :1])
    if by == 1:
        return jnp.concatenate([value[:, 1:], zero], axis=1)
    return jnp.concatenate([zero, value[:, :-1]], axis=1)


def norm_parts(vals, gain):
    scale = lax.rsqrt(jnp.mean(vals * vals, axis=-1, keepdims=True) + epsilon)
    normed = vals * scale
    lifted = normed * gain
    return scale, normed, lifted, jax.nn.sigmoid(lifted)


def norm_silu(vals, gain):
    _, _, lifted, sig = norm_parts(vals, gain)
    return lifted * sig


def norm_silu_back(grad, vals, gain):
    scale, normed, lifted, sig = norm_parts(vals, gain)
    d_lift = grad * sig * (1.0 + lifted * (1.0 - sig))
    d_gain = jnp.sum(d_lift * normed, axis=0, keepdims=True)
    d_norm = d_lift * gain
    d_vals = scale * (d_norm - normed * jnp.mean(d_norm * normed, axis=-1, keepdims=True))
    return d_vals, d_gain


def conv(window, weight, frames, rows, back):
    cols, chans = window.shape[2], window.shape[3]
    parts = [None] * 3
    for t in range(3):
        for h in range(3):
            t0, h0 = (2 - t, 2 - h) if back else (t, h)
            piece = window[t0 : t0 + frames, h0 : h0 + rows].reshape(frames * rows * cols, chans)
            for k in range(3):
                dims = (((1,), (1 if back else 0,)), ((), ()))
                prod = lax.dot_general(piece, weight[t, h, k], dims, preferred_element_type=f32)
                parts[k] = prod if parts[k] is None else parts[k] + prod
    parts = [part.reshape(frames * rows, cols, chans) for part in parts]
    sign = -1 if back else 1
    total = parts[1] + shift_cols(parts[0], -sign) + shift_cols(parts[2], sign)
    return total.reshape(frames * rows * cols, chans)


def first_kernel(
    feat_ref, cot_ref, w1_ref, w2_ref, b1_ref, g1_ref, g2_ref, act1_ref, act2_ref, gmid_ref, sums_ref
):
    frames, rows, cols, chans = act2_ref.shape
    for f in range(frames + 2):
        vals = feat_ref[f].astype(f32).reshape(-1, chans)
        act1_ref[f] = norm_silu(vals, g1_ref[...]).astype(bf16).reshape(rows + 2, cols, chans)
    mid = (conv(act1_ref, w1_ref, frames, rows, False) + b1_ref[...]).astype(bf16).astype(f32)
    act2_ref[...] = norm_silu(mid, g2_ref[...]).astype(bf16).reshape(act2_ref.shape)
    grad = conv(cot_ref, w2_ref, frames, rows, True)
    gmid, d_gain = norm_silu_back(grad, mid, g2_ref[...])
    gmid = gmid.astype(bf16)
    gmid_ref[...] = gmid.reshape(gmid_ref.shape)
    cot = cot_ref[:frames, 1 : rows + 1].astype(f32).reshape(-1, chans)
    sums_ref[...] = jnp.concatenate(
        [
            d_gain,
            jnp.sum(gmid.astype(f32), axis=0, keepdims=True),
            jnp.sum(cot, axis=0, keepdims=True),
            jnp.zeros((5, chans), f32),
        ],
        axis=0,
    )


def last_kernel(
    act2_ref, gmid_ref, feat_ref, cot_ref, w1_ref, w2_ref, b2_ref, g1_ref, out_ref, gin_ref, sums_ref
):
    frames, rows, cols, chans = out_ref.shape
    feat = feat_ref[...].astype(f32).reshape(-1, chans)
    out = feat + conv(act2_ref, w2_ref, frames, rows, False) + b2_ref[...]
    out_ref[...] = out.astype(bf16).reshape(out_ref.shape)
    grad = conv(gmid_ref, w1_ref, frames, rows, True)
    d_vals, d_gain = norm_silu_back(grad, feat, g1_ref[...])
    gin = d_vals + cot_ref[...].astype(f32).reshape(-1, chans)
    gin_ref[...] = gin.astype(bf16).reshape(gin_ref.shape)
    sums_ref[...] = jnp.concatenate([d_gain, jnp.zeros((7, chans), f32)], axis=0)


def pack_rows(chans):
    return chans + chans // 2


def wgrad_kernel(x_ref, y_ref, out_ref, xk_ref):
    frames, rows, cols, chans = x_ref.shape
    cells = frames * rows * cols
    values = x_ref[...].astype(f32).reshape(frames * rows, cols, chans)
    xk_ref[0] = shift_cols(values, 1).astype(bf16).reshape(cells, chans)
    xk_ref[1] = x_ref[...].reshape(cells, chans)
    xk_ref[2] = shift_cols(values, -1).astype(bf16).reshape(cells, chans)
    step = pack_rows(chans)
    odd = lax.axis_index("tm") % 2 == 1
    dims = (((0,), (0,)), ((), ()))

    def store(tap, grad):
        grad = grad.astype(bf16)
        base = tap * step
        half = chans // 2
        out_ref[base : base + chans] = grad[:, :128]
        out_ref[base + chans : base + step] = jnp.concatenate(
            [grad[:half, 128:], grad[half:, 128:]], axis=1
        )

    for t in range(3):
        for h in range(3):
            piece = y_ref[t : t + frames, h : h + rows].reshape(cells, chans)

            @pl.when(odd)
            def _():
                for k in range(3):
                    grad = lax.dot_general(piece, xk_ref[k], dims, preferred_element_type=f32)
                    store((t * 3 + h) * 3 + k, grad)

            @pl.when(jnp.logical_not(odd))
            def _():
                for k in range(3):
                    grad = lax.dot_general(xk_ref[k], piece, dims, preferred_element_type=f32)
                    store(((2 - t) * 3 + 2 - h) * 3 + 2 - k, grad)

    used = 27 * step
    out_ref[used:] = jnp.zeros((out_ref.shape[0] - used, 128), bf16)


def unpack_kernel(one_ref, two_ref, out_one_ref, out_two_ref):
    chans = out_one_ref.shape[1]
    half = chans // 2
    for src, dst in ((one_ref, out_one_ref), (two_ref, out_two_ref)):
        low = src[:chans]
        high = src[chans:]
        dst[0, :, :128] = low
        dst[0, :half, 128:] = high[:, : chans - 128]
        dst[0, half:, 128:] = high[:, chans - 128 :]


def params(limit=50 * 2**20, **kw):
    return pltpu.CompilerParams(vmem_limit_bytes=limit, **kw)


vmem = pl.BlockSpec(memory_space=pltpu.VMEM)


def call(kernel, outs, args, flops, scratch=()):
    return pl.pallas_call(
        kernel,
        out_shape=outs,
        in_specs=[vmem] * len(args),
        out_specs=[vmem] * len(outs),
        scratch_shapes=list(scratch),
        compiler_params=params(),
        cost_estimate=pl.CostEstimate(flops=flops, bytes_accessed=8 * 2**20, transcendentals=0),
    )(*args)


def moved(value, axis, by):
    size = lax.axis_size(axis)
    return lax.ppermute(value, axis, [(i, i + by) for i in range(size) if 0 <= i + by < size])


def windows(ahead, behind):
    both = jnp.stack([ahead, behind])
    above = moved(both[:, :, -1:], "height", 1)
    below = moved(both[:, :, :1], "height", -1)
    both = jnp.concatenate([above, both, below], axis=2)
    earlier = moved(both[0, -2:], "tm", 1)
    later = moved(both[1, :2], "tm", -1)
    return jnp.concatenate([earlier, both[0]], axis=0), jnp.concatenate([both[1], later], axis=0)


def total_of(pieces):
    return functools.reduce(lambda a, b: a + b, [p.astype(f32) for p in pieces])


def piece_at(value, index):
    return lax.dynamic_index_in_dim(value, index, 0, keepdims=False)


def body(features, weight_one, bias_one, gain_one, weight_two, bias_two, gain_two, cotangent):
    frames, rows, cols, chans = features.shape
    tm, height = lax.axis_size("tm"), lax.axis_size("height")
    planes = height // 4
    c, me = lax.axis_index("tm"), lax.axis_index("height")
    p, q = me % 4, me // 4
    line = lambda v: v.reshape(1, chans)
    local = jax.ShapeDtypeStruct(features.shape, bf16)
    sums = jax.ShapeDtypeStruct((8, chans), f32)
    flops = 4 * frames * rows * cols * 27 * chans * chans

    feat_win, cot_win = windows(features, cotangent)
    act1_win, act2, gmid, sums_one = call(
        first_kernel,
        (jax.ShapeDtypeStruct(feat_win.shape, bf16), local, local, sums),
        (feat_win, cot_win, weight_one, weight_two, line(bias_one), line(gain_one), line(gain_two)),
        flops,
    )

    odd = c % 2 == 1
    swap = [(i, i ^ 1) for i in range(tm)]
    mine = jnp.where(odd, gmid, act2)
    other = lax.ppermute(jnp.where(odd, act2, gmid), "tm", swap)
    x_pair = jnp.where(odd, jnp.concatenate([other, mine]), jnp.concatenate([mine, other]))
    edge = lax.ppermute(jnp.where(odd, cot_win[-2:], feat_edge(act1_win)), "tm", swap)
    y_pair = jnp.where(
        odd, jnp.concatenate([edge, act1_win]), jnp.concatenate([cot_win, edge])
    )
    unit = 4 * planes * 16
    flat_rows = -(-27 * pack_rows(chans) // unit) * unit
    (flat,) = call(
        wgrad_kernel,
        (jax.ShapeDtypeStruct((flat_rows, 128), bf16),),
        (x_pair, y_pair),
        flops,
        [pltpu.VMEM((3, 2 * frames * rows * cols, chans), bf16)],
    )

    act2_win, gmid_win = windows(act2, gmid)
    block_out, grad_input, sums_two = call(
        last_kernel,
        (local, local, sums),
        (act2_win, gmid_win, features, cotangent, weight_one, weight_two, line(bias_two), line(gain_one)),
        flops,
    )
    small = lax.psum(jnp.concatenate([sums_one, sums_two]), ("tm", "height")).astype(bf16)

    def plane_move(value, d):
        return lax.ppermute(value, "height", [(i, i ^ d) for i in range(height)])

    def column_move(value, d):
        pairs = [(z * 4 + j, (z + d) % planes * 4 + j) for z in range(planes) for j in range(4)]
        return lax.ppermute(value, "height", pairs)

    flat = flat.reshape(4, flat_rows // 4, 128)
    arrived = [plane_move(piece_at(flat, p ^ d), d) for d in (1, 2, 3)]
    part = total_of([piece_at(flat, p), *arrived]).astype(bf16)
    part = part.reshape(planes, -1, 128)
    arrived = [column_move(piece_at(part, (q + d) % planes), d) for d in range(1, planes)]
    part = total_of([piece_at(part, q), *arrived])
    step = 2
    while step < tm:
        part = part + lax.ppermute(part, "tm", [(i, i ^ step) for i in range(tm)])
        step *= 2
    part = part.astype(bf16)

    got = [part] + [column_move(part, d) for d in range(1, planes)]
    stack = jnp.stack(got)
    order = (q - jnp.arange(planes)) % planes
    quarter = jnp.take(stack, order, axis=0).reshape(-1, 128)
    got = [quarter] + [plane_move(quarter, d) for d in (1, 2, 3)]
    other = [lax.ppermute(g, "tm", swap) for g in got]

    def ordered(pieces):
        stack = jnp.stack(pieces)
        return jnp.take(stack, jnp.arange(4) ^ p, axis=0).reshape(-1, 128)

    mine, other = ordered(got), ordered(other)
    flat_one, flat_two = jnp.where(odd, mine, other), jnp.where(odd, other, mine)
    step = pack_rows(chans)
    taps = jax.ShapeDtypeStruct((27, chans, chans), bf16)
    grad_one, grad_two = pl.pallas_call(
        unpack_kernel,
        grid=(27,),
        out_shape=(taps, taps),
        in_specs=[pl.BlockSpec((step, 128), lambda i: (i, 0))] * 2,
        out_specs=[pl.BlockSpec((1, chans, chans), lambda i: (i, 0, 0))] * 2,
        compiler_params=params(),
    )(flat_one, flat_two)
    shape = weight_one.shape
    return (
        block_out,
        grad_input,
        grad_one.reshape(shape),
        grad_two.reshape(shape),
        small[1],
        small[2],
        small[8],
        small[0],
    )


def feat_edge(act1_win):
    return act1_win[:2]


def solution(mesh):
    split = P("tm", "height", None, None)
    return jax.shard_map(
        body,
        mesh=mesh,
        in_specs=(split, P(), P(), P(), P(), P(), P(), split),
        out_specs=(split, split, P(), P(), P(), P(), P(), P()),
        check_vma=False,
    )
```

```python
import functools

import jax
import jax.numpy as jnp
from jax import lax
from jax.experimental import pallas as pl
from jax.experimental.pallas import tpu as pltpu
from jax.sharding import PartitionSpec as P

epsilon = 1e-06
bf16 = jnp.bfloat16
f32 = jnp.float32
chunks = ((0, 4), (4, 3))
taps_each = 7
taps_all = 27


def shift_cols(value, by):
    zero = jnp.zeros_like(value[:, :1])
    if by == 1:
        return jnp.concatenate([value[:, 1:], zero], axis=1)
    return jnp.concatenate([zero, value[:, :-1]], axis=1)


def norm_parts(vals, gain):
    scale = lax.rsqrt(jnp.mean(vals * vals, axis=-1, keepdims=True) + epsilon)
    normed = vals * scale
    lifted = normed * gain
    return scale, normed, lifted, jax.nn.sigmoid(lifted)


def norm_silu(vals, gain):
    _, _, lifted, sig = norm_parts(vals, gain)
    return lifted * sig


def norm_silu_back(grad, vals, gain):
    scale, normed, lifted, sig = norm_parts(vals, gain)
    d_lift = grad * sig * (1.0 + lifted * (1.0 - sig))
    d_gain = jnp.sum(d_lift * normed, axis=0, keepdims=True)
    d_norm = d_lift * gain
    d_vals = scale * (d_norm - normed * jnp.mean(d_norm * normed, axis=-1, keepdims=True))
    return d_vals, d_gain


def conv(window, weight, frames, rows, back):
    cols, chans = window.shape[2], window.shape[3]
    parts = [None] * 3
    for t in range(3):
        for h in range(3):
            t0, h0 = (2 - t, 2 - h) if back else (t, h)
            piece = window[t0 : t0 + frames, h0 : h0 + rows].reshape(frames * rows * cols, chans)
            for k in range(3):
                dims = (((1,), (1 if back else 0,)), ((), ()))
                prod = lax.dot_general(piece, weight[t, h, k], dims, preferred_element_type=f32)
                parts[k] = prod if parts[k] is None else parts[k] + prod
    parts = [part.reshape(frames * rows, cols, chans) for part in parts]
    sign = -1 if back else 1
    total = parts[1] + shift_cols(parts[0], -sign) + shift_cols(parts[2], sign)
    return total.reshape(frames * rows * cols, chans)


def fill(window, first, second, above, below):
    count, rows = first.shape[0], first.shape[1]
    window[:count, 1 : rows + 1] = first[...]
    window[count:, 1 : rows + 1] = second[...]
    window[:, :1] = above
    window[:, rows + 1 :] = below


def first_kernel(
    feat_ref, earlier_ref, cot_ref, later_ref, above_ref, below_ref, w1_ref, w2_ref, b1_ref, g1_ref, g2_ref,
    act2_ref, gmid_ref, give_ref, keep_ref, sums_ref, ahead, behind,
):
    frames, rows, cols, chans = act2_ref.shape
    half = frames + 2
    fill(ahead, earlier_ref, feat_ref, above_ref[:half], below_ref[:half])
    fill(behind, cot_ref, later_ref, above_ref[half:], below_ref[half:])
    for f in range(half):
        vals = ahead[f].astype(f32).reshape(-1, chans)
        ahead[f] = norm_silu(vals, g1_ref[...]).astype(bf16).reshape(rows + 2, cols, chans)
    mid = (conv(ahead, w1_ref, frames, rows, False) + b1_ref[...]).astype(bf16).astype(f32)
    act2 = norm_silu(mid, g2_ref[...]).astype(bf16).reshape(act2_ref.shape)
    act2_ref[...] = act2
    grad = conv(behind, w2_ref, frames, rows, True)
    gmid, d_gain = norm_silu_back(grad, mid, g2_ref[...])
    gmid = gmid.astype(bf16)
    cot = cot_ref[...].astype(f32).reshape(-1, chans)
    sums_ref[...] = jnp.concatenate(
        [
            d_gain,
            jnp.sum(gmid.astype(f32), axis=0, keepdims=True),
            jnp.sum(cot, axis=0, keepdims=True),
            jnp.zeros((5, chans), f32),
        ],
        axis=0,
    )
    gmid = gmid.reshape(gmid_ref.shape)
    gmid_ref[...] = gmid
    odd = lax.axis_index("tm") % 2 == 1

    @pl.when(odd)
    def _():
        give_ref[...] = act2
        keep_ref[...] = gmid

    @pl.when(jnp.logical_not(odd))
    def _():
        give_ref[...] = gmid
        keep_ref[...] = act2


def last_kernel(
    act2_ref, earlier_ref, gmid_ref, later_ref, above_ref, below_ref, feat_ref, cot_ref, w1_ref, w2_ref, b2_ref, g1_ref,
    out_ref, gin_ref, sums_ref, ahead, behind,
):
    frames, rows, cols, chans = out_ref.shape
    half = frames + 2
    fill(ahead, earlier_ref, act2_ref, above_ref[:half], below_ref[:half])
    fill(behind, gmid_ref, later_ref, above_ref[half:], below_ref[half:])
    feat = feat_ref[...].astype(f32).reshape(-1, chans)
    out = feat + conv(ahead, w2_ref, frames, rows, False) + b2_ref[...]
    out_ref[...] = out.astype(bf16).reshape(out_ref.shape)
    grad = conv(behind, w1_ref, frames, rows, True)
    d_vals, d_gain = norm_silu_back(grad, feat, g1_ref[...])
    gin = d_vals + cot_ref[...].astype(f32).reshape(-1, chans)
    gin_ref[...] = gin.astype(bf16).reshape(gin_ref.shape)
    sums_ref[...] = jnp.concatenate([d_gain, jnp.zeros((7, chans), f32)], axis=0)


def pack_rows(chans):
    return chans + chans // 2


def wgrad_kernel(blocks, taps, *refs):
    xs, ys = refs[:4], refs[4:8]
    gain_ref, out_ref, plane, xk = refs[8:]
    two, rows, cols, _ = ys[0].shape
    chans = gain_ref.shape[1]
    tall = 4 * rows
    cells = 2 * two * tall * cols
    odd = lax.axis_index("tm") % 2 == 1
    p = lax.axis_index("height") % 4
    single = blocks == 2
    start = jnp.where(odd, 2, 0) if single else 0
    if single:
        plane[pl.ds(jnp.where(odd, 0, 4), 2)] = jnp.zeros((2,) + plane.shape[1:], bf16)

    def put_y(values, row, count):
        for b in range(blocks):
            part = values[..., b * chans : (b + 1) * chans]
            place = (pl.ds(start + 2 * b, 2), pl.ds(row, count))

            @pl.when(odd)
            def _():
                flat = part.astype(f32).reshape(-1, chans)
                plane[place] = norm_silu(flat, gain_ref[...]).astype(bf16).reshape(part.shape)

            @pl.when(jnp.logical_not(odd))
            def _():
                plane[place] = part

    for d in range(4):
        at = p ^ d
        put_y(ys[d][...], 1 + rows * at, rows)
        for b in range(2):
            part = xs[d][:, :rows, :, b * chans : (b + 1) * chans]
            wide = part.astype(f32).reshape(two * rows, cols, chans)
            place = (pl.ds(2 * b, 2), pl.ds(rows * at, rows))
            xk[(0,) + place] = shift_cols(wide, 1).astype(bf16).reshape(part.shape)
            xk[(1,) + place] = part
            xk[(2,) + place] = shift_cols(wide, -1).astype(bf16).reshape(part.shape)

        @pl.when(at == 0)
        def _():
            put_y(xs[d][:, rows:, :, : blocks * chans], 0, 1)

        @pl.when(at == 3)
        def _():
            put_y(xs[d][:, rows:, :, : blocks * chans], tall + 1, 1)

    step = pack_rows(chans)
    dims = (((0,), (0,)), ((), ()))
    first, count = taps
    half = chans // 2

    def store(base, grad):
        grad = grad.astype(bf16)
        out_ref[base : base + chans] = grad[:, :128]
        out_ref[base + chans : base + step] = jnp.concatenate(
            [grad[:half, 128:], grad[half:, 128:]], axis=1
        )

    for j in range(count):
        tap = jnp.minimum(p * taps_each + first + j, taps_all - 1)
        t, h, k = tap // 9, tap // 3 % 3, tap % 3

        @pl.when(odd)
        def _():
            piece = plane[pl.ds(t, 4), pl.ds(h, tall)].reshape(cells, chans)
            x = xk[k].reshape(cells, chans)
            store(j * step, lax.dot_general(piece, x, dims, preferred_element_type=f32))

        @pl.when(jnp.logical_not(odd))
        def _():
            piece = plane[pl.ds(2 - t, 4), pl.ds(2 - h, tall)].reshape(cells, chans)
            x = xk[2 - k].reshape(cells, chans)
            store(j * step, lax.dot_general(x, piece, dims, preferred_element_type=f32))

    used = count * step
    if used < out_ref.shape[0]:
        out_ref[used:] = jnp.zeros((out_ref.shape[0] - used, 128), bf16)


def unpack_kernel(*refs):
    outs = refs[-2:]
    chans = outs[0].shape[1]
    half = chans // 2
    step = pack_rows(chans)
    odd = lax.axis_index("tm") % 2 == 1
    p = lax.axis_index("height") % 4
    at = 0
    for first, count in chunks:
        for own in (True, False):
            for d in range(4):
                src = refs[at]
                at += 1
                for j in range(count):
                    tap = (p ^ d) * taps_each + first + j
                    low = src[j * step : j * step + chans]
                    high = src[j * step + chans : (j + 1) * step]
                    for which in range(2):
                        mine = odd if which == 0 else jnp.logical_not(odd)
                        cond = mine if own else jnp.logical_not(mine)

                        @pl.when(jnp.logical_and(cond, tap < taps_all))
                        def _():
                            dst = outs[which].at[tap]
                            dst[:, :128] = low
                            dst[:half, 128:] = high[:, : chans - 128]
                            dst[half:, 128:] = high[:, chans - 128 :]


vmem = pl.BlockSpec(memory_space=pltpu.VMEM)


def call(kernel, outs, args, flops, scratch=()):
    return pl.pallas_call(
        kernel,
        out_shape=outs,
        in_specs=[vmem] * len(args),
        out_specs=[vmem] * len(outs),
        scratch_shapes=list(scratch),
        compiler_params=pltpu.CompilerParams(vmem_limit_bytes=50 * 2**20),
        cost_estimate=pl.CostEstimate(flops=flops, bytes_accessed=8 * 2**20, transcendentals=0),
    )(*args)


def moved(value, axis, by):
    size = lax.axis_size(axis)
    return lax.ppermute(value, axis, [(i, i + by) for i in range(size) if 0 <= i + by < size])


def frame_parts(ahead, behind):
    return moved(ahead[-2:], "tm", 1), moved(behind[:2], "tm", -1)


def row_parts(ahead, earlier, behind, later):
    all_of = (earlier, ahead, behind, later)
    above = moved(jnp.concatenate([v[:, -1:] for v in all_of]), "height", 1)
    below = moved(jnp.concatenate([v[:, :1] for v in all_of]), "height", -1)
    return above, below


def total_of(pieces):
    return functools.reduce(lambda a, b: a + b, [p.astype(f32) for p in pieces])


def piece_at(value, index):
    return lax.dynamic_index_in_dim(value, index, 0, keepdims=False)


def body(features, weight_one, bias_one, gain_one, weight_two, bias_two, gain_two, cotangent):
    frames, rows, cols, chans = features.shape
    tm, height = lax.axis_size("tm"), lax.axis_size("height")
    planes = height // 4
    c, me = lax.axis_index("tm"), lax.axis_index("height")
    odd = c % 2 == 1
    p, q = me % 4, me // 4
    swap = [(i, i ^ 1) for i in range(tm)]
    line = lambda v: v.reshape(1, chans)
    local = jax.ShapeDtypeStruct(features.shape, bf16)
    sums = jax.ShapeDtypeStruct((8, chans), f32)
    flops = 4 * frames * rows * cols * 27 * chans * chans
    window = pltpu.VMEM((frames + 2, rows + 2, cols, chans), bf16)

    def plane_move(value, d):
        return lax.ppermute(value, "height", [(i, i ^ d) for i in range(height)])

    def column_move(value, d):
        pairs = [(z * 4 + j, (z + d) % planes * 4 + j) for z in range(planes) for j in range(4)]
        return lax.ppermute(value, "height", pairs)

    def lanes(odd_blocks, even_blocks):
        return jnp.where(odd, jnp.concatenate(odd_blocks, -1), jnp.concatenate(even_blocks, -1))

    earlier, later = frame_parts(features, cotangent)
    above, below = row_parts(features, earlier, cotangent, later)

    odd_blocks = [(earlier, above[:2], below[:2]), (features, above[2:4], below[2:4])]
    even_blocks = [(cotangent, above[4:6], below[4:6]), (later, above[6:], below[6:])]
    if tm > 2:
        extra = tuple(
            lax.ppermute(jnp.where(odd, b, a), "tm", swap) for a, b in zip(odd_blocks[0], even_blocks[1])
        )
        odd_blocks, even_blocks = [extra, *odd_blocks], [*even_blocks, extra]
    blocks = len(odd_blocks)
    y_own = lanes([b[0] for b in odd_blocks], [b[0] for b in even_blocks])
    ys = [y_own] + [plane_move(y_own, d) for d in (1, 2, 3)]
    edge_above = lanes([b[1] for b in odd_blocks], [b[1] for b in even_blocks])
    edge_below = lanes([b[2] for b in odd_blocks], [b[2] for b in even_blocks])
    edge = jnp.where(p == 0, edge_above, edge_below)

    act2, gmid, give, keep, sums_one = call(
        first_kernel,
        (local, local, local, local, sums),
        (
            features, earlier, cotangent, later, above, below,
            weight_one, weight_two, line(bias_one), line(gain_one), line(gain_two),
        ),
        flops,
        [window, window],
    )
    other = lax.ppermute(give, "tm", swap)
    x_own = lanes([other, keep], [keep, other])
    if blocks > 2:
        x_own = jnp.pad(x_own, ((0, 0), (0, 0), (0, 0), (0, (blocks - 2) * chans)))
    x_own = jnp.concatenate([x_own, edge], axis=1)
    xs = [x_own] + [plane_move(x_own, d) for d in (1, 2, 3)]

    earlier2, later2 = frame_parts(act2, gmid)
    above2, below2 = row_parts(act2, earlier2, gmid, later2)

    step = pack_rows(chans)
    unit = 16 * planes
    cells = (2 * frames, 4 * rows, cols, chans)
    parts = []
    for taps in chunks:
        packed = -(-taps[1] * step // unit) * unit
        (flat,) = call(
            functools.partial(wgrad_kernel, blocks, taps),
            (jax.ShapeDtypeStruct((packed, 128), bf16),),
            (*xs, *ys, line(gain_one)),
            flops // 2,
            [
                pltpu.VMEM((2 * frames + 2, 4 * rows + 2, cols, chans), bf16),
                pltpu.VMEM((3, *cells), bf16),
            ],
        )
        flat = flat.reshape(planes, packed // planes, 128)
        arrived = [column_move(piece_at(flat, (q + d) % planes), d) for d in range(1, planes)]
        part = total_of([piece_at(flat, q), *arrived])
        hop = 2
        while hop < tm:
            part = part + lax.ppermute(part, "tm", [(i, i ^ hop) for i in range(tm)])
            hop *= 2
        parts.append(part.astype(bf16))

    block_out, grad_input, sums_two = call(
        last_kernel,
        (local, local, sums),
        (
            act2, earlier2, gmid, later2, above2, below2, features, cotangent,
            weight_one, weight_two, line(bias_two), line(gain_one),
        ),
        flops,
        [window, window],
    )

    small = jnp.concatenate([sums_one[:3], sums_two[:1]]).reshape(-1, 128)
    count = small.shape[0]

    def with_small(value, small):
        high = small.astype(bf16)
        low = (small - high.astype(f32)).astype(bf16)
        pad = jnp.zeros((-2 * count % 16, 128), bf16)
        return jnp.concatenate([value, high, low, pad])

    def without_small(pieces, rows):
        total = total_of([v[rows : rows + count].astype(f32) + v[rows + count : rows + 2 * count].astype(f32) for v in pieces])
        return [v[:rows] for v in pieces], total

    hop = 2
    while hop < tm:
        small = small + lax.ppermute(small, "tm", [(i, i ^ hop) for i in range(tm)])
        hop *= 2

    final = []
    for n, part in enumerate(parts):
        last = n == len(parts) - 1
        size = part.shape[0]
        send = with_small(part, small) if last else part
        got = [send] + [column_move(send, d) for d in range(1, planes)]
        if last:
            got, small = without_small(got, size)
        stack = jnp.stack(got)
        quarter = jnp.take(stack, (q - jnp.arange(planes)) % planes, axis=0).reshape(-1, 128)
        size = quarter.shape[0]
        send = with_small(quarter, small) if last else quarter
        got = [send] + [plane_move(send, d) for d in (1, 2, 3)]
        others = [lax.ppermute(g, "tm", swap) for g in got]
        if last:
            _, small = without_small(got + others, size)
        final += [*got, *others]

    gradient = jax.ShapeDtypeStruct((taps_all, chans, chans), bf16)
    grad_one, grad_two = call(unpack_kernel, (gradient, gradient), final, 0)
    shape = weight_one.shape
    small = small.reshape(4, chans).astype(bf16)
    return (
        block_out,
        grad_input,
        grad_one.reshape(shape),
        grad_two.reshape(shape),
        small[1],
        small[2],
        small[3],
        small[0],
    )


def solution(mesh):
    split = P("tm", "height", None, None)
    return jax.shard_map(
        body,
        mesh=mesh,
        in_specs=(split, P(), P(), P(), P(), P(), P(), split),
        out_specs=(split, split, P(), P(), P(), P(), P(), P()),
        check_vma=False,
    )
```

```python
import functools

import jax
import jax.numpy as jnp
from jax import lax
from jax.experimental import pallas as pl
from jax.experimental.pallas import tpu as pltpu
from jax.sharding import PartitionSpec as P

epsilon = 1e-06
bf16 = jnp.bfloat16
f32 = jnp.float32
chunks = ((0, 3), (3, 4))
taps_each = 7
taps_all = 27


def shift_cols(value, by):
    zero = jnp.zeros_like(value[:, :1])
    if by == 1:
        return jnp.concatenate([value[:, 1:], zero], axis=1)
    return jnp.concatenate([zero, value[:, :-1]], axis=1)


def norm_parts(vals, gain):
    scale = lax.rsqrt(jnp.mean(vals * vals, axis=-1, keepdims=True) + epsilon)
    normed = vals * scale
    lifted = normed * gain
    return scale, normed, lifted, jax.nn.sigmoid(lifted)


def norm_silu(vals, gain):
    _, _, lifted, sig = norm_parts(vals, gain)
    return lifted * sig


def norm_silu_back(grad, vals, gain):
    scale, normed, lifted, sig = norm_parts(vals, gain)
    d_lift = grad * sig * (1.0 + lifted * (1.0 - sig))
    d_gain = jnp.sum(d_lift * normed, axis=0, keepdims=True)
    d_norm = d_lift * gain
    d_vals = scale * (d_norm - normed * jnp.mean(d_norm * normed, axis=-1, keepdims=True))
    return d_vals, d_gain


def conv(window, weight, frames, rows, back):
    cols, chans = window.shape[2], window.shape[3]
    parts = [None] * 3
    for t in range(3):
        for h in range(3):
            t0, h0 = (2 - t, 2 - h) if back else (t, h)
            piece = window[t0 : t0 + frames, h0 : h0 + rows].reshape(frames * rows * cols, chans)
            for k in range(3):
                dims = (((1,), (1 if back else 0,)), ((), ()))
                prod = lax.dot_general(piece, weight[t, h, k], dims, preferred_element_type=f32)
                parts[k] = prod if parts[k] is None else parts[k] + prod
    parts = [part.reshape(frames * rows, cols, chans) for part in parts]
    sign = -1 if back else 1
    total = parts[1] + shift_cols(parts[0], -sign) + shift_cols(parts[2], sign)
    return total.reshape(frames * rows * cols, chans)


def fill_rows(window, at, edges, row):
    chans = window.shape[3]
    for f in range(2):
        window[at + f, row] = edges[:, f * chans : (f + 1) * chans]


def fill_edges(ahead, behind, above, below, passed_ahead, passed_behind):
    last = ahead.shape[1] - 1
    for row, own, i in ((0, above, 0), (last, below, 1)):
        fill_rows(ahead, 2, own[0], row)
        fill_rows(behind, 0, own[1], row)
        fill_rows(ahead, 0, passed_ahead[i], row)
        fill_rows(behind, 2, passed_behind[i], row)


def fill_packed(window, at, packed):
    rows, chans = packed.shape[0], window.shape[3]
    for f in range(2):
        window[at + f, 1 : rows + 1] = packed[..., f * chans : (f + 1) * chans]


def started(copies, sems):
    made = [pltpu.make_async_copy(src, dst, sems.at[i]) for i, (src, dst) in enumerate(copies)]
    for copy in made:
        copy.start()
    return made


def pack_frames(values):
    return jnp.concatenate([values[0], values[1]], axis=-1)


def first_kernel(
    feat_any, earlier_any, cot_any, later_any, above_ref, below_ref, pa_ref, pb_ref, w1_any, w2_any, b1_any, g1_any, g2_any,
    act2_ref, gmid_ref, give_ref, keep_ref, sums_ref, ahead, behind, w1, w2, b1, g1, g2, sems,
):
    frames, rows, cols, chans = feat_any.shape
    own = pl.ds(1, rows)
    copies = started(
        (
            (feat_any, ahead.at[pl.ds(2, 2), own]),
            (earlier_any, ahead.at[pl.ds(0, 2), own]),
            (g1_any, g1),
            (w1_any, w1),
            (b1_any, b1),
            (g2_any, g2),
            (cot_any, behind.at[pl.ds(0, 2), own]),
            (later_any, behind.at[pl.ds(2, 2), own]),
            (w2_any, w2),
        ),
        sems,
    )
    fill_edges(ahead, behind, above_ref, below_ref, pa_ref, pb_ref)
    for copy in copies[:3]:
        copy.wait()
    for f in range(frames + 2):
        vals = ahead[f].astype(f32).reshape(-1, chans)
        ahead[f] = norm_silu(vals, g1[...]).astype(bf16).reshape(rows + 2, cols, chans)
    for copy in copies[3:6]:
        copy.wait()
    mid = (conv(ahead, w1, frames, rows, False) + b1[...]).astype(bf16).astype(f32)
    act2 = norm_silu(mid, g2[...]).astype(bf16).reshape(frames, rows, cols, chans)
    act2 = pack_frames(act2)
    act2_ref[...] = act2
    for copy in copies[6:]:
        copy.wait()
    grad = conv(behind, w2, frames, rows, True)
    gmid, d_gain = norm_silu_back(grad, mid, g2[...])
    gmid = gmid.astype(bf16)
    cot = behind[:2, 1 : rows + 1].astype(f32).reshape(-1, chans)
    sums_ref[...] = jnp.concatenate(
        [
            d_gain,
            jnp.sum(gmid.astype(f32), axis=0, keepdims=True),
            jnp.sum(cot, axis=0, keepdims=True),
            jnp.zeros((5, chans), f32),
        ],
        axis=0,
    )
    gmid = pack_frames(gmid.reshape(frames, rows, cols, chans))
    gmid_ref[...] = gmid
    odd = lax.axis_index("tm") % 2 == 1

    @pl.when(odd)
    def _():
        give_ref[...] = act2
        keep_ref[...] = gmid

    @pl.when(jnp.logical_not(odd))
    def _():
        give_ref[...] = gmid
        keep_ref[...] = act2


def last_kernel(
    act2_ref, earlier_ref, gmid_ref, later_ref, above_ref, below_ref, pa_ref, pb_ref,
    feat_any, cot_any, w1_any, w2_any, b2_any, g1_any,
    out_ref, gin_ref, sums_ref, ahead, behind, feat, cot, w1, w2, b2, g1, sems,
):
    frames, rows, cols, chans = out_ref.shape
    copies = started(
        ((w2_any, w2), (b2_any, b2), (feat_any, feat), (w1_any, w1), (cot_any, cot), (g1_any, g1)), sems
    )
    fill_packed(ahead, 0, earlier_ref)
    fill_packed(ahead, 2, act2_ref)
    fill_packed(behind, 0, gmid_ref)
    fill_packed(behind, 2, later_ref)
    fill_edges(ahead, behind, above_ref, below_ref, pa_ref, pb_ref)
    for copy in copies[:3]:
        copy.wait()
    values = feat[...].astype(f32).reshape(-1, chans)
    out = values + conv(ahead, w2, frames, rows, False) + b2[...]
    out_ref[...] = out.astype(bf16).reshape(out_ref.shape)
    for copy in copies[3:]:
        copy.wait()
    grad = conv(behind, w1, frames, rows, True)
    d_vals, d_gain = norm_silu_back(grad, values, g1[...])
    gin = d_vals + cot[...].astype(f32).reshape(-1, chans)
    gin_ref[...] = gin.astype(bf16).reshape(gin_ref.shape)
    sums_ref[...] = jnp.concatenate([d_gain, jnp.zeros((7, chans), f32)], axis=0)


def pack_rows(chans):
    return chans + chans // 2


def wgrad_kernel(blocks, taps, passes, *refs):
    xs, ys = refs[:4], refs[4:8]
    gain_ref, refs = refs[8], refs[9:]
    if passes:
        (one_ref, two_ref, out_ref, up_ref, down_ref), refs = refs[:5], refs[5:]
        for i, ref in enumerate((one_ref, two_ref)):
            up_ref[i] = ref[ref.shape[0] - 1]
            down_ref[i] = ref[0]
    else:
        out_ref, refs = refs[0], refs[1:]
    plane, xk = refs
    _, rows, cols, _ = ys[0].shape
    chans = gain_ref.shape[1]
    tall = 4 * rows
    cells = 4 * tall * cols
    odd = lax.axis_index("tm") % 2 == 1
    p = lax.axis_index("height") % 4
    single = blocks == 2
    start = jnp.where(odd, 2, 0) if single else 0
    if single:
        plane[pl.ds(jnp.where(odd, 0, 4), 2)] = jnp.zeros((2,) + plane.shape[1:], bf16)

    def put_y(values, row, count):
        for b in range(blocks):
            for f in range(2):
                part = values[b, :, :, f * chans : (f + 1) * chans]
                place = (start + 2 * b + f, pl.ds(row, count))

                @pl.when(odd)
                def _():
                    flat = part.astype(f32).reshape(-1, chans)
                    plane[place] = norm_silu(flat, gain_ref[...]).astype(bf16).reshape(part.shape)

                @pl.when(jnp.logical_not(odd))
                def _():
                    plane[place] = part

    for d in range(4):
        at = p ^ d
        put_y(ys[d][...], 1 + rows * at, rows)
        for b in range(2):
            for f in range(2):
                part = xs[d][b, :rows, :, f * chans : (f + 1) * chans]
                wide = part.astype(f32)
                place = (2 * b + f, pl.ds(rows * at, rows))
                xk[(0,) + place] = shift_cols(wide, 1).astype(bf16)
                xk[(1,) + place] = part
                xk[(2,) + place] = shift_cols(wide, -1).astype(bf16)

        @pl.when(at == 0)
        def _():
            put_y(xs[d][:, rows:], 0, 1)

        @pl.when(at == 3)
        def _():
            put_y(xs[d][:, rows:], tall + 1, 1)

    step = pack_rows(chans)
    dims = (((0,), (0,)), ((), ()))
    first, count = taps
    half = chans // 2

    def store(base, grad):
        grad = grad.astype(bf16)
        out_ref[base : base + chans] = grad[:, :128]
        out_ref[base + chans : base + step] = jnp.concatenate(
            [grad[:half, 128:], grad[half:, 128:]], axis=1
        )

    for j in range(count):
        tap = jnp.minimum(p * taps_each + first + j, taps_all - 1)
        t, h, k = tap // 9, tap // 3 % 3, tap % 3

        @pl.when(odd)
        def _():
            piece = plane[pl.ds(t, 4), pl.ds(h, tall)].reshape(cells, chans)
            x = xk[k].reshape(cells, chans)
            store(j * step, lax.dot_general(piece, x, dims, preferred_element_type=f32))

        @pl.when(jnp.logical_not(odd))
        def _():
            piece = plane[pl.ds(2 - t, 4), pl.ds(2 - h, tall)].reshape(cells, chans)
            x = xk[2 - k].reshape(cells, chans)
            store(j * step, lax.dot_general(x, piece, dims, preferred_element_type=f32))

    used = count * step
    if used < out_ref.shape[0]:
        out_ref[used:] = jnp.zeros((out_ref.shape[0] - used, 128), bf16)


def unpack_kernel(taps, held, *refs):
    pieces = refs[:8]
    outs, stage, sems = refs[8 + 2 * held : 10 + 2 * held], refs[-2], refs[-1]
    first, count = taps
    chans = stage.shape[1]
    half = chans // 2
    step = pack_rows(chans)
    odd = lax.axis_index("tm") % 2 == 1
    p = lax.axis_index("height") % 4
    made = []
    for n, src in enumerate(pieces):
        for j in range(count):
            tap = (p ^ (n % 4)) * taps_each + first + j
            slot = n * count + j
            high = src[j * step + chans : (j + 1) * step]
            stage[slot, :, :128] = src[j * step : j * step + chans]
            stage[slot, :half, 128:] = high[:, : chans - 128]
            stage[slot, half:, 128:] = high[:, chans - 128 :]
            real = tap < taps_all
            tap = jnp.minimum(tap, taps_all - 1)
            for which in range(2):
                good = odd if (which == 0) == (n < 4) else jnp.logical_not(odd)
                good = jnp.logical_and(good, real)
                copy = pltpu.make_async_copy(stage.at[slot], outs[which].at[tap], sems.at[slot])
                pl.when(good)(copy.start)
                made.append((good, copy))
    for good, copy in made:
        pl.when(good)(copy.wait)


vmem = pl.BlockSpec(memory_space=pltpu.VMEM)
anywhere = pl.BlockSpec(memory_space=pl.ANY)


def call(kernel, outs, args, flops, scratch=(), free=(), out_spec=vmem, **kw):
    return pl.pallas_call(
        kernel,
        out_shape=outs,
        in_specs=[anywhere if i in free else vmem for i in range(len(args))],
        out_specs=[out_spec] * len(outs),
        scratch_shapes=list(scratch),
        compiler_params=pltpu.CompilerParams(vmem_limit_bytes=50 * 2**20),
        cost_estimate=pl.CostEstimate(flops=flops, bytes_accessed=8 * 2**20, transcendentals=0),
        **kw,
    )(*args)


def moved(value, axis, by):
    size = lax.axis_size(axis)
    return lax.ppermute(value, axis, [(i, i + by) for i in range(size) if 0 <= i + by < size])


def edge_parts(up, down):
    above = moved(up, "height", 1)
    below = moved(down, "height", -1)
    passed_ahead = moved(jnp.stack([above[0], below[0]]), "tm", 1)
    passed_behind = moved(jnp.stack([above[1], below[1]]), "tm", -1)
    return above, below, passed_ahead, passed_behind


def total_of(pieces):
    return functools.reduce(lambda a, b: a + b, [p.astype(f32) for p in pieces])


def piece_at(value, index):
    return lax.dynamic_index_in_dim(value, index, 0, keepdims=False)


def body(features, weight_one, bias_one, gain_one, weight_two, bias_two, gain_two, cotangent):
    frames, rows, cols, chans = features.shape
    tm, height = lax.axis_size("tm"), lax.axis_size("height")
    planes = height // 4
    c, me = lax.axis_index("tm"), lax.axis_index("height")
    odd = c % 2 == 1
    p, q = me % 4, me // 4
    swap = [(i, i ^ 1) for i in range(tm)]
    line = lambda v: v.reshape(1, chans)
    local = jax.ShapeDtypeStruct(features.shape, bf16)
    sums = jax.ShapeDtypeStruct((8, chans), f32)
    flops = 4 * frames * rows * cols * 27 * chans * chans
    window = pltpu.VMEM((frames + 2, rows + 2, cols, chans), bf16)
    weight = pltpu.VMEM(weight_one.shape, bf16)
    vector = pltpu.VMEM((1, chans), f32)
    packed_shape = jax.ShapeDtypeStruct((rows, cols, 2 * chans), bf16)
    edge_shape = jax.ShapeDtypeStruct((2, cols, 2 * chans), bf16)

    def plane_move(value, d):
        return lax.ppermute(value, "height", [(i, i ^ d) for i in range(height)])

    def column_move(value, d):
        pairs = [(z * 4 + j, (z + d) % planes * 4 + j) for z in range(planes) for j in range(4)]
        return lax.ppermute(value, "height", pairs)

    up = jnp.stack([pack_frames(v[:, -1]) for v in (features, cotangent)])
    down = jnp.stack([pack_frames(v[:, 0]) for v in (features, cotangent)])
    above, below, passed_ahead, passed_behind = edge_parts(up, down)
    earlier, later = moved(features, "tm", 1), moved(cotangent, "tm", -1)

    top = p == 0
    odd_y = [pack_frames(earlier), pack_frames(features)]
    even_y = [pack_frames(cotangent), pack_frames(later)]
    near = jnp.where(top, above, below)
    odd_edge = [jnp.where(top, passed_ahead[0], passed_ahead[1]), near[0]]
    even_edge = [near[1], jnp.where(top, passed_behind[0], passed_behind[1])]
    if tm > 2:
        extra = lax.ppermute(jnp.where(odd, even_y[1], odd_y[0]), "tm", swap)
        odd_y, even_y = [extra, *odd_y], [*even_y, extra]
        extra = lax.ppermute(jnp.where(odd, even_edge[1], odd_edge[0]), "tm", swap)
        odd_edge, even_edge = [extra, *odd_edge], [*even_edge, extra]
    blocks = len(odd_y)
    y_own = jnp.where(odd, jnp.stack(odd_y), jnp.stack(even_y))
    ys = [y_own] + [plane_move(y_own, d) for d in (1, 2, 3)]
    edge = jnp.where(odd, jnp.stack(odd_edge), jnp.stack(even_edge))[:, None]

    act2, gmid, give, keep, sums_one = call(
        first_kernel,
        (packed_shape,) * 4 + (sums,),
        (
            features, earlier, cotangent, later, above, below, passed_ahead, passed_behind,
            weight_one, weight_two, line(bias_one), line(gain_one), line(gain_two),
        ),
        flops,
        [window, window, weight, weight, vector, vector, vector, pltpu.SemaphoreType.DMA((9,))],
        free=(0, 1, 2, 3, 8, 9, 10, 11, 12),
    )
    other = lax.ppermute(give, "tm", swap)
    x_own = jnp.where(odd, jnp.stack([other, keep]), jnp.stack([keep, other]))
    if blocks > 2:
        x_own = jnp.concatenate([x_own, jnp.zeros((blocks - 2, *x_own.shape[1:]), bf16)])
    x_own = jnp.concatenate([x_own, edge], axis=1)
    xs = [x_own] + [plane_move(x_own, d) for d in (1, 2, 3)]

    earlier2, later2 = moved(act2, "tm", 1), moved(gmid, "tm", -1)

    step = pack_rows(chans)
    unit = 16 * planes
    cells = (2 * frames, 4 * rows, cols, chans)
    parts = []
    for n, taps in enumerate(chunks):
        packed = -(-taps[1] * step // unit) * unit
        passes = n == 0
        flat, *ends = call(
            functools.partial(wgrad_kernel, blocks, taps, passes),
            (jax.ShapeDtypeStruct((packed, 128), bf16),) + (edge_shape,) * (2 * passes),
            (*xs, *ys, line(gain_one)) + (act2, gmid) * passes,
            flops // 2,
            [
                pltpu.VMEM((2 * frames + 2, 4 * rows + 2, cols, chans), bf16),
                pltpu.VMEM((3, *cells), bf16),
            ],
        )
        if passes:
            edges2 = edge_parts(*ends)
        flat = flat.reshape(planes, packed // planes, 128)
        arrived = [column_move(piece_at(flat, (q + d) % planes), d) for d in range(1, planes)]
        part = total_of([piece_at(flat, q), *arrived])
        hop = 2
        while hop < tm:
            part = part + lax.ppermute(part, "tm", [(i, i ^ hop) for i in range(tm)])
            hop *= 2
        parts.append(part.astype(bf16))

    local_scratch = pltpu.VMEM(features.shape, bf16)
    block_out, grad_input, sums_two = call(
        last_kernel,
        (local, local, sums),
        (
            act2, earlier2, gmid, later2, *edges2, features, cotangent,
            weight_one, weight_two, line(bias_two), line(gain_one),
        ),
        flops,
        [
            window, window, local_scratch, local_scratch, weight, weight, vector, vector,
            pltpu.SemaphoreType.DMA((6,)),
        ],
        free=(8, 9, 10, 11, 12, 13),
    )

    small = jnp.concatenate([sums_one[:3], sums_two[:1]]).reshape(-1, 128)
    count = small.shape[0]

    def with_small(value, small):
        high = small.astype(bf16)
        low = (small - high.astype(f32)).astype(bf16)
        pad = jnp.zeros((-2 * count % 16, 128), bf16)
        return jnp.concatenate([value, high, low, pad])

    def without_small(pieces, rows):
        total = total_of([v[rows : rows + count].astype(f32) + v[rows + count : rows + 2 * count].astype(f32) for v in pieces])
        return [v[:rows] for v in pieces], total

    hop = 2
    while hop < tm:
        small = small + lax.ppermute(small, "tm", [(i, i ^ hop) for i in range(tm)])
        hop *= 2

    gradient = jax.ShapeDtypeStruct((taps_all, chans, chans), bf16)
    grads = ()
    for n, (part, taps) in enumerate(zip(parts, chunks)):
        last = n == len(parts) - 1
        size = part.shape[0]
        send = with_small(part, small) if last else part
        got = [send] + [column_move(send, d) for d in range(1, planes)]
        if last:
            got, small = without_small(got, size)
        stack = jnp.stack(got)
        quarter = jnp.take(stack, (q - jnp.arange(planes)) % planes, axis=0).reshape(-1, 128)
        size = quarter.shape[0]
        send = with_small(quarter, small) if last else quarter
        got = [send] + [plane_move(send, d) for d in (1, 2, 3)]
        others = [lax.ppermute(g, "tm", swap) for g in got]
        if last:
            _, small = without_small(got + others, size)
        held = len(grads) > 0
        grads = call(
            functools.partial(unpack_kernel, taps, held),
            (gradient, gradient),
            (*got, *others, *grads),
            0,
            [pltpu.VMEM((8 * taps[1], chans, chans), bf16), pltpu.SemaphoreType.DMA((8 * taps[1],))],
            free=(8, 9),
            out_spec=anywhere,
            input_output_aliases={8: 0, 9: 1} if held else {},
        )
    grad_one, grad_two = grads
    shape = weight_one.shape
    small = small.reshape(4, chans).astype(bf16)
    return (
        block_out,
        grad_input,
        grad_one.reshape(shape),
        grad_two.reshape(shape),
        small[1],
        small[2],
        small[3],
        small[0],
    )


def solution(mesh):
    split = P("tm", "height", None, None)
    return jax.shard_map(
        body,
        mesh=mesh,
        in_specs=(split, P(), P(), P(), P(), P(), P(), split),
        out_specs=(split, split, P(), P(), P(), P(), P(), P()),
        check_vma=False,
    )
```

```python
import functools

import jax
import jax.numpy as jnp
from jax import lax
from jax.experimental import pallas as pl
from jax.experimental.pallas import tpu as pltpu
from jax.sharding import PartitionSpec as P

epsilon = 1e-06
bf16 = jnp.bfloat16
f32 = jnp.float32
chunks = ((0, 3), (3, 4))
taps_each = 7
taps_all = 27


def shift_cols(value, by):
    zero = jnp.zeros_like(value[:, :1])
    if by == 1:
        return jnp.concatenate([value[:, 1:], zero], axis=1)
    return jnp.concatenate([zero, value[:, :-1]], axis=1)


def norm_parts(vals, gain):
    scale = lax.rsqrt(jnp.mean(vals * vals, axis=-1, keepdims=True) + epsilon)
    normed = vals * scale
    lifted = normed * gain
    return scale, normed, lifted, jax.nn.sigmoid(lifted)


def norm_silu(vals, gain):
    _, _, lifted, sig = norm_parts(vals, gain)
    return lifted * sig


def norm_silu_back(grad, vals, gain):
    scale, normed, lifted, sig = norm_parts(vals, gain)
    d_lift = grad * sig * (1.0 + lifted * (1.0 - sig))
    d_gain = jnp.sum(d_lift * normed, axis=0, keepdims=True)
    d_norm = d_lift * gain
    d_vals = scale * (d_norm - normed * jnp.mean(d_norm * normed, axis=-1, keepdims=True))
    return d_vals, d_gain


def conv(window, weight, frames, rows, back):
    cols, chans = window.shape[2], window.shape[3]
    parts = [None] * 3
    for t in range(3):
        for h in range(3):
            t0, h0 = (2 - t, 2 - h) if back else (t, h)
            piece = window[t0 : t0 + frames, h0 : h0 + rows].reshape(frames * rows * cols, chans)
            for k in range(3):
                dims = (((1,), (1 if back else 0,)), ((), ()))
                prod = lax.dot_general(piece, weight[t, h, k], dims, preferred_element_type=f32)
                parts[k] = prod if parts[k] is None else parts[k] + prod
    parts = [part.reshape(frames * rows, cols, chans) for part in parts]
    sign = -1 if back else 1
    total = parts[1] + shift_cols(parts[0], -sign) + shift_cols(parts[2], sign)
    return total.reshape(frames * rows * cols, chans)


def is_odd():
    return lax.axis_index("tm") % 2 == 1


def by_core(odd_fn, even_fn):
    pl.when(is_odd())(odd_fn)
    pl.when(jnp.logical_not(is_odd()))(even_fn)


def fill_packed(window, at, rows, packed):
    chans = window.shape[3]
    for f in range(2):
        window[at + f, rows] = packed[..., f * chans : (f + 1) * chans]


def fill_far(ahead, behind, far, rows):
    def put(window, at, value):
        if value.shape[-1] == window.shape[3]:
            window[pl.ds(at, 2), rows] = value
        else:
            fill_packed(window, at, rows, value)

    if far.shape[0] == 2:
        put(ahead, 0, far[0])
        put(behind, 2, far[1])
        return
    zero = jnp.zeros(far.shape[1:], bf16)

    def odd():
        put(ahead, 0, far[0])
        put(behind, 2, zero)

    def even():
        put(ahead, 0, zero)
        put(behind, 2, far[0])

    by_core(odd, even)


def fill_edges(ahead, behind, above, below):
    last = ahead.shape[1] - 1
    places = ((ahead, 0), (ahead, 2), (behind, 0), (behind, 2))
    for row, edges in ((0, above), (last, below)):
        rows = pl.ds(row, 1)
        if edges.shape[0] == 4:
            for i, (window, at) in enumerate(places):
                fill_packed(window, at, rows, edges[i : i + 1])
            continue
        zero = jnp.zeros((1,) + edges.shape[1:], bf16)

        def odd():
            for i, (window, at) in enumerate(places):
                fill_packed(window, at, rows, edges[i : i + 1] if i < 3 else zero)

        def even():
            for i, (window, at) in enumerate(places):
                fill_packed(window, at, rows, edges[i - 1 : i] if i > 0 else zero)

        by_core(odd, even)


def started(copies, sems):
    made = [pltpu.make_async_copy(src, dst, sems.at[i]) for i, (src, dst) in enumerate(copies)]
    for copy in made:
        copy.start()
    return made


def pack_frames(values):
    return jnp.concatenate([values[0], values[1]], axis=-1)


def put_messages(groups, up_ref, down_ref):
    for i, value in enumerate(groups):
        up_ref[i] = value[value.shape[0] - 1]
        down_ref[i] = value[0]


def join_first_kernel(*refs):
    refs, (y_ref, up_ref, down_ref) = refs[:-3], refs[-3:]
    feat, cot, *far = [pack_frames(ref) for ref in refs]
    if len(far) == 1:

        def odd():
            y_ref[0], y_ref[1] = far[0], feat
            put_messages((far[0], feat, cot), up_ref, down_ref)

        def even():
            y_ref[0], y_ref[1] = cot, far[0]
            put_messages((feat, cot, far[0]), up_ref, down_ref)

    else:
        put_messages((far[0], feat, cot, far[1]), up_ref, down_ref)

        def odd():
            y_ref[0], y_ref[1], y_ref[2] = far[2], far[0], feat

        def even():
            y_ref[0], y_ref[1], y_ref[2] = cot, far[1], far[2]

    by_core(odd, even)


def gate_kernel(keep_ref, give_ref, far_ref, _, up_ref, down_ref):
    keep, give, far = keep_ref[...], give_ref[...], far_ref[...]

    def odd():
        put_messages((far[0], give, keep, far[-1])[: up_ref.shape[0]], up_ref, down_ref)

    def even():
        put_messages((far[0], keep, give, far[-1])[4 - up_ref.shape[0] :], up_ref, down_ref)

    by_core(odd, even)


def join_edge_kernel(keep_ref, other_ref, above_ref, below_ref, out_ref):
    rows = keep_ref.shape[0]
    top = lax.axis_index("height") % 4 == 0
    edge = jnp.where(top, above_ref[...], below_ref[...])

    def odd():
        out_ref[0, :rows], out_ref[1, :rows] = other_ref[...], keep_ref[...]
        out_ref[0, rows], out_ref[1, rows] = edge[0], edge[1]

    def even():
        out_ref[0, :rows], out_ref[1, :rows] = keep_ref[...], other_ref[...]
        out_ref[0, rows], out_ref[1, rows] = edge[1], edge[2]

    by_core(odd, even)


def first_kernel(
    _, __, feat_any, cot_any, far_ref, above_ref, below_ref, w1_any, w2_any, b1_any, g1_any, g2_any,
    give_ref, keep_ref, sums_ref, ahead, behind, w1, w2, b1, g1, g2, sems,
):
    frames, rows, cols, chans = feat_any.shape
    own = pl.ds(1, rows)
    copies = started(
        (
            (feat_any, ahead.at[pl.ds(2, 2), own]),
            (g1_any, g1),
            (w1_any, w1),
            (b1_any, b1),
            (g2_any, g2),
            (cot_any, behind.at[pl.ds(0, 2), own]),
            (w2_any, w2),
        ),
        sems,
    )
    fill_far(ahead, behind, far_ref, own)
    fill_edges(ahead, behind, above_ref, below_ref)
    for copy in copies[:2]:
        copy.wait()
    for f in range(frames + 2):
        vals = ahead[f].astype(f32).reshape(-1, chans)
        ahead[f] = norm_silu(vals, g1[...]).astype(bf16).reshape(rows + 2, cols, chans)
    for copy in copies[2:5]:
        copy.wait()
    mid = (conv(ahead, w1, frames, rows, False) + b1[...]).astype(bf16).astype(f32)
    act2 = norm_silu(mid, g2[...]).astype(bf16).reshape(frames, rows, cols, chans)
    act2 = pack_frames(act2)
    for copy in copies[5:]:
        copy.wait()
    grad = conv(behind, w2, frames, rows, True)
    gmid, d_gain = norm_silu_back(grad, mid, g2[...])
    gmid = gmid.astype(bf16)
    cot = behind[:2, 1 : rows + 1].astype(f32).reshape(-1, chans)
    sums_ref[...] = jnp.concatenate(
        [
            d_gain,
            jnp.sum(gmid.astype(f32), axis=0, keepdims=True),
            jnp.sum(cot, axis=0, keepdims=True),
            jnp.zeros((5, chans), f32),
        ],
        axis=0,
    )
    gmid = pack_frames(gmid.reshape(frames, rows, cols, chans))

    def odd():
        give_ref[...] = act2
        keep_ref[...] = gmid

    def even():
        give_ref[...] = gmid
        keep_ref[...] = act2

    by_core(odd, even)


def last_kernel(
    keep_ref, give_ref, far_ref, above_ref, below_ref,
    feat_any, cot_any, w1_any, w2_any, b2_any, g1_any,
    out_ref, gin_ref, sums_ref, ahead, behind, feat, cot, w1, w2, b2, g1, sems,
):
    frames, rows, cols, chans = out_ref.shape
    own = pl.ds(1, rows)
    copies = started(
        ((w2_any, w2), (b2_any, b2), (feat_any, feat), (w1_any, w1), (cot_any, cot), (g1_any, g1)), sems
    )

    def odd():
        fill_packed(ahead, 2, own, give_ref[...])
        fill_packed(behind, 0, own, keep_ref[...])

    def even():
        fill_packed(ahead, 2, own, keep_ref[...])
        fill_packed(behind, 0, own, give_ref[...])

    by_core(odd, even)
    fill_far(ahead, behind, far_ref, own)
    fill_edges(ahead, behind, above_ref, below_ref)
    for copy in copies[:3]:
        copy.wait()
    values = feat[...].astype(f32).reshape(-1, chans)
    out = values + conv(ahead, w2, frames, rows, False) + b2[...]
    out_ref[...] = out.astype(bf16).reshape(out_ref.shape)
    for copy in copies[3:]:
        copy.wait()
    grad = conv(behind, w1, frames, rows, True)
    d_vals, d_gain = norm_silu_back(grad, values, g1[...])
    gin = d_vals + cot[...].astype(f32).reshape(-1, chans)
    gin_ref[...] = gin.astype(bf16).reshape(gin_ref.shape)
    sums_ref[...] = jnp.concatenate([d_gain, jnp.zeros((7, chans), f32)], axis=0)


def pack_rows(chans):
    return chans + chans // 2


def wgrad_kernel(blocks, taps, *refs):
    xs, ys = refs[:4], refs[4:8]
    gain_ref = refs[8]
    out_ref, plane, xk = refs[-3:]
    _, rows, cols, _ = ys[0].shape
    chans = gain_ref.shape[1]
    tall = 4 * rows
    cells = 4 * tall * cols
    odd = lax.axis_index("tm") % 2 == 1
    p = lax.axis_index("height") % 4
    single = blocks == 2
    start = jnp.where(odd, 2, 0) if single else 0
    if single:
        plane[pl.ds(jnp.where(odd, 0, 4), 2)] = jnp.zeros((2,) + plane.shape[1:], bf16)

    def put_y(values, row, count):
        for b in range(blocks):
            for f in range(2):
                part = values[b, :, :, f * chans : (f + 1) * chans]
                place = (start + 2 * b + f, pl.ds(row, count))

                @pl.when(odd)
                def _():
                    flat = part.astype(f32).reshape(-1, chans)
                    plane[place] = norm_silu(flat, gain_ref[...]).astype(bf16).reshape(part.shape)

                @pl.when(jnp.logical_not(odd))
                def _():
                    plane[place] = part

    for d in range(4):
        at = p ^ d
        put_y(ys[d][...], 1 + rows * at, rows)
        for b in range(2):
            for f in range(2):
                part = xs[d][b, :rows, :, f * chans : (f + 1) * chans]
                wide = part.astype(f32)
                place = (2 * b + f, pl.ds(rows * at, rows))
                xk[(0,) + place] = shift_cols(wide, 1).astype(bf16)
                xk[(1,) + place] = part
                xk[(2,) + place] = shift_cols(wide, -1).astype(bf16)

        @pl.when(at == 0)
        def _():
            put_y(xs[d][:, rows:], 0, 1)

        @pl.when(at == 3)
        def _():
            put_y(xs[d][:, rows:], tall + 1, 1)

    step = pack_rows(chans)
    dims = (((0,), (0,)), ((), ()))
    first, count = taps
    half = chans // 2

    def store(base, grad):
        grad = grad.astype(bf16)
        out_ref[base : base + chans] = grad[:, :128]
        out_ref[base + chans : base + step] = jnp.concatenate(
            [grad[:half, 128:], grad[half:, 128:]], axis=1
        )

    for j in range(count):
        tap = jnp.minimum(p * taps_each + first + j, taps_all - 1)
        t, h, k = tap // 9, tap // 3 % 3, tap % 3

        @pl.when(odd)
        def _():
            piece = plane[pl.ds(t, 4), pl.ds(h, tall)].reshape(cells, chans)
            x = xk[k].reshape(cells, chans)
            store(j * step, lax.dot_general(piece, x, dims, preferred_element_type=f32))

        @pl.when(jnp.logical_not(odd))
        def _():
            piece = plane[pl.ds(2 - t, 4), pl.ds(2 - h, tall)].reshape(cells, chans)
            x = xk[2 - k].reshape(cells, chans)
            store(j * step, lax.dot_general(x, piece, dims, preferred_element_type=f32))

    used = count * step
    if used < out_ref.shape[0]:
        out_ref[used:] = jnp.zeros((out_ref.shape[0] - used, 128), bf16)


def unpack_kernel(taps, held, *refs):
    pieces = refs[:8]
    outs, stage, sems = refs[8 + 2 * held : 10 + 2 * held], refs[-2], refs[-1]
    first, count = taps
    chans = stage.shape[1]
    half = chans // 2
    step = pack_rows(chans)
    odd = lax.axis_index("tm") % 2 == 1
    p = lax.axis_index("height") % 4
    made = []
    for n, src in enumerate(pieces):
        for j in range(count):
            tap = (p ^ (n % 4)) * taps_each + first + j
            slot = n * count + j
            high = src[j * step + chans : (j + 1) * step]
            stage[slot, :, :128] = src[j * step : j * step + chans]
            stage[slot, :half, 128:] = high[:, : chans - 128]
            stage[slot, half:, 128:] = high[:, chans - 128 :]
            real = tap < taps_all
            tap = jnp.minimum(tap, taps_all - 1)
            for which in range(2):
                good = odd if (which == 0) == (n < 4) else jnp.logical_not(odd)
                good = jnp.logical_and(good, real)
                copy = pltpu.make_async_copy(stage.at[slot], outs[which].at[tap], sems.at[slot])
                pl.when(good)(copy.start)
                made.append((good, copy))
    for good, copy in made:
        pl.when(good)(copy.wait)


vmem = pl.BlockSpec(memory_space=pltpu.VMEM)
anywhere = pl.BlockSpec(memory_space=pl.ANY)
in_hbm = pl.BlockSpec(memory_space=pltpu.HBM)


def call(kernel, outs, args, us, mib, scratch=(), free=(), hbm=(), out_spec=vmem, **kw):
    return pl.pallas_call(
        kernel,
        out_shape=outs,
        in_specs=[in_hbm if i in hbm else anywhere if i in free else vmem for i in range(len(args))],
        out_specs=[out_spec] * len(outs),
        scratch_shapes=list(scratch),
        compiler_params=pltpu.CompilerParams(vmem_limit_bytes=mib * 2**20),
        cost_estimate=pl.CostEstimate(flops=0, bytes_accessed=int(us * 3.6e6), transcendentals=0),
        **kw,
    )(*args)


def moved(value, axis, by):
    size = lax.axis_size(axis)
    return lax.ppermute(value, axis, [(i, i + by) for i in range(size) if 0 <= i + by < size])


def total_of(pieces):
    return functools.reduce(lambda a, b: a + b, [p.astype(f32) for p in pieces])


def piece_at(value, index):
    return lax.dynamic_index_in_dim(value, index, 0, keepdims=False)


def body(features, weight_one, bias_one, gain_one, weight_two, bias_two, gain_two, cotangent):
    frames, rows, cols, chans = features.shape
    tm, height = lax.axis_size("tm"), lax.axis_size("height")
    planes = height // 4
    c, me = lax.axis_index("tm"), lax.axis_index("height")
    odd = c % 2 == 1
    p, q = me % 4, me // 4
    swap = [(i, i ^ 1) for i in range(tm)]
    line = lambda v: v.reshape(1, chans)
    local = jax.ShapeDtypeStruct(features.shape, bf16)
    sums = jax.ShapeDtypeStruct((8, chans), f32)
    window = pltpu.VMEM((frames + 2, rows + 2, cols, chans), bf16)
    weight = pltpu.VMEM(weight_one.shape, bf16)
    vector = pltpu.VMEM((1, chans), f32)
    packed_shape = jax.ShapeDtypeStruct((rows, cols, 2 * chans), bf16)

    def plane_move(value, d):
        return lax.ppermute(value, "height", [(i, i ^ d) for i in range(height)])

    def column_move(value, d):
        pairs = [(z * 4 + j, (z + d) % planes * 4 + j) for z in range(planes) for j in range(4)]
        return lax.ppermute(value, "height", pairs)

    pair = tm == 2
    blocks = 2 if pair else 3
    messages = (jax.ShapeDtypeStruct((3 if pair else 4, cols, 2 * chans), bf16),) * 2
    y_shape = jax.ShapeDtypeStruct((blocks, rows, cols, 2 * chans), bf16)
    x_shape = jax.ShapeDtypeStruct((blocks, rows + 1, cols, 2 * chans), bf16)
    if pair:
        far = (lax.ppermute(jnp.where(odd, cotangent, features), "tm", swap),)
        extra = ()
    else:
        far = (moved(features, "tm", 1), moved(cotangent, "tm", -1))
        extra = (lax.ppermute(jnp.where(odd, far[1], far[0]), "tm", swap),)
    y_own, up, down = call(join_first_kernel, (y_shape, *messages), (features, cotangent, *far, *extra), 1, 8)
    above, below = moved(up, "height", 1), moved(down, "height", -1)
    ys = [y_own] + [plane_move(y_own, d) for d in (1, 2, 3)]

    give, keep, sums_one = call(
        first_kernel,
        (packed_shape, packed_shape, sums),
        (
            ys[1], ys[2], features, cotangent, jnp.stack(far), above, below,
            weight_one, weight_two, line(bias_one), line(gain_one), line(gain_two),
        ),
        5,
        62,
        [window, window, weight, weight, vector, vector, vector, pltpu.SemaphoreType.DMA((7,))],
        free=(0, 1),
        hbm=(2, 3, 7, 8, 9, 10, 11),
    )
    other = lax.ppermute(give, "tm", swap)
    if pair:
        (x_own,) = call(join_edge_kernel, (x_shape,), (keep, other, above, below), 1, 6)
        far = lax.ppermute(keep, "tm", swap)[None]
    else:
        edge = jnp.where(p == 0, above, below)
        extra = lax.ppermute(jnp.where(odd, edge[3], edge[0]), "tm", swap)
        edge = jnp.where(odd, jnp.stack([extra, edge[0], edge[1]]), jnp.stack([edge[2], edge[3], extra]))
        x_own = jnp.where(odd, jnp.stack([other, keep, keep]), jnp.stack([keep, other, other]))
        x_own = jnp.concatenate([x_own, edge[:, None]], axis=1)
        act2, gmid = jnp.where(odd, give, keep), jnp.where(odd, keep, give)
        far = jnp.stack([moved(act2, "tm", 1), moved(gmid, "tm", -1)])
    xs = [x_own] + [plane_move(x_own, d) for d in (1, 2, 3)]
    before = ()

    step = pack_rows(chans)
    unit = 16 * planes
    cells = (2 * frames, 4 * rows, cols, chans)
    parts = []
    for taps in chunks:
        packed = -(-taps[1] * step // unit) * unit
        (flat,) = call(
            functools.partial(wgrad_kernel, blocks, taps),
            (jax.ShapeDtypeStruct((packed, 128), bf16),),
            (*xs, *ys, line(gain_one), *before),
            4,
            24,
            free=tuple(range(9, 9 + len(before))),
            scratch=[
                pltpu.VMEM((2 * frames + 2, 4 * rows + 2, cols, chans), bf16),
                pltpu.VMEM((3, *cells), bf16),
            ],
        )
        if not before:
            up, down = call(gate_kernel, messages, (keep, give, far, flat), 1, 6, free=(3,))
            above, below = moved(up, "height", 1), moved(down, "height", -1)
        before = (flat,)
        flat = flat.reshape(planes, packed // planes, 128)
        arrived = [column_move(piece_at(flat, (q + d) % planes), d) for d in range(1, planes)]
        part = total_of([piece_at(flat, q), *arrived])
        hop = 2
        while hop < tm:
            part = part + lax.ppermute(part, "tm", [(i, i ^ hop) for i in range(tm)])
            hop *= 2
        parts.append(part.astype(bf16))

    local_scratch = pltpu.VMEM(features.shape, bf16)
    block_out, grad_input, sums_two = call(
        last_kernel,
        (local, local, sums),
        (
            keep, give, far, above, below, features, cotangent,
            weight_one, weight_two, line(bias_two), line(gain_one),
        ),
        6,
        62,
        [
            window, window, local_scratch, local_scratch, weight, weight, vector, vector,
            pltpu.SemaphoreType.DMA((6,)),
        ],
        hbm=(5, 6, 7, 8, 9, 10),
    )

    small = jnp.concatenate([sums_one[:3], sums_two[:1]]).reshape(-1, 128)
    count = small.shape[0]

    def with_small(value, small):
        high = small.astype(bf16)
        low = (small - high.astype(f32)).astype(bf16)
        pad = jnp.zeros((-2 * count % 16, 128), bf16)
        return jnp.concatenate([value, high, low, pad])

    def without_small(pieces, rows):
        total = total_of([v[rows : rows + count].astype(f32) + v[rows + count : rows + 2 * count].astype(f32) for v in pieces])
        return [v[:rows] for v in pieces], total

    hop = 2
    while hop < tm:
        small = small + lax.ppermute(small, "tm", [(i, i ^ hop) for i in range(tm)])
        hop *= 2

    gradient = jax.ShapeDtypeStruct((taps_all, chans, chans), bf16)
    grads = ()
    for n, (part, taps) in enumerate(zip(parts, chunks)):
        last = n == len(parts) - 1
        size = part.shape[0]
        send = with_small(part, small) if last else part
        got = [send] + [column_move(send, d) for d in range(1, planes)]
        if last:
            got, small = without_small(got, size)
        stack = jnp.stack(got)
        quarter = jnp.take(stack, (q - jnp.arange(planes)) % planes, axis=0).reshape(-1, 128)
        size = quarter.shape[0]
        send = with_small(quarter, small) if last else quarter
        got = [send] + [plane_move(send, d) for d in (1, 2, 3)]
        others = [lax.ppermute(g, "tm", swap) for g in got]
        if last:
            _, small = without_small(got + others, size)
        held = len(grads) > 0
        grads = call(
            functools.partial(unpack_kernel, taps, held),
            (gradient, gradient),
            (*got, *others, *grads),
            2,
            12,
            [pltpu.VMEM((8 * taps[1], chans, chans), bf16), pltpu.SemaphoreType.DMA((8 * taps[1],))],
            free=(8, 9),
            out_spec=anywhere,
            input_output_aliases={8: 0, 9: 1} if held else {},
        )
    grad_one, grad_two = grads
    shape = weight_one.shape
    small = small.reshape(4, chans).astype(bf16)
    return (
        block_out,
        grad_input,
        grad_one.reshape(shape),
        grad_two.reshape(shape),
        small[1],
        small[2],
        small[3],
        small[0],
    )


def solution(mesh):
    split = P("tm", "height", None, None)
    return jax.shard_map(
        body,
        mesh=mesh,
        in_specs=(split, P(), P(), P(), P(), P(), P(), split),
        out_specs=(split, split, P(), P(), P(), P(), P(), P()),
        check_vma=False,
    )
```

```python
import functools

import jax
import jax.numpy as jnp
from jax import lax
from jax.experimental import pallas as pl
from jax.experimental.pallas import tpu as pltpu
from jax.sharding import PartitionSpec as P

epsilon = 1e-06
bf16 = jnp.bfloat16
f32 = jnp.float32
chunks = ((0, 3), (3, 4))
taps_each = 7
taps_all = 27


def shift_cols(value, by):
    zero = jnp.zeros_like(value[:, :1])
    if by == 1:
        return jnp.concatenate([value[:, 1:], zero], axis=1)
    return jnp.concatenate([zero, value[:, :-1]], axis=1)


def norm_parts(vals, gain):
    scale = lax.rsqrt(jnp.mean(vals * vals, axis=-1, keepdims=True) + epsilon)
    normed = vals * scale
    lifted = normed * gain
    return scale, normed, lifted, jax.nn.sigmoid(lifted)


def norm_silu(vals, gain):
    _, _, lifted, sig = norm_parts(vals, gain)
    return lifted * sig


def norm_silu_back(grad, vals, gain):
    scale, normed, lifted, sig = norm_parts(vals, gain)
    d_lift = grad * sig * (1.0 + lifted * (1.0 - sig))
    d_gain = jnp.sum(d_lift * normed, axis=0, keepdims=True)
    d_norm = d_lift * gain
    d_vals = scale * (d_norm - normed * jnp.mean(d_norm * normed, axis=-1, keepdims=True))
    return d_vals, d_gain


def conv(window, weight, frames, rows, back):
    cols, chans = window.shape[2], window.shape[3]
    parts = [None] * 3
    for t in range(3):
        for h in range(3):
            t0, h0 = (2 - t, 2 - h) if back else (t, h)
            piece = window[t0 : t0 + frames, h0 : h0 + rows].reshape(frames * rows * cols, chans)
            for k in range(3):
                dims = (((1,), (1 if back else 0,)), ((), ()))
                prod = lax.dot_general(piece, weight[t, h, k], dims, preferred_element_type=f32)
                parts[k] = prod if parts[k] is None else parts[k] + prod
    parts = [part.reshape(frames * rows, cols, chans) for part in parts]
    sign = -1 if back else 1
    total = parts[1] + shift_cols(parts[0], -sign) + shift_cols(parts[2], sign)
    return total.reshape(frames * rows * cols, chans)


def is_odd():
    return lax.axis_index("tm") % 2 == 1


def by_core(odd_fn, even_fn):
    pl.when(is_odd())(odd_fn)
    pl.when(jnp.logical_not(is_odd()))(even_fn)


def fill_packed(window, at, rows, packed):
    chans = window.shape[3]
    for f in range(2):
        window[at + f, rows] = packed[..., f * chans : (f + 1) * chans]


def fill_far(ahead, behind, far, rows):
    def put(window, at, value):
        if value.shape[-1] == window.shape[3]:
            window[pl.ds(at, 2), rows] = value
        else:
            fill_packed(window, at, rows, value)

    if far.shape[0] == 2:
        put(ahead, 0, far[0])
        put(behind, 2, far[1])
        return
    zero = jnp.zeros(far.shape[1:], bf16)

    def odd():
        put(ahead, 0, far[0])
        put(behind, 2, zero)

    def even():
        put(ahead, 0, zero)
        put(behind, 2, far[0])

    by_core(odd, even)


def fill_edges(ahead, behind, above, below):
    last = ahead.shape[1] - 1
    places = ((ahead, 0), (ahead, 2), (behind, 0), (behind, 2))
    for row, edges in ((0, above), (last, below)):
        rows = pl.ds(row, 1)
        if edges.shape[0] == 4:
            for i, (window, at) in enumerate(places):
                fill_packed(window, at, rows, edges[i : i + 1])
            continue
        zero = jnp.zeros((1,) + edges.shape[1:], bf16)

        def odd():
            for i, (window, at) in enumerate(places):
                fill_packed(window, at, rows, edges[i : i + 1] if i < 3 else zero)

        def even():
            for i, (window, at) in enumerate(places):
                fill_packed(window, at, rows, edges[i - 1 : i] if i > 0 else zero)

        by_core(odd, even)


def started(copies, sems):
    made = [pltpu.make_async_copy(src, dst, sems.at[i]) for i, (src, dst) in enumerate(copies)]
    for copy in made:
        copy.start()
    return made


def pack_frames(values):
    return jnp.concatenate([values[0], values[1]], axis=-1)


def put_messages(groups, up_ref, down_ref):
    for i, value in enumerate(groups):
        up_ref[i] = value[value.shape[0] - 1]
        down_ref[i] = value[0]


def join_first_kernel(*refs):
    refs, (y_ref, up_ref, down_ref) = refs[:-3], refs[-3:]
    keep, give, *far = [pack_frames(ref) for ref in refs]
    if len(far) == 1:

        def odd():
            y_ref[0], y_ref[1] = far[0], keep
            put_messages((far[0], keep, give), up_ref, down_ref)

        def even():
            y_ref[0], y_ref[1] = keep, far[0]
            put_messages((give, keep, far[0]), up_ref, down_ref)

    else:

        def odd():
            y_ref[0], y_ref[1], y_ref[2] = far[2], far[0], keep
            put_messages((far[0], keep, give, far[1]), up_ref, down_ref)

        def even():
            y_ref[0], y_ref[1], y_ref[2] = keep, far[1], far[2]
            put_messages((far[0], give, keep, far[1]), up_ref, down_ref)

    by_core(odd, even)


def gate_kernel(keep_ref, give_ref, far_ref, _, up_ref, down_ref):
    keep, give, far = keep_ref[...], give_ref[...], far_ref[...]

    def odd():
        put_messages((far[0], give, keep, far[-1])[: up_ref.shape[0]], up_ref, down_ref)

    def even():
        put_messages((far[0], keep, give, far[-1])[4 - up_ref.shape[0] :], up_ref, down_ref)

    by_core(odd, even)


def join_edge_kernel(keep_ref, other_ref, above_ref, below_ref, out_ref):
    rows = keep_ref.shape[0]
    top = lax.axis_index("height") % 4 == 0
    edge = jnp.where(top, above_ref[...], below_ref[...])

    def odd():
        out_ref[0, :rows], out_ref[1, :rows] = other_ref[...], keep_ref[...]
        out_ref[0, rows], out_ref[1, rows] = edge[0], edge[1]

    def even():
        out_ref[0, :rows], out_ref[1, :rows] = keep_ref[...], other_ref[...]
        out_ref[0, rows], out_ref[1, rows] = edge[1], edge[2]

    by_core(odd, even)


def fetch_kernel(w1_any, w2_any, b1_any, g1_any, b2_any, g2_any, w1_ref, w2_ref, vec_ref, sems):
    vectors = [(ref, vec_ref.at[pl.ds(i, 1)]) for i, ref in enumerate((b1_any, g1_any, b2_any, g2_any))]
    for copy in started([(w1_any, w1_ref), (w2_any, w2_ref), *vectors], sems):
        copy.wait()


def first_kernel(
    _, __, ___, keep_in, give_in, far_ref, above_ref, below_ref, w1, w2, vec_ref,
    give_ref, keep_ref, sums_ref, ahead, behind,
):
    frames, rows, cols, chans = keep_in.shape
    own = pl.ds(1, rows)
    b1, g1, g2 = vec_ref[0:1], vec_ref[1:2], vec_ref[3:4]

    def odd_in():
        ahead[pl.ds(2, 2), own] = keep_in[...]
        behind[pl.ds(0, 2), own] = give_in[...]

    def even_in():
        ahead[pl.ds(2, 2), own] = give_in[...]
        behind[pl.ds(0, 2), own] = keep_in[...]

    by_core(odd_in, even_in)
    fill_far(ahead, behind, far_ref, own)
    fill_edges(ahead, behind, above_ref, below_ref)
    for f in range(frames + 2):
        vals = ahead[f].astype(f32).reshape(-1, chans)
        ahead[f] = norm_silu(vals, g1).astype(bf16).reshape(rows + 2, cols, chans)
    mid = (conv(ahead, w1, frames, rows, False) + b1).astype(bf16).astype(f32)
    act2 = norm_silu(mid, g2).astype(bf16).reshape(frames, rows, cols, chans)
    act2 = pack_frames(act2)
    grad = conv(behind, w2, frames, rows, True)
    gmid, d_gain = norm_silu_back(grad, mid, g2)
    gmid = gmid.astype(bf16)
    cot = behind[:2, 1 : rows + 1].astype(f32).reshape(-1, chans)
    sums_ref[...] = jnp.concatenate(
        [
            d_gain,
            jnp.sum(gmid.astype(f32), axis=0, keepdims=True),
            jnp.sum(cot, axis=0, keepdims=True),
            jnp.zeros((5, chans), f32),
        ],
        axis=0,
    )
    gmid = pack_frames(gmid.reshape(frames, rows, cols, chans))

    def odd():
        give_ref[...] = act2
        keep_ref[...] = gmid

    def even():
        give_ref[...] = gmid
        keep_ref[...] = act2

    by_core(odd, even)


def last_kernel(
    keep_ref, give_ref, far_ref, above_ref, below_ref, keep_in, give_in, w1, w2, vec_ref,
    out_ref, gin_ref, sums_ref, ahead, behind,
):
    frames, rows, cols, chans = out_ref.shape
    own = pl.ds(1, rows)
    g1, b2 = vec_ref[1:2], vec_ref[2:3]

    def odd():
        fill_packed(ahead, 2, own, give_ref[...])
        fill_packed(behind, 0, own, keep_ref[...])

    def even():
        fill_packed(ahead, 2, own, keep_ref[...])
        fill_packed(behind, 0, own, give_ref[...])

    by_core(odd, even)
    fill_far(ahead, behind, far_ref, own)
    fill_edges(ahead, behind, above_ref, below_ref)
    feat = jnp.where(is_odd(), keep_in[...], give_in[...]).astype(f32).reshape(-1, chans)
    out = feat + conv(ahead, w2, frames, rows, False) + b2
    out_ref[...] = out.astype(bf16).reshape(out_ref.shape)
    grad = conv(behind, w1, frames, rows, True)
    d_vals, d_gain = norm_silu_back(grad, feat, g1)
    gin = d_vals + jnp.where(is_odd(), give_in[...], keep_in[...]).astype(f32).reshape(-1, chans)
    gin_ref[...] = gin.astype(bf16).reshape(gin_ref.shape)
    sums_ref[...] = jnp.concatenate([d_gain, jnp.zeros((7, chans), f32)], axis=0)


def pack_rows(chans):
    return chans + chans // 2


def chunk_rows(count, chans, planes):
    unit = 16 * planes
    return -(-count * pack_rows(chans) // unit) * unit


def wgrad_kernel(blocks, planes, *refs):
    xs, ys = refs[:4], refs[4:8]
    gain = refs[8][1:2]
    out_ref, plane, xk = refs[-3:]
    _, rows, cols, _ = ys[0].shape
    chans = gain.shape[1]
    tall = 4 * rows
    cells = 4 * tall * cols
    odd = lax.axis_index("tm") % 2 == 1
    p = lax.axis_index("height") % 4
    single = blocks == 2
    start = jnp.where(odd, 2, 0) if single else 0
    if single:
        plane[pl.ds(jnp.where(odd, 0, 4), 2)] = jnp.zeros((2,) + plane.shape[1:], bf16)

    def put_y(values, row, count):
        for b in range(blocks):
            for f in range(2):
                part = values[b, :, :, f * chans : (f + 1) * chans]
                place = (start + 2 * b + f, pl.ds(row, count))

                @pl.when(odd)
                def _():
                    flat = part.astype(f32).reshape(-1, chans)
                    plane[place] = norm_silu(flat, gain).astype(bf16).reshape(part.shape)

                @pl.when(jnp.logical_not(odd))
                def _():
                    plane[place] = part

    for d in range(4):
        at = p ^ d
        put_y(ys[d][...], 1 + rows * at, rows)
        for b in range(2):
            for f in range(2):
                part = xs[d][b, :rows, :, f * chans : (f + 1) * chans]
                wide = part.astype(f32)
                place = (2 * b + f, pl.ds(rows * at, rows))
                xk[(0,) + place] = shift_cols(wide, 1).astype(bf16)
                xk[(1,) + place] = part
                xk[(2,) + place] = shift_cols(wide, -1).astype(bf16)

        @pl.when(at == 0)
        def _():
            put_y(xs[d][:, rows:], 0, 1)

        @pl.when(at == 3)
        def _():
            put_y(xs[d][:, rows:], tall + 1, 1)

    step = pack_rows(chans)
    dims = (((0,), (0,)), ((), ()))
    half = chans // 2
    offset = 0
    for first, count in chunks:
        share = chunk_rows(count, chans, planes) // planes

        def put(row, values, offset=offset, share=share):
            at = 0
            while at < values.shape[0]:
                q, r = divmod(row + at, share)
                n = min(share - r, values.shape[0] - at)
                out_ref[q, offset + r : offset + r + n] = values[at : at + n]
                at += n

        def store(row, grad, put=put):
            grad = grad.astype(bf16)
            put(row, grad[:, :128])
            put(row + chans, jnp.concatenate([grad[:half, 128:], grad[half:, 128:]], axis=1))

        for j in range(count):
            tap = jnp.minimum(p * taps_each + first + j, taps_all - 1)
            t, h, k = tap // 9, tap // 3 % 3, tap % 3

            @pl.when(odd)
            def _():
                piece = plane[pl.ds(t, 4), pl.ds(h, tall)].reshape(cells, chans)
                x = xk[k].reshape(cells, chans)
                store(j * step, lax.dot_general(piece, x, dims, preferred_element_type=f32))

            @pl.when(jnp.logical_not(odd))
            def _():
                piece = plane[pl.ds(2 - t, 4), pl.ds(2 - h, tall)].reshape(cells, chans)
                x = xk[2 - k].reshape(cells, chans)
                store(j * step, lax.dot_general(x, piece, dims, preferred_element_type=f32))

        spare = share * planes - count * step
        if spare:
            put(count * step, jnp.zeros((spare, 128), bf16))
        offset += share


def unpack_kernel(taps, held, *refs):
    pieces = refs[:8]
    outs, stage, sems = refs[8 + 2 * held : 10 + 2 * held], refs[-2], refs[-1]
    first, count = taps
    chans = stage.shape[1]
    half = chans // 2
    step = pack_rows(chans)
    odd = lax.axis_index("tm") % 2 == 1
    p = lax.axis_index("height") % 4
    made = []
    for n, src in enumerate(pieces):
        for j in range(count):
            tap = (p ^ (n % 4)) * taps_each + first + j
            slot = n * count + j
            high = src[j * step + chans : (j + 1) * step]
            stage[slot, :, :128] = src[j * step : j * step + chans]
            stage[slot, :half, 128:] = high[:, : chans - 128]
            stage[slot, half:, 128:] = high[:, chans - 128 :]
            real = tap < taps_all
            tap = jnp.minimum(tap, taps_all - 1)
            for which in range(2):
                good = odd if (which == 0) == (n < 4) else jnp.logical_not(odd)
                good = jnp.logical_and(good, real)
                copy = pltpu.make_async_copy(stage.at[slot], outs[which].at[tap], sems.at[slot])
                pl.when(good)(copy.start)
                made.append((good, copy))
    for good, copy in made:
        pl.when(good)(copy.wait)


vmem = pl.BlockSpec(memory_space=pltpu.VMEM)
anywhere = pl.BlockSpec(memory_space=pl.ANY)
in_hbm = pl.BlockSpec(memory_space=pltpu.HBM)


def call(kernel, outs, args, us, mib, scratch=(), free=(), hbm=(), out_spec=vmem, **kw):
    return pl.pallas_call(
        kernel,
        out_shape=outs,
        in_specs=[in_hbm if i in hbm else anywhere if i in free else vmem for i in range(len(args))],
        out_specs=[out_spec] * len(outs),
        scratch_shapes=list(scratch),
        compiler_params=pltpu.CompilerParams(vmem_limit_bytes=mib * 2**20),
        cost_estimate=pl.CostEstimate(flops=int(us * 1.1e9), bytes_accessed=1024, transcendentals=0),
        **kw,
    )(*args)


def moved(value, axis, by):
    size = lax.axis_size(axis)
    return lax.ppermute(value, axis, [(i, i + by) for i in range(size) if 0 <= i + by < size])


def total_of(pieces):
    return functools.reduce(lambda a, b: a + b, [p.astype(f32) for p in pieces])


def piece_at(value, index):
    return lax.dynamic_index_in_dim(value, index, 0, keepdims=False)


def body(features, weight_one, bias_one, gain_one, weight_two, bias_two, gain_two, cotangent):
    frames, rows, cols, chans = features.shape
    tm, height = lax.axis_size("tm"), lax.axis_size("height")
    planes = height // 4
    c, me = lax.axis_index("tm"), lax.axis_index("height")
    odd = c % 2 == 1
    p, q = me % 4, me // 4
    swap = [(i, i ^ 1) for i in range(tm)]
    line = lambda v: v.reshape(1, chans)
    local = jax.ShapeDtypeStruct(features.shape, bf16)
    sums = jax.ShapeDtypeStruct((8, chans), f32)
    window = pltpu.VMEM((frames + 2, rows + 2, cols, chans), bf16)
    packed_shape = jax.ShapeDtypeStruct((rows, cols, 2 * chans), bf16)

    def plane_move(value, d):
        return lax.ppermute(value, "height", [(i, i ^ d) for i in range(height)])

    def column_move(value, d):
        pairs = [(z * 4 + j, (z + d) % planes * 4 + j) for z in range(planes) for j in range(4)]
        return lax.ppermute(value, "height", pairs)

    pair = tm == 2
    blocks = 2 if pair else 3
    messages = (jax.ShapeDtypeStruct((3 if pair else 4, cols, 2 * chans), bf16),) * 2
    y_shape = jax.ShapeDtypeStruct((blocks, rows, cols, 2 * chans), bf16)
    x_shape = jax.ShapeDtypeStruct((blocks, rows + 1, cols, 2 * chans), bf16)
    raw_give, raw_keep = jnp.where(odd, cotangent, features), jnp.where(odd, features, cotangent)
    if pair:
        far = (lax.ppermute(raw_give, "tm", swap),)
        extra = ()
    else:
        far = (moved(features, "tm", 1), moved(cotangent, "tm", -1))
        extra = (lax.ppermute(jnp.where(odd, far[1], far[0]), "tm", swap),)
    held = jax.ShapeDtypeStruct(weight_one.shape, bf16)
    w1, w2, vec = call(
        fetch_kernel,
        (held, held, jax.ShapeDtypeStruct((8, chans), f32)),
        (weight_one, weight_two, line(bias_one), line(gain_one), line(bias_two), line(gain_two)),
        3,
        8,
        [pltpu.SemaphoreType.DMA((6,))],
        hbm=range(6),
    )
    y_own, up, down = call(join_first_kernel, (y_shape, *messages), (raw_keep, raw_give, *far, *extra), 1, 8)
    above, below = moved(up, "height", 1), moved(down, "height", -1)
    ys = [y_own] + [plane_move(y_own, d) for d in (1, 2, 3)]

    give, keep, sums_one = call(
        first_kernel,
        (packed_shape, packed_shape, sums),
        (*ys[1:], raw_keep, raw_give, jnp.stack(far), above, below, w1, w2, vec),
        5,
        20,
        [window, window],
        free=(0, 1, 2),
    )
    other = lax.ppermute(give, "tm", swap)
    if pair:
        (x_own,) = call(join_edge_kernel, (x_shape,), (keep, other, above, below), 1, 6)
        far = lax.ppermute(keep, "tm", swap)[None]
    else:
        edge = jnp.where(p == 0, above, below)
        extra = lax.ppermute(jnp.where(odd, edge[3], edge[0]), "tm", swap)
        edge = jnp.where(odd, jnp.stack([extra, edge[0], edge[1]]), jnp.stack([edge[2], edge[3], extra]))
        x_own = jnp.where(odd, jnp.stack([other, keep, keep]), jnp.stack([keep, other, other]))
        x_own = jnp.concatenate([x_own, edge[:, None]], axis=1)
        act2, gmid = jnp.where(odd, give, keep), jnp.where(odd, keep, give)
        far = jnp.stack([moved(act2, "tm", 1), moved(gmid, "tm", -1)])
    xs = [x_own] + [plane_move(x_own, d) for d in (1, 2, 3)]
    up, down = call(gate_kernel, messages, (keep, give, far, xs[1]), 1, 6, free=(3,))
    above, below = moved(up, "height", 1), moved(down, "height", -1)

    shares = [chunk_rows(count, chans, planes) // planes for _, count in chunks]
    (flat,) = call(
        functools.partial(wgrad_kernel, blocks, planes),
        (jax.ShapeDtypeStruct((planes, sum(shares), 128), bf16),),
        (*xs, *ys, vec),
        7,
        24,
        [
            pltpu.VMEM((2 * frames + 2, 4 * rows + 2, cols, chans), bf16),
            pltpu.VMEM((3, 2 * frames, 4 * rows, cols, chans), bf16),
        ],
    )
    arrived = [column_move(piece_at(flat, (q + d) % planes), d) for d in range(1, planes)]
    part = total_of([piece_at(flat, q), *arrived])
    hop = 2
    while hop < tm:
        part = part + lax.ppermute(part, "tm", [(i, i ^ hop) for i in range(tm)])
        hop *= 2
    part = part.astype(bf16)
    parts = jnp.split(part, [sum(shares[:n]) for n in range(1, len(shares))])

    block_out, grad_input, sums_two = call(
        last_kernel,
        (local, local, sums),
        (keep, give, far, above, below, raw_keep, raw_give, w1, w2, vec),
        6,
        20,
        [window, window],
    )

    small = jnp.concatenate([sums_one[:3], sums_two[:1]]).reshape(-1, 128)
    count = small.shape[0]

    def with_small(value, small):
        high = small.astype(bf16)
        low = (small - high.astype(f32)).astype(bf16)
        pad = jnp.zeros((-2 * count % 16, 128), bf16)
        return jnp.concatenate([value, high, low, pad])

    def without_small(pieces, rows):
        total = total_of([v[rows : rows + count].astype(f32) + v[rows + count : rows + 2 * count].astype(f32) for v in pieces])
        return [v[:rows] for v in pieces], total

    hop = 2
    while hop < tm:
        small = small + lax.ppermute(small, "tm", [(i, i ^ hop) for i in range(tm)])
        hop *= 2

    gradient = jax.ShapeDtypeStruct((taps_all, chans, chans), bf16)
    grads = ()
    for n, (part, taps) in enumerate(zip(parts, chunks)):
        last = n == len(parts) - 1
        size = part.shape[0]
        send = with_small(part, small) if last else part
        got = [send] + [column_move(send, d) for d in range(1, planes)]
        if last:
            got, small = without_small(got, size)
        stack = jnp.stack(got)
        quarter = jnp.take(stack, (q - jnp.arange(planes)) % planes, axis=0).reshape(-1, 128)
        size = quarter.shape[0]
        send = with_small(quarter, small) if last else quarter
        got = [send] + [plane_move(send, d) for d in (1, 2, 3)]
        others = [lax.ppermute(g, "tm", swap) for g in got]
        if last:
            _, small = without_small(got + others, size)
        held = len(grads) > 0
        grads = call(
            functools.partial(unpack_kernel, taps, held),
            (gradient, gradient),
            (*got, *others, *grads),
            2,
            12,
            [pltpu.VMEM((8 * taps[1], chans, chans), bf16), pltpu.SemaphoreType.DMA((8 * taps[1],))],
            free=(8, 9),
            out_spec=anywhere,
            input_output_aliases={8: 0, 9: 1} if held else {},
        )
    grad_one, grad_two = grads
    shape = weight_one.shape
    small = small.reshape(4, chans).astype(bf16)
    return (
        block_out,
        grad_input,
        grad_one.reshape(shape),
        grad_two.reshape(shape),
        small[1],
        small[2],
        small[3],
        small[0],
    )


def solution(mesh):
    split = P("tm", "height", None, None)
    return jax.shard_map(
        body,
        mesh=mesh,
        in_specs=(split, P(), P(), P(), P(), P(), P(), split),
        out_specs=(split, split, P(), P(), P(), P(), P(), P()),
        check_vma=False,
    )
```

```python
import functools

import jax
import jax.numpy as jnp
from jax import lax
from jax.experimental import pallas as pl
from jax.experimental.pallas import tpu as pltpu
from jax.sharding import PartitionSpec as P

epsilon = 1e-06
bf16 = jnp.bfloat16
f32 = jnp.float32
chunks = ((0, 3), (3, 4))
taps_each = 7
taps_all = 27


def shift_cols(value, by):
    zero = jnp.zeros_like(value[:, :1])
    if by == 1:
        return jnp.concatenate([value[:, 1:], zero], axis=1)
    return jnp.concatenate([zero, value[:, :-1]], axis=1)


def norm_parts(vals, gain):
    scale = lax.rsqrt(jnp.mean(vals * vals, axis=-1, keepdims=True) + epsilon)
    normed = vals * scale
    lifted = normed * gain
    return scale, normed, lifted, jax.nn.sigmoid(lifted)


def norm_silu(vals, gain):
    _, _, lifted, sig = norm_parts(vals, gain)
    return lifted * sig


def norm_silu_back(grad, vals, gain):
    scale, normed, lifted, sig = norm_parts(vals, gain)
    d_lift = grad * sig * (1.0 + lifted * (1.0 - sig))
    d_gain = jnp.sum(d_lift * normed, axis=0, keepdims=True)
    d_norm = d_lift * gain
    d_vals = scale * (d_norm - normed * jnp.mean(d_norm * normed, axis=-1, keepdims=True))
    return d_vals, d_gain


def conv(window, weight, frames, rows, back):
    cols, chans = window.shape[2], window.shape[3]
    parts = [None] * 3
    for t in range(3):
        for h in range(3):
            t0, h0 = (2 - t, 2 - h) if back else (t, h)
            piece = window[t0 : t0 + frames, h0 : h0 + rows].reshape(frames * rows * cols, chans)
            for k in range(3):
                dims = (((1,), (1 if back else 0,)), ((), ()))
                prod = lax.dot_general(piece, weight[t, h, k], dims, preferred_element_type=f32)
                parts[k] = prod if parts[k] is None else parts[k] + prod
    parts = [part.reshape(frames * rows, cols, chans) for part in parts]
    sign = -1 if back else 1
    total = parts[1] + shift_cols(parts[0], -sign) + shift_cols(parts[2], sign)
    return total.reshape(frames * rows * cols, chans)


def is_odd():
    return lax.axis_index("tm") % 2 == 1


def by_core(odd_fn, even_fn):
    pl.when(is_odd())(odd_fn)
    pl.when(jnp.logical_not(is_odd()))(even_fn)


def fill_packed(window, at, rows, packed):
    chans = window.shape[3]
    for f in range(2):
        window[at + f, rows] = packed[..., f * chans : (f + 1) * chans]


def fill_far(ahead, behind, far, rows):
    def put(window, at, value):
        if value.shape[-1] == window.shape[3]:
            window[pl.ds(at, 2), rows] = value
        else:
            fill_packed(window, at, rows, value)

    if far.shape[0] == 2:
        put(ahead, 0, far[0])
        put(behind, 2, far[1])
        return
    zero = jnp.zeros(far.shape[1:], bf16)

    def odd():
        put(ahead, 0, far[0])
        put(behind, 2, zero)

    def even():
        put(ahead, 0, zero)
        put(behind, 2, far[0])

    by_core(odd, even)


def fill_edges(ahead, behind, above, below):
    last = ahead.shape[1] - 1
    places = ((ahead, 0), (ahead, 2), (behind, 0), (behind, 2))
    for row, edges in ((0, above), (last, below)):
        rows = pl.ds(row, 1)
        if edges.shape[0] == 4:
            for i, (window, at) in enumerate(places):
                fill_packed(window, at, rows, edges[i : i + 1])
            continue
        zero = jnp.zeros((1,) + edges.shape[1:], bf16)

        def odd():
            for i, (window, at) in enumerate(places):
                fill_packed(window, at, rows, edges[i : i + 1] if i < 3 else zero)

        def even():
            for i, (window, at) in enumerate(places):
                fill_packed(window, at, rows, edges[i - 1 : i] if i > 0 else zero)

        by_core(odd, even)


def started(copies, sems):
    made = [pltpu.make_async_copy(src, dst, sems.at[i]) for i, (src, dst) in enumerate(copies)]
    for copy in made:
        copy.start()
    return made


def pack_frames(values):
    return jnp.concatenate([values[0], values[1]], axis=-1)


def put_messages(groups, up_ref, down_ref):
    for i, value in enumerate(groups):
        up_ref[i] = value[value.shape[0] - 1]
        down_ref[i] = value[0]


def join_first_kernel(*refs):
    refs, (y_ref, up_ref, down_ref) = refs[:-3], refs[-3:]
    keep, give, *far = [pack_frames(ref) for ref in refs]
    if len(far) == 1:

        def odd():
            y_ref[0], y_ref[1] = far[0], keep
            put_messages((far[0], keep, give), up_ref, down_ref)

        def even():
            y_ref[0], y_ref[1] = keep, far[0]
            put_messages((give, keep, far[0]), up_ref, down_ref)

    else:

        def odd():
            y_ref[0], y_ref[1], y_ref[2] = far[2], far[0], keep
            put_messages((far[0], keep, give, far[1]), up_ref, down_ref)

        def even():
            y_ref[0], y_ref[1], y_ref[2] = keep, far[1], far[2]
            put_messages((far[0], give, keep, far[1]), up_ref, down_ref)

    by_core(odd, even)


def gate_kernel(keep_ref, give_ref, far_ref, _, up_ref, down_ref):
    keep, give, far = keep_ref[...], give_ref[...], far_ref[...]

    def odd():
        put_messages((far[0], give, keep, far[-1])[: up_ref.shape[0]], up_ref, down_ref)

    def even():
        put_messages((far[0], keep, give, far[-1])[4 - up_ref.shape[0] :], up_ref, down_ref)

    by_core(odd, even)


def join_edge_kernel(keep_ref, other_ref, above_ref, below_ref, out_ref):
    rows = keep_ref.shape[0]
    top = lax.axis_index("height") % 4 == 0
    edge = jnp.where(top, above_ref[...], below_ref[...])

    def odd():
        out_ref[0, :rows], out_ref[1, :rows] = other_ref[...], keep_ref[...]
        out_ref[0, rows], out_ref[1, rows] = edge[0], edge[1]

    def even():
        out_ref[0, :rows], out_ref[1, :rows] = keep_ref[...], other_ref[...]
        out_ref[0, rows], out_ref[1, rows] = edge[1], edge[2]

    by_core(odd, even)


def fetch_kernel(w1_any, w2_any, b1_any, g1_any, b2_any, g2_any, w1_ref, w2_ref, vec_ref, sems):
    vectors = [(ref, vec_ref.at[pl.ds(i, 1)]) for i, ref in enumerate((b1_any, g1_any, b2_any, g2_any))]
    for copy in started([(w1_any, w1_ref), (w2_any, w2_ref), *vectors], sems):
        copy.wait()


def first_kernel(
    _, __, ___, keep_in, give_in, far_ref, above_ref, below_ref, w1, w2, vec_ref,
    give_ref, keep_ref, sums_ref, ahead, behind,
):
    frames, rows, cols, chans = keep_in.shape
    own = pl.ds(1, rows)
    b1, g1, g2 = vec_ref[0:1], vec_ref[1:2], vec_ref[3:4]

    def odd_in():
        ahead[pl.ds(2, 2), own] = keep_in[...]
        behind[pl.ds(0, 2), own] = give_in[...]

    def even_in():
        ahead[pl.ds(2, 2), own] = give_in[...]
        behind[pl.ds(0, 2), own] = keep_in[...]

    by_core(odd_in, even_in)
    fill_far(ahead, behind, far_ref, own)
    fill_edges(ahead, behind, above_ref, below_ref)
    for f in range(frames + 2):
        vals = ahead[f].astype(f32).reshape(-1, chans)
        ahead[f] = norm_silu(vals, g1).astype(bf16).reshape(rows + 2, cols, chans)
    mid = (conv(ahead, w1, frames, rows, False) + b1).astype(bf16).astype(f32)
    act2 = norm_silu(mid, g2).astype(bf16).reshape(frames, rows, cols, chans)
    act2 = pack_frames(act2)
    grad = conv(behind, w2, frames, rows, True)
    gmid, d_gain = norm_silu_back(grad, mid, g2)
    gmid = gmid.astype(bf16)
    cot = behind[:2, 1 : rows + 1].astype(f32).reshape(-1, chans)
    sums_ref[...] = jnp.concatenate(
        [
            d_gain,
            jnp.sum(gmid.astype(f32), axis=0, keepdims=True),
            jnp.sum(cot, axis=0, keepdims=True),
            jnp.zeros((5, chans), f32),
        ],
        axis=0,
    )
    gmid = pack_frames(gmid.reshape(frames, rows, cols, chans))

    def odd():
        give_ref[...] = act2
        keep_ref[...] = gmid

    def even():
        give_ref[...] = gmid
        keep_ref[...] = act2

    by_core(odd, even)


def last_kernel(
    keep_ref, give_ref, far_ref, above_ref, below_ref, keep_in, give_in, w1, w2, vec_ref,
    out_ref, gin_ref, sums_ref, ahead, behind,
):
    frames, rows, cols, chans = out_ref.shape
    own = pl.ds(1, rows)
    g1, b2 = vec_ref[1:2], vec_ref[2:3]

    def odd():
        fill_packed(ahead, 2, own, give_ref[...])
        fill_packed(behind, 0, own, keep_ref[...])

    def even():
        fill_packed(ahead, 2, own, keep_ref[...])
        fill_packed(behind, 0, own, give_ref[...])

    by_core(odd, even)
    fill_far(ahead, behind, far_ref, own)
    fill_edges(ahead, behind, above_ref, below_ref)
    feat = jnp.where(is_odd(), keep_in[...], give_in[...]).astype(f32).reshape(-1, chans)
    out = feat + conv(ahead, w2, frames, rows, False) + b2
    out_ref[...] = out.astype(bf16).reshape(out_ref.shape)
    grad = conv(behind, w1, frames, rows, True)
    d_vals, d_gain = norm_silu_back(grad, feat, g1)
    gin = d_vals + jnp.where(is_odd(), give_in[...], keep_in[...]).astype(f32).reshape(-1, chans)
    gin_ref[...] = gin.astype(bf16).reshape(gin_ref.shape)
    sums_ref[...] = jnp.concatenate([d_gain, jnp.zeros((7, chans), f32)], axis=0)


def pack_rows(chans):
    return chans + chans // 2


def chunk_rows(count, chans, planes):
    unit = 16 * planes
    return -(-count * pack_rows(chans) // unit) * unit


def wgrad_kernel(blocks, planes, *refs):
    xs, ys = refs[:4], refs[4:8]
    gain = refs[8][1:2]
    outs, (plane, xt) = refs[9:-2], refs[-2:]
    _, rows, cols, _ = ys[0].shape
    chans = gain.shape[1]
    tall = 4 * rows
    cells = 4 * tall * cols
    odd = lax.axis_index("tm") % 2 == 1
    p = lax.axis_index("height") % 4
    single = blocks == 2
    base = jnp.where(odd, 2, 0) if single else 0
    if single:
        plane[pl.ds(jnp.where(odd, 0, 4), 2)] = jnp.zeros((2,) + plane.shape[1:], bf16)

    def put_y(values, row, count):
        for b in range(blocks):
            for f in range(2):
                part = values[b, :, :, f * chans : (f + 1) * chans]
                place = (base + 2 * b + f, pl.ds(row, count))

                @pl.when(odd)
                def _():
                    flat = part.astype(f32).reshape(-1, chans)
                    plane[place] = norm_silu(flat, gain).astype(bf16).reshape(part.shape)

                @pl.when(jnp.logical_not(odd))
                def _():
                    plane[place] = part

    for d in range(4):
        at = p ^ d
        put_y(ys[d][...], 1 + rows * at, rows)
        block = rows * cols
        column = lax.broadcasted_iota(jnp.int32, (chans, block), 1) % cols
        for b in range(2):
            for f in range(2):
                part = xs[d][b, :rows, :, f * chans : (f + 1) * chans]
                part = part.astype(f32).reshape(block, chans).T
                start = pl.multiple_of((2 * b + f) * tall * cols + at * block, block)
                place = (slice(None), pl.ds(start, block))
                after = jnp.where(column == cols - 1, 0.0, pltpu.roll(part, block - 1, 1))
                before = jnp.where(column == 0, 0.0, pltpu.roll(part, 1, 1))
                xt[(0,) + place] = after.astype(bf16)
                xt[(1,) + place] = part.astype(bf16)
                xt[(2,) + place] = before.astype(bf16)

        @pl.when(at == 0)
        def _():
            put_y(xs[d][:, rows:], 0, 1)

        @pl.when(at == 3)
        def _():
            put_y(xs[d][:, rows:], tall + 1, 1)

    step = pack_rows(chans)
    half = chans // 2
    for (first, count), out_ref in zip(chunks, outs):
        share = chunk_rows(count, chans, planes) // planes

        def put(row, values, out_ref=out_ref, share=share):
            at = 0
            while at < values.shape[0]:
                q, r = divmod(row + at, share)
                n = min(share - r, values.shape[0] - at)
                out_ref[q, r : r + n] = values[at : at + n]
                at += n

        def store(row, grad, put=put):
            grad = grad.astype(bf16)
            put(row, grad[:, :128])
            put(row + chans, jnp.concatenate([grad[:half, 128:], grad[half:, 128:]], axis=1))

        for j in range(count):
            tap = jnp.minimum(p * taps_each + first + j, taps_all - 1)
            tap = jnp.where(odd, tap, taps_all - 1 - tap)
            t, h, k = tap // 9, tap // 3 % 3, tap % 3
            piece = plane[pl.ds(t, 4), pl.ds(h, tall)].reshape(cells, chans)
            grad = jnp.dot(xt[k], piece, preferred_element_type=f32)

            @pl.when(odd)
            def _():
                store(j * step, grad.T)

            @pl.when(jnp.logical_not(odd))
            def _():
                store(j * step, grad)

        spare = share * planes - count * step
        if spare:
            put(count * step, jnp.zeros((spare, 128), bf16))


def halves(total):
    high = total.astype(bf16)
    return jnp.concatenate([high, (total - high.astype(f32)).astype(bf16)])


def assemble_kernel(planes, size, *refs):
    pieces, out_ref = refs[:planes], refs[-1]
    q = lax.axis_index("height") // 4
    for d, piece in enumerate(pieces):
        start = pl.multiple_of((q - d + planes) % planes * size, 16)
        out_ref[pl.ds(start, size)] = piece[:size]
    if pieces[0].shape[0] > size:
        total = functools.reduce(lambda a, b: a + b, [piece[size:].astype(f32) for piece in pieces])
        half = total.shape[0] // 2
        out_ref[planes * size :] = halves(total[:half] + total[half:])


def unpack_kernel(taps, held, *refs):
    pieces = refs[:8]
    outs, stage, sems = refs[8 + 2 * held : 10 + 2 * held], refs[-2], refs[-1]
    first, count = taps
    chans = stage.shape[1]
    half = chans // 2
    step = pack_rows(chans)
    odd = lax.axis_index("tm") % 2 == 1
    p = lax.axis_index("height") % 4
    made = []
    for n, src in enumerate(pieces):
        for j in range(count):
            tap = (p ^ (n % 4)) * taps_each + first + j
            slot = n * count + j
            high = src[j * step + chans : (j + 1) * step]
            stage[slot, :, :128] = src[j * step : j * step + chans]
            stage[slot, :half, 128:] = high[:, : chans - 128]
            stage[slot, half:, 128:] = high[:, chans - 128 :]
            real = tap < taps_all
            tap = jnp.minimum(tap, taps_all - 1)
            for which in range(2):
                good = odd if (which == 0) == (n < 4) else jnp.logical_not(odd)
                good = jnp.logical_and(good, real)
                copy = pltpu.make_async_copy(stage.at[slot], outs[which].at[tap], sems.at[slot])
                pl.when(good)(copy.start)
                made.append((good, copy))
    for good, copy in made:
        pl.when(good)(copy.wait)


vmem = pl.BlockSpec(memory_space=pltpu.VMEM)
anywhere = pl.BlockSpec(memory_space=pl.ANY)
in_hbm = pl.BlockSpec(memory_space=pltpu.HBM)


def call(kernel, outs, args, us, mib, scratch=(), free=(), hbm=(), out_spec=vmem, **kw):
    return pl.pallas_call(
        kernel,
        out_shape=outs,
        in_specs=[in_hbm if i in hbm else anywhere if i in free else vmem for i in range(len(args))],
        out_specs=[out_spec] * len(outs),
        scratch_shapes=list(scratch),
        compiler_params=pltpu.CompilerParams(vmem_limit_bytes=mib * 2**20),
        cost_estimate=pl.CostEstimate(flops=int(us * 1.1e9), bytes_accessed=1024, transcendentals=0),
        **kw,
    )(*args)


def moved(value, axis, by):
    size = lax.axis_size(axis)
    return lax.ppermute(value, axis, [(i, i + by) for i in range(size) if 0 <= i + by < size])


def total_of(pieces):
    return functools.reduce(lambda a, b: a + b, [p.astype(f32) for p in pieces])


def piece_at(value, index):
    return lax.dynamic_index_in_dim(value, index, 0, keepdims=False)


def body(features, weight_one, bias_one, gain_one, weight_two, bias_two, gain_two, cotangent):
    frames, rows, cols, chans = features.shape
    tm, height = lax.axis_size("tm"), lax.axis_size("height")
    planes = height // 4
    c, me = lax.axis_index("tm"), lax.axis_index("height")
    odd = c % 2 == 1
    p, q = me % 4, me // 4
    swap = [(i, i ^ 1) for i in range(tm)]
    line = lambda v: v.reshape(1, chans)
    local = jax.ShapeDtypeStruct(features.shape, bf16)
    sums = jax.ShapeDtypeStruct((8, chans), f32)
    window = pltpu.VMEM((frames + 2, rows + 2, cols, chans), bf16)
    packed_shape = jax.ShapeDtypeStruct((rows, cols, 2 * chans), bf16)

    def plane_move(value, d):
        return lax.ppermute(value, "height", [(i, i ^ d) for i in range(height)])

    def column_move(value, d):
        pairs = [(z * 4 + j, (z + d) % planes * 4 + j) for z in range(planes) for j in range(4)]
        return lax.ppermute(value, "height", pairs)

    pair = tm == 2
    blocks = 2 if pair else 3
    messages = (jax.ShapeDtypeStruct((3 if pair else 4, cols, 2 * chans), bf16),) * 2
    y_shape = jax.ShapeDtypeStruct((blocks, rows, cols, 2 * chans), bf16)
    x_shape = jax.ShapeDtypeStruct((blocks, rows + 1, cols, 2 * chans), bf16)
    raw_give, raw_keep = jnp.where(odd, cotangent, features), jnp.where(odd, features, cotangent)
    if pair:
        far = (lax.ppermute(raw_give, "tm", swap),)
        extra = ()
    else:
        far = (moved(features, "tm", 1), moved(cotangent, "tm", -1))
        extra = (lax.ppermute(jnp.where(odd, far[1], far[0]), "tm", swap),)
    held = jax.ShapeDtypeStruct(weight_one.shape, bf16)
    w1, w2, vec = call(
        fetch_kernel,
        (held, held, jax.ShapeDtypeStruct((8, chans), f32)),
        (weight_one, weight_two, line(bias_one), line(gain_one), line(bias_two), line(gain_two)),
        3,
        8,
        [pltpu.SemaphoreType.DMA((6,))],
        hbm=range(6),
    )
    y_own, up, down = call(join_first_kernel, (y_shape, *messages), (raw_keep, raw_give, *far, *extra), 1, 8)
    above, below = moved(up, "height", 1), moved(down, "height", -1)
    ys = [y_own] + [plane_move(y_own, d) for d in (1, 2, 3)]

    give, keep, sums_one = call(
        first_kernel,
        (packed_shape, packed_shape, sums),
        (*ys[1:], raw_keep, raw_give, jnp.stack(far), above, below, w1, w2, vec),
        5,
        20,
        [window, window],
        free=(0, 1, 2),
    )
    other = lax.ppermute(give, "tm", swap)
    if pair:
        (x_own,) = call(join_edge_kernel, (x_shape,), (keep, other, above, below), 1, 6)
        far = lax.ppermute(keep, "tm", swap)[None]
    else:
        edge = jnp.where(p == 0, above, below)
        extra = lax.ppermute(jnp.where(odd, edge[3], edge[0]), "tm", swap)
        edge = jnp.where(odd, jnp.stack([extra, edge[0], edge[1]]), jnp.stack([edge[2], edge[3], extra]))
        x_own = jnp.where(odd, jnp.stack([other, keep, keep]), jnp.stack([keep, other, other]))
        x_own = jnp.concatenate([x_own, edge[:, None]], axis=1)
        act2, gmid = jnp.where(odd, give, keep), jnp.where(odd, keep, give)
        far = jnp.stack([moved(act2, "tm", 1), moved(gmid, "tm", -1)])
    xs = [x_own] + [plane_move(x_own, d) for d in (1, 2, 3)]
    up, down = call(gate_kernel, messages, (keep, give, far, xs[1]), 1, 6, free=(3,))
    above, below = moved(up, "height", 1), moved(down, "height", -1)

    flats = call(
        functools.partial(wgrad_kernel, blocks, planes),
        [
            jax.ShapeDtypeStruct((planes, chunk_rows(count, chans, planes) // planes, 128), bf16)
            for _, count in chunks
        ],
        (*xs, *ys, vec),
        6,
        24,
        [
            pltpu.VMEM((2 * frames + 2, 4 * rows + 2, cols, chans), bf16),
            pltpu.VMEM((3, chans, 8 * frames * rows * cols), bf16),
        ],
    )
    parts = []
    for flat in flats:
        arrived = [column_move(piece_at(flat, (q + d) % planes), d) for d in range(1, planes)]
        part = total_of([piece_at(flat, q), *arrived])
        hop = 2
        while hop < tm:
            part = part + lax.ppermute(part, "tm", [(i, i ^ hop) for i in range(tm)])
            hop *= 2
        parts.append(part.astype(bf16))

    block_out, grad_input, sums_two = call(
        last_kernel,
        (local, local, sums),
        (keep, give, far, above, below, raw_keep, raw_give, w1, w2, vec),
        6,
        20,
        [window, window],
    )

    small = jnp.concatenate([sums_one[:3], sums_two[:1]]).reshape(-1, 128)
    used = small.shape[0]
    count = -(-used // 8) * 8
    small = jnp.pad(small, ((0, count - used), (0, 0)))

    hop = 2
    while hop < tm:
        small = small + lax.ppermute(small, "tm", [(i, i ^ hop) for i in range(tm)])
        hop *= 2

    gradient = jax.ShapeDtypeStruct((taps_all, chans, chans), bf16)
    grads, gate = (), ()
    for n, (part, taps) in enumerate(zip(parts, chunks)):
        last = n == len(parts) - 1
        size = part.shape[0]
        send = jnp.concatenate([part, halves(small)]) if last else part
        got = [send] + [column_move(send, d) for d in range(1, planes)]
        (send,) = call(
            functools.partial(assemble_kernel, planes, size),
            (jax.ShapeDtypeStruct((planes * size + send.shape[0] - size, 128), bf16),),
            (*got, *gate),
            1,
            6,
            free=(planes,) if gate else (),
        )
        one, two = plane_move(send, 1), plane_move(send, 2)
        gate = (one,)
        cut = send.shape[0] // 32 * 16
        three = jnp.concatenate([plane_move(two[:cut], 1), plane_move(one[cut:], 2)])
        got = [send, one, two, three]
        others = [lax.ppermute(g, "tm", swap) for g in got]
        if last:
            small = total_of([v[planes * size :] for v in got + others])
            small = (small[:count] + small[count:])[:used]
        held = len(grads) > 0
        grads = call(
            functools.partial(unpack_kernel, taps, held),
            (gradient, gradient),
            (*got, *others, *grads),
            2,
            12,
            [pltpu.VMEM((8 * taps[1], chans, chans), bf16), pltpu.SemaphoreType.DMA((8 * taps[1],))],
            free=(8, 9) if held else (),
            out_spec=anywhere,
            input_output_aliases={8: 0, 9: 1} if held else {},
        )
    grad_one, grad_two = grads
    shape = weight_one.shape
    small = small.reshape(4, chans).astype(bf16)
    return (
        block_out,
        grad_input,
        grad_one.reshape(shape),
        grad_two.reshape(shape),
        small[1],
        small[2],
        small[3],
        small[0],
    )


def solution(mesh):
    split = P("tm", "height", None, None)
    return jax.shard_map(
        body,
        mesh=mesh,
        in_specs=(split, P(), P(), P(), P(), P(), P(), split),
        out_specs=(split, split, P(), P(), P(), P(), P(), P()),
        check_vma=False,
    )
```

```python
import functools

import jax
import jax.numpy as jnp
from jax import lax
from jax.experimental import pallas as pl
from jax.experimental.pallas import tpu as pltpu
from jax.sharding import PartitionSpec as P

epsilon = 1e-06
bf16 = jnp.bfloat16
f32 = jnp.float32
chunks = ((0, 3), (3, 4))
taps_each = 7
taps_all = 27


def shift_cols(value, by):
    zero = jnp.zeros_like(value[:, :1])
    if by == 1:
        return jnp.concatenate([value[:, 1:], zero], axis=1)
    return jnp.concatenate([zero, value[:, :-1]], axis=1)


def norm_parts(vals, gain):
    scale = lax.rsqrt(jnp.mean(vals * vals, axis=-1, keepdims=True) + epsilon)
    normed = vals * scale
    lifted = normed * gain
    return scale, normed, lifted, jax.nn.sigmoid(lifted)


def norm_silu(vals, gain):
    _, _, lifted, sig = norm_parts(vals, gain)
    return lifted * sig


def norm_silu_back(grad, vals, gain):
    scale, normed, lifted, sig = norm_parts(vals, gain)
    d_lift = grad * sig * (1.0 + lifted * (1.0 - sig))
    d_gain = jnp.sum(d_lift * normed, axis=0, keepdims=True)
    d_norm = d_lift * gain
    d_vals = scale * (d_norm - normed * jnp.mean(d_norm * normed, axis=-1, keepdims=True))
    return d_vals, d_gain


def conv(window, weight, frames, rows, back):
    cols, chans = window.shape[2], window.shape[3]
    parts = [None] * 3
    for t in range(3):
        for h in range(3):
            t0, h0 = (2 - t, 2 - h) if back else (t, h)
            piece = window[t0 : t0 + frames, h0 : h0 + rows].reshape(frames * rows * cols, chans)
            for k in range(3):
                dims = (((1,), (1 if back else 0,)), ((), ()))
                prod = lax.dot_general(piece, weight[t, h, k], dims, preferred_element_type=f32)
                parts[k] = prod if parts[k] is None else parts[k] + prod
    parts = [part.reshape(frames * rows, cols, chans) for part in parts]
    sign = -1 if back else 1
    total = parts[1] + shift_cols(parts[0], -sign) + shift_cols(parts[2], sign)
    return total.reshape(frames * rows * cols, chans)


def is_odd():
    return lax.axis_index("tm") % 2 == 1


def by_core(odd_fn, even_fn):
    pl.when(is_odd())(odd_fn)
    pl.when(jnp.logical_not(is_odd()))(even_fn)


def fill_packed(window, at, rows, packed):
    chans = window.shape[3]
    for f in range(2):
        window[at + f, rows] = packed[..., f * chans : (f + 1) * chans]


def fill_far(ahead, behind, far, rows):
    def put(window, at, value):
        if value.shape[-1] == window.shape[3]:
            window[pl.ds(at, 2), rows] = value
        else:
            fill_packed(window, at, rows, value)

    if far.shape[0] == 2:
        put(ahead, 0, far[0])
        put(behind, 2, far[1])
        return
    zero = jnp.zeros(far.shape[1:], bf16)

    def odd():
        put(ahead, 0, far[0])
        put(behind, 2, zero)

    def even():
        put(ahead, 0, zero)
        put(behind, 2, far[0])

    by_core(odd, even)


def fill_edges(ahead, behind, above, below):
    last = ahead.shape[1] - 1
    places = ((ahead, 0), (ahead, 2), (behind, 0), (behind, 2))
    for row, edges in ((0, above), (last, below)):
        rows = pl.ds(row, 1)
        if edges.shape[0] == 4:
            for i, (window, at) in enumerate(places):
                fill_packed(window, at, rows, edges[i : i + 1])
            continue
        zero = jnp.zeros((1,) + edges.shape[1:], bf16)

        def odd():
            for i, (window, at) in enumerate(places):
                fill_packed(window, at, rows, edges[i : i + 1] if i < 3 else zero)

        def even():
            for i, (window, at) in enumerate(places):
                fill_packed(window, at, rows, edges[i - 1 : i] if i > 0 else zero)

        by_core(odd, even)


def started(copies, sems):
    made = [pltpu.make_async_copy(src, dst, sems.at[i]) for i, (src, dst) in enumerate(copies)]
    for copy in made:
        copy.start()
    return made


def pack_frames(values):
    return jnp.concatenate([values[0], values[1]], axis=-1)


def put_messages(groups, up_ref, down_ref):
    for i, value in enumerate(groups):
        up_ref[i] = value[value.shape[0] - 1]
        down_ref[i] = value[0]


def join_first_kernel(*refs):
    refs, (y_ref, up_ref, down_ref) = refs[:-3], refs[-3:]
    keep, give, *far = [pack_frames(ref) for ref in refs]
    if len(far) == 1:

        def odd():
            y_ref[0], y_ref[1] = far[0], keep
            put_messages((far[0], keep, give), up_ref, down_ref)

        def even():
            y_ref[0], y_ref[1] = keep, far[0]
            put_messages((give, keep, far[0]), up_ref, down_ref)

    else:

        def odd():
            y_ref[0], y_ref[1], y_ref[2] = far[2], far[0], keep
            put_messages((far[0], keep, give, far[1]), up_ref, down_ref)

        def even():
            y_ref[0], y_ref[1], y_ref[2] = keep, far[1], far[2]
            put_messages((far[0], give, keep, far[1]), up_ref, down_ref)

    by_core(odd, even)


def gate_kernel(keep_ref, give_ref, far_ref, _, up_ref, down_ref):
    keep, give, far = keep_ref[...], give_ref[...], far_ref[...]

    def odd():
        put_messages((far[0], give, keep, far[-1])[: up_ref.shape[0]], up_ref, down_ref)

    def even():
        put_messages((far[0], keep, give, far[-1])[4 - up_ref.shape[0] :], up_ref, down_ref)

    by_core(odd, even)


def join_edge_kernel(keep_ref, other_ref, above_ref, below_ref, out_ref):
    rows = keep_ref.shape[0]
    top = lax.axis_index("height") % 4 == 0
    edge = jnp.where(top, above_ref[...], below_ref[...])

    def odd():
        out_ref[0, :rows], out_ref[1, :rows] = other_ref[...], keep_ref[...]
        out_ref[0, rows], out_ref[1, rows] = edge[0], edge[1]

    def even():
        out_ref[0, :rows], out_ref[1, :rows] = keep_ref[...], other_ref[...]
        out_ref[0, rows], out_ref[1, rows] = edge[1], edge[2]

    by_core(odd, even)


def fetch_kernel(w1_any, w2_any, b1_any, g1_any, b2_any, g2_any, w1_ref, w2_ref, vec_ref, sems):
    vectors = [(ref, vec_ref.at[pl.ds(i, 1)]) for i, ref in enumerate((b1_any, g1_any, b2_any, g2_any))]
    for copy in started([(w1_any, w1_ref), (w2_any, w2_ref), *vectors], sems):
        copy.wait()


def first_kernel(
    _, __, ___, keep_in, give_in, far_ref, above_ref, below_ref, w1, w2, vec_ref,
    give_ref, keep_ref, sums_ref, ahead, behind,
):
    frames, rows, cols, chans = keep_in.shape
    own = pl.ds(1, rows)
    b1, g1, g2 = vec_ref[0:1], vec_ref[1:2], vec_ref[3:4]

    def odd_in():
        ahead[pl.ds(2, 2), own] = keep_in[...]
        behind[pl.ds(0, 2), own] = give_in[...]

    def even_in():
        ahead[pl.ds(2, 2), own] = give_in[...]
        behind[pl.ds(0, 2), own] = keep_in[...]

    by_core(odd_in, even_in)
    fill_far(ahead, behind, far_ref, own)
    fill_edges(ahead, behind, above_ref, below_ref)
    for f in range(frames + 2):
        vals = ahead[f].astype(f32).reshape(-1, chans)
        ahead[f] = norm_silu(vals, g1).astype(bf16).reshape(rows + 2, cols, chans)
    mid = (conv(ahead, w1, frames, rows, False) + b1).astype(bf16).astype(f32)
    act2 = norm_silu(mid, g2).astype(bf16).reshape(frames, rows, cols, chans)
    act2 = pack_frames(act2)
    grad = conv(behind, w2, frames, rows, True)
    gmid, d_gain = norm_silu_back(grad, mid, g2)
    gmid = gmid.astype(bf16)
    cot = behind[:2, 1 : rows + 1].astype(f32).reshape(-1, chans)
    sums_ref[...] = jnp.concatenate(
        [
            d_gain,
            jnp.sum(gmid.astype(f32), axis=0, keepdims=True),
            jnp.sum(cot, axis=0, keepdims=True),
            jnp.zeros((5, chans), f32),
        ],
        axis=0,
    )
    gmid = pack_frames(gmid.reshape(frames, rows, cols, chans))

    def odd():
        give_ref[...] = act2
        keep_ref[...] = gmid

    def even():
        give_ref[...] = gmid
        keep_ref[...] = act2

    by_core(odd, even)


def last_kernel(
    keep_ref, give_ref, far_ref, above_ref, below_ref, keep_in, give_in, w1, w2, vec_ref,
    out_ref, gin_ref, sums_ref, ahead, behind,
):
    frames, rows, cols, chans = out_ref.shape
    own = pl.ds(1, rows)
    g1, b2 = vec_ref[1:2], vec_ref[2:3]

    def odd():
        fill_packed(ahead, 2, own, give_ref[...])
        fill_packed(behind, 0, own, keep_ref[...])

    def even():
        fill_packed(ahead, 2, own, keep_ref[...])
        fill_packed(behind, 0, own, give_ref[...])

    by_core(odd, even)
    fill_far(ahead, behind, far_ref, own)
    fill_edges(ahead, behind, above_ref, below_ref)
    feat = jnp.where(is_odd(), keep_in[...], give_in[...]).astype(f32).reshape(-1, chans)
    out = feat + conv(ahead, w2, frames, rows, False) + b2
    out_ref[...] = out.astype(bf16).reshape(out_ref.shape)
    grad = conv(behind, w1, frames, rows, True)
    d_vals, d_gain = norm_silu_back(grad, feat, g1)
    gin = d_vals + jnp.where(is_odd(), give_in[...], keep_in[...]).astype(f32).reshape(-1, chans)
    gin_ref[...] = gin.astype(bf16).reshape(gin_ref.shape)
    sums_ref[...] = jnp.concatenate([d_gain, jnp.zeros((7, chans), f32)], axis=0)


def pack_rows(chans):
    return chans + chans // 2


def chunk_rows(count, chans, planes):
    unit = 16 * planes
    return -(-count * pack_rows(chans) // unit) * unit


def wgrad_kernel(blocks, planes, *refs):
    xs, ys = refs[:4], refs[4:8]
    gain = refs[8][1:2]
    out_ref, plane, xk = refs[-3:]
    _, rows, cols, _ = ys[0].shape
    chans = gain.shape[1]
    tall = 4 * rows
    cells = 4 * tall * cols
    odd = lax.axis_index("tm") % 2 == 1
    p = lax.axis_index("height") % 4
    single = blocks == 2
    start = jnp.where(odd, 2, 0) if single else 0
    if single:
        plane[pl.ds(jnp.where(odd, 0, 4), 2)] = jnp.zeros((2,) + plane.shape[1:], bf16)

    def put_y(values, row, count):
        for b in range(blocks):
            for f in range(2):
                part = values[b, :, :, f * chans : (f + 1) * chans]
                place = (start + 2 * b + f, pl.ds(row, count))

                @pl.when(odd)
                def _():
                    flat = part.astype(f32).reshape(-1, chans)
                    plane[place] = norm_silu(flat, gain).astype(bf16).reshape(part.shape)

                @pl.when(jnp.logical_not(odd))
                def _():
                    plane[place] = part

    for d in range(4):
        at = p ^ d
        put_y(ys[d][...], 1 + rows * at, rows)
        for b in range(2):
            for f in range(2):
                part = xs[d][b, :rows, :, f * chans : (f + 1) * chans]
                wide = part.astype(f32)
                place = (2 * b + f, pl.ds(rows * at, rows))
                xk[(0,) + place] = shift_cols(wide, 1).astype(bf16)
                xk[(1,) + place] = part
                xk[(2,) + place] = shift_cols(wide, -1).astype(bf16)

        @pl.when(at == 0)
        def _():
            put_y(xs[d][:, rows:], 0, 1)

        @pl.when(at == 3)
        def _():
            put_y(xs[d][:, rows:], tall + 1, 1)

    step = pack_rows(chans)
    dims = (((0,), (0,)), ((), ()))
    half = chans // 2
    offset = 0
    for first, count in chunks:
        share = chunk_rows(count, chans, planes) // planes

        def put(row, values, offset=offset, share=share):
            at = 0
            while at < values.shape[0]:
                q, r = divmod(row + at, share)
                n = min(share - r, values.shape[0] - at)
                out_ref[q, offset + r : offset + r + n] = values[at : at + n]
                at += n

        def store(row, grad, put=put):
            grad = grad.astype(bf16)
            put(row, grad[:, :128])
            put(row + chans, jnp.concatenate([grad[:half, 128:], grad[half:, 128:]], axis=1))

        for j in range(count):
            tap = jnp.minimum(p * taps_each + first + j, taps_all - 1)
            t, h, k = tap // 9, tap // 3 % 3, tap % 3

            @pl.when(odd)
            def _():
                piece = plane[pl.ds(t, 4), pl.ds(h, tall)].reshape(cells, chans)
                x = xk[k].reshape(cells, chans)
                store(j * step, lax.dot_general(piece, x, dims, preferred_element_type=f32))

            @pl.when(jnp.logical_not(odd))
            def _():
                piece = plane[pl.ds(2 - t, 4), pl.ds(2 - h, tall)].reshape(cells, chans)
                x = xk[2 - k].reshape(cells, chans)
                store(j * step, lax.dot_general(x, piece, dims, preferred_element_type=f32))

        spare = share * planes - count * step
        if spare:
            put(count * step, jnp.zeros((spare, 128), bf16))
        offset += share


def halves(total):
    high = total.astype(bf16)
    return jnp.concatenate([high, (total - high.astype(f32)).astype(bf16)])


def assemble_kernel(planes, size, *refs):
    pieces, out_ref = refs[:planes], refs[-1]
    q = lax.axis_index("height") // 4
    for d, piece in enumerate(pieces):
        start = pl.multiple_of((q - d + planes) % planes * size, 16)
        out_ref[pl.ds(start, size)] = piece[:size]
    if pieces[0].shape[0] > size:
        total = functools.reduce(lambda a, b: a + b, [piece[size:].astype(f32) for piece in pieces])
        half = total.shape[0] // 2
        out_ref[planes * size :] = halves(total[:half] + total[half:])


def unpack_kernel(taps, held, *refs):
    pieces = refs[:8]
    outs, stage, sems = refs[8 + 2 * held : 10 + 2 * held], refs[-2], refs[-1]
    first, count = taps
    chans = stage.shape[1]
    half = chans // 2
    step = pack_rows(chans)
    odd = lax.axis_index("tm") % 2 == 1
    p = lax.axis_index("height") % 4
    made = []
    for n, src in enumerate(pieces):
        for j in range(count):
            tap = (p ^ (n % 4)) * taps_each + first + j
            slot = n * count + j
            high = src[j * step + chans : (j + 1) * step]
            stage[slot, :, :128] = src[j * step : j * step + chans]
            stage[slot, :half, 128:] = high[:, : chans - 128]
            stage[slot, half:, 128:] = high[:, chans - 128 :]
            real = tap < taps_all
            tap = jnp.minimum(tap, taps_all - 1)
            for which in range(2):
                good = odd if (which == 0) == (n < 4) else jnp.logical_not(odd)
                good = jnp.logical_and(good, real)
                copy = pltpu.make_async_copy(stage.at[slot], outs[which].at[tap], sems.at[slot])
                pl.when(good)(copy.start)
                made.append((good, copy))
    for good, copy in made:
        pl.when(good)(copy.wait)


vmem = pl.BlockSpec(memory_space=pltpu.VMEM)
anywhere = pl.BlockSpec(memory_space=pl.ANY)
in_hbm = pl.BlockSpec(memory_space=pltpu.HBM)


def call(kernel, outs, args, us, mib, scratch=(), free=(), hbm=(), out_spec=vmem, **kw):
    return pl.pallas_call(
        kernel,
        out_shape=outs,
        in_specs=[in_hbm if i in hbm else anywhere if i in free else vmem for i in range(len(args))],
        out_specs=[out_spec] * len(outs),
        scratch_shapes=list(scratch),
        compiler_params=pltpu.CompilerParams(vmem_limit_bytes=mib * 2**20),
        cost_estimate=pl.CostEstimate(flops=int(us * 1.1e9), bytes_accessed=1024, transcendentals=0),
        **kw,
    )(*args)


def moved(value, axis, by):
    size = lax.axis_size(axis)
    return lax.ppermute(value, axis, [(i, i + by) for i in range(size) if 0 <= i + by < size])


def total_of(pieces):
    return functools.reduce(lambda a, b: a + b, [p.astype(f32) for p in pieces])


def piece_at(value, index):
    return lax.dynamic_index_in_dim(value, index, 0, keepdims=False)


def body(features, weight_one, bias_one, gain_one, weight_two, bias_two, gain_two, cotangent):
    frames, rows, cols, chans = features.shape
    tm, height = lax.axis_size("tm"), lax.axis_size("height")
    planes = height // 4
    c, me = lax.axis_index("tm"), lax.axis_index("height")
    odd = c % 2 == 1
    p, q = me % 4, me // 4
    swap = [(i, i ^ 1) for i in range(tm)]
    line = lambda v: v.reshape(1, chans)
    local = jax.ShapeDtypeStruct(features.shape, bf16)
    sums = jax.ShapeDtypeStruct((8, chans), f32)
    window = pltpu.VMEM((frames + 2, rows + 2, cols, chans), bf16)
    packed_shape = jax.ShapeDtypeStruct((rows, cols, 2 * chans), bf16)

    def plane_move(value, d):
        return lax.ppermute(value, "height", [(i, i ^ d) for i in range(height)])

    def column_move(value, d):
        pairs = [(z * 4 + j, (z + d) % planes * 4 + j) for z in range(planes) for j in range(4)]
        return lax.ppermute(value, "height", pairs)

    pair = tm == 2
    blocks = 2 if pair else 3
    messages = (jax.ShapeDtypeStruct((3 if pair else 4, cols, 2 * chans), bf16),) * 2
    y_shape = jax.ShapeDtypeStruct((blocks, rows, cols, 2 * chans), bf16)
    x_shape = jax.ShapeDtypeStruct((blocks, rows + 1, cols, 2 * chans), bf16)
    raw_give, raw_keep = jnp.where(odd, cotangent, features), jnp.where(odd, features, cotangent)
    if pair:
        far = (lax.ppermute(raw_give, "tm", swap),)
        extra = ()
    else:
        far = (moved(features, "tm", 1), moved(cotangent, "tm", -1))
        extra = (lax.ppermute(jnp.where(odd, far[1], far[0]), "tm", swap),)
    held = jax.ShapeDtypeStruct(weight_one.shape, bf16)
    w1, w2, vec = call(
        fetch_kernel,
        (held, held, jax.ShapeDtypeStruct((8, chans), f32)),
        (weight_one, weight_two, line(bias_one), line(gain_one), line(bias_two), line(gain_two)),
        3,
        8,
        [pltpu.SemaphoreType.DMA((6,))],
        hbm=range(6),
    )
    y_own, up, down = call(join_first_kernel, (y_shape, *messages), (raw_keep, raw_give, *far, *extra), 1, 8)
    above, below = moved(up, "height", 1), moved(down, "height", -1)
    ys = [y_own] + [plane_move(y_own, d) for d in (1, 2, 3)]

    give, keep, sums_one = call(
        first_kernel,
        (packed_shape, packed_shape, sums),
        (*ys[1:], raw_keep, raw_give, jnp.stack(far), above, below, w1, w2, vec),
        5,
        20,
        [window, window],
        free=(0, 1, 2),
    )
    other = lax.ppermute(give, "tm", swap)
    if pair:
        (x_own,) = call(join_edge_kernel, (x_shape,), (keep, other, above, below), 1, 6)
        far = lax.ppermute(keep, "tm", swap)[None]
    else:
        edge = jnp.where(p == 0, above, below)
        extra = lax.ppermute(jnp.where(odd, edge[3], edge[0]), "tm", swap)
        edge = jnp.where(odd, jnp.stack([extra, edge[0], edge[1]]), jnp.stack([edge[2], edge[3], extra]))
        x_own = jnp.where(odd, jnp.stack([other, keep, keep]), jnp.stack([keep, other, other]))
        x_own = jnp.concatenate([x_own, edge[:, None]], axis=1)
        act2, gmid = jnp.where(odd, give, keep), jnp.where(odd, keep, give)
        far = jnp.stack([moved(act2, "tm", 1), moved(gmid, "tm", -1)])
    xs = [x_own] + [plane_move(x_own, d) for d in (1, 2, 3)]
    up, down = call(gate_kernel, messages, (keep, give, far, xs[1]), 1, 6, free=(3,))
    above, below = moved(up, "height", 1), moved(down, "height", -1)

    shares = [chunk_rows(count, chans, planes) // planes for _, count in chunks]
    (flat,) = call(
        functools.partial(wgrad_kernel, blocks, planes),
        (jax.ShapeDtypeStruct((planes, sum(shares), 128), bf16),),
        (*xs, *ys, vec),
        7,
        24,
        [
            pltpu.VMEM((2 * frames + 2, 4 * rows + 2, cols, chans), bf16),
            pltpu.VMEM((3, 2 * frames, 4 * rows, cols, chans), bf16),
        ],
    )
    arrived = [column_move(piece_at(flat, (q + d) % planes), d) for d in range(1, planes)]
    part = total_of([piece_at(flat, q), *arrived])
    hop = 2
    while hop < tm:
        part = part + lax.ppermute(part, "tm", [(i, i ^ hop) for i in range(tm)])
        hop *= 2
    part = part.astype(bf16)
    parts = jnp.split(part, [sum(shares[:n]) for n in range(1, len(shares))])

    block_out, grad_input, sums_two = call(
        last_kernel,
        (local, local, sums),
        (keep, give, far, above, below, raw_keep, raw_give, w1, w2, vec),
        6,
        20,
        [window, window],
    )

    small = jnp.concatenate([sums_one[:3], sums_two[:1]]).reshape(-1, 128)
    used = small.shape[0]
    count = -(-used // 8) * 8
    small = jnp.pad(small, ((0, count - used), (0, 0)))

    hop = 2
    while hop < tm:
        small = small + lax.ppermute(small, "tm", [(i, i ^ hop) for i in range(tm)])
        hop *= 2

    gradient = jax.ShapeDtypeStruct((taps_all, chans, chans), bf16)
    grads, gate = (), ()
    for n, (part, taps) in enumerate(zip(parts, chunks)):
        last = n == len(parts) - 1
        size = part.shape[0]
        send = jnp.concatenate([part, halves(small)]) if last else part
        got = [send] + [column_move(send, d) for d in range(1, planes)]
        (send,) = call(
            functools.partial(assemble_kernel, planes, size),
            (jax.ShapeDtypeStruct((planes * size + send.shape[0] - size, 128), bf16),),
            got,
            1,
            6,
        )
        one, two = plane_move(send, 1), plane_move(send, 2)
        cut = send.shape[0] // 32 * 16
        if False:
            three = jnp.concatenate([plane_move(two[:cut], 1), plane_move(one[cut:], 2)])
        else:
            three = plane_move(send, 3)
        got = [send, one, two, three]
        others = [lax.ppermute(g, "tm", swap) for g in got]
        if last:
            small = total_of([v[planes * size :] for v in got + others])
            small = (small[:count] + small[count:])[:used]
        held = len(grads) > 0
        grads = call(
            functools.partial(unpack_kernel, taps, held),
            (gradient, gradient),
            (*got, *others, *grads),
            2,
            12,
            [pltpu.VMEM((8 * taps[1], chans, chans), bf16), pltpu.SemaphoreType.DMA((8 * taps[1],))],
            free=(8, 9) if held else (),
            out_spec=anywhere,
            input_output_aliases={8: 0, 9: 1} if held else {},
        )
    grad_one, grad_two = grads
    shape = weight_one.shape
    small = small.reshape(4, chans).astype(bf16)
    return (
        block_out,
        grad_input,
        grad_one.reshape(shape),
        grad_two.reshape(shape),
        small[1],
        small[2],
        small[3],
        small[0],
    )


def solution(mesh):
    split = P("tm", "height", None, None)
    return jax.shard_map(
        body,
        mesh=mesh,
        in_specs=(split, P(), P(), P(), P(), P(), P(), split),
        out_specs=(split, split, P(), P(), P(), P(), P(), P()),
        check_vma=False,
    )
```

```python
import functools

import jax
import jax.numpy as jnp
from jax import lax
from jax.experimental import pallas as pl
from jax.experimental.pallas import tpu as pltpu
from jax.sharding import PartitionSpec as P

epsilon = 1e-06
bf16 = jnp.bfloat16
f32 = jnp.float32
chunks = ((0, 3), (3, 4))
taps_each = 7
taps_all = 27


def shift_cols(value, by):
    zero = jnp.zeros_like(value[:, :1])
    if by == 1:
        return jnp.concatenate([value[:, 1:], zero], axis=1)
    return jnp.concatenate([zero, value[:, :-1]], axis=1)


def norm_parts(vals, gain):
    scale = lax.rsqrt(jnp.mean(vals * vals, axis=-1, keepdims=True) + epsilon)
    normed = vals * scale
    lifted = normed * gain
    return scale, normed, lifted, jax.nn.sigmoid(lifted)


def norm_silu(vals, gain):
    _, _, lifted, sig = norm_parts(vals, gain)
    return lifted * sig


def norm_silu_back(grad, vals, gain):
    scale, normed, lifted, sig = norm_parts(vals, gain)
    d_lift = grad * sig * (1.0 + lifted * (1.0 - sig))
    d_gain = jnp.sum(d_lift * normed, axis=0, keepdims=True)
    d_norm = d_lift * gain
    d_vals = scale * (d_norm - normed * jnp.mean(d_norm * normed, axis=-1, keepdims=True))
    return d_vals, d_gain


def conv(window, weight, frames, rows, back):
    cols, chans = window.shape[2], window.shape[3]
    parts = [None] * 3
    for t in range(3):
        for h in range(3):
            t0, h0 = (2 - t, 2 - h) if back else (t, h)
            piece = window[t0 : t0 + frames, h0 : h0 + rows].reshape(frames * rows * cols, chans)
            for k in range(3):
                dims = (((1,), (1 if back else 0,)), ((), ()))
                prod = lax.dot_general(piece, weight[t, h, k], dims, preferred_element_type=f32)
                parts[k] = prod if parts[k] is None else parts[k] + prod
    parts = [part.reshape(frames * rows, cols, chans) for part in parts]
    sign = -1 if back else 1
    total = parts[1] + shift_cols(parts[0], -sign) + shift_cols(parts[2], sign)
    return total.reshape(frames * rows * cols, chans)


def is_odd():
    return lax.axis_index("tm") % 2 == 1


def by_core(odd_fn, even_fn):
    pl.when(is_odd())(odd_fn)
    pl.when(jnp.logical_not(is_odd()))(even_fn)


def fill_packed(window, at, rows, packed):
    chans = window.shape[3]
    for f in range(2):
        window[at + f, rows] = packed[..., f * chans : (f + 1) * chans]


def fill_far(ahead, behind, far, rows):
    def put(window, at, value):
        if value.shape[-1] == window.shape[3]:
            window[pl.ds(at, 2), rows] = value
        else:
            fill_packed(window, at, rows, value)

    if far.shape[0] == 2:
        put(ahead, 0, far[0])
        put(behind, 2, far[1])
        return
    zero = jnp.zeros(far.shape[1:], bf16)

    def odd():
        put(ahead, 0, far[0])
        put(behind, 2, zero)

    def even():
        put(ahead, 0, zero)
        put(behind, 2, far[0])

    by_core(odd, even)


def fill_edges(ahead, behind, above, below):
    last = ahead.shape[1] - 1
    places = ((ahead, 0), (ahead, 2), (behind, 0), (behind, 2))
    for row, edges in ((0, above), (last, below)):
        rows = pl.ds(row, 1)
        if edges.shape[0] == 4:
            for i, (window, at) in enumerate(places):
                fill_packed(window, at, rows, edges[i : i + 1])
            continue
        zero = jnp.zeros((1,) + edges.shape[1:], bf16)

        def odd():
            for i, (window, at) in enumerate(places):
                fill_packed(window, at, rows, edges[i : i + 1] if i < 3 else zero)

        def even():
            for i, (window, at) in enumerate(places):
                fill_packed(window, at, rows, edges[i - 1 : i] if i > 0 else zero)

        by_core(odd, even)


def started(copies, sems):
    made = [pltpu.make_async_copy(src, dst, sems.at[i]) for i, (src, dst) in enumerate(copies)]
    for copy in made:
        copy.start()
    return made


def pack_frames(values):
    return jnp.concatenate([values[0], values[1]], axis=-1)


def put_messages(groups, up_ref, down_ref):
    for i, value in enumerate(groups):
        up_ref[i] = value[value.shape[0] - 1]
        down_ref[i] = value[0]


def join_first_kernel(*refs):
    refs, (y_ref, up_ref, down_ref) = refs[:-3], refs[-3:]
    keep, give, *far = [pack_frames(ref) for ref in refs]
    if len(far) == 1:

        def odd():
            y_ref[0], y_ref[1] = far[0], keep
            put_messages((far[0], keep, give), up_ref, down_ref)

        def even():
            y_ref[0], y_ref[1] = keep, far[0]
            put_messages((give, keep, far[0]), up_ref, down_ref)

    else:

        def odd():
            y_ref[0], y_ref[1], y_ref[2] = far[2], far[0], keep
            put_messages((far[0], keep, give, far[1]), up_ref, down_ref)

        def even():
            y_ref[0], y_ref[1], y_ref[2] = keep, far[1], far[2]
            put_messages((far[0], give, keep, far[1]), up_ref, down_ref)

    by_core(odd, even)


def gate_kernel(keep_ref, give_ref, far_ref, _, up_ref, down_ref):
    keep, give, far = keep_ref[...], give_ref[...], far_ref[...]

    def odd():
        put_messages((far[0], give, keep, far[-1])[: up_ref.shape[0]], up_ref, down_ref)

    def even():
        put_messages((far[0], keep, give, far[-1])[4 - up_ref.shape[0] :], up_ref, down_ref)

    by_core(odd, even)


def join_edge_kernel(keep_ref, other_ref, above_ref, below_ref, out_ref):
    rows = keep_ref.shape[0]
    top = lax.axis_index("height") % 4 == 0
    edge = jnp.where(top, above_ref[...], below_ref[...])

    def odd():
        out_ref[0, :rows], out_ref[1, :rows] = other_ref[...], keep_ref[...]
        out_ref[0, rows], out_ref[1, rows] = edge[0], edge[1]

    def even():
        out_ref[0, :rows], out_ref[1, :rows] = keep_ref[...], other_ref[...]
        out_ref[0, rows], out_ref[1, rows] = edge[1], edge[2]

    by_core(odd, even)


def fetch_kernel(w1_any, w2_any, b1_any, g1_any, b2_any, g2_any, w1_ref, w2_ref, vec_ref, sems):
    vectors = [(ref, vec_ref.at[pl.ds(i, 1)]) for i, ref in enumerate((b1_any, g1_any, b2_any, g2_any))]
    for copy in started([(w1_any, w1_ref), (w2_any, w2_ref), *vectors], sems):
        copy.wait()


def first_kernel(
    _, __, ___, keep_in, give_in, far_ref, above_ref, below_ref, w1, w2, vec_ref,
    give_ref, keep_ref, sums_ref, ahead, behind,
):
    frames, rows, cols, chans = keep_in.shape
    own = pl.ds(1, rows)
    b1, g1, g2 = vec_ref[0:1], vec_ref[1:2], vec_ref[3:4]

    def odd_in():
        ahead[pl.ds(2, 2), own] = keep_in[...]
        behind[pl.ds(0, 2), own] = give_in[...]

    def even_in():
        ahead[pl.ds(2, 2), own] = give_in[...]
        behind[pl.ds(0, 2), own] = keep_in[...]

    by_core(odd_in, even_in)
    fill_far(ahead, behind, far_ref, own)
    fill_edges(ahead, behind, above_ref, below_ref)
    for f in range(frames + 2):
        vals = ahead[f].astype(f32).reshape(-1, chans)
        ahead[f] = norm_silu(vals, g1).astype(bf16).reshape(rows + 2, cols, chans)
    mid = (conv(ahead, w1, frames, rows, False) + b1).astype(bf16).astype(f32)
    act2 = norm_silu(mid, g2).astype(bf16).reshape(frames, rows, cols, chans)
    act2 = pack_frames(act2)
    grad = conv(behind, w2, frames, rows, True)
    gmid, d_gain = norm_silu_back(grad, mid, g2)
    gmid = gmid.astype(bf16)
    cot = behind[:2, 1 : rows + 1].astype(f32).reshape(-1, chans)
    sums_ref[...] = jnp.concatenate(
        [
            d_gain,
            jnp.sum(gmid.astype(f32), axis=0, keepdims=True),
            jnp.sum(cot, axis=0, keepdims=True),
            jnp.zeros((5, chans), f32),
        ],
        axis=0,
    )
    gmid = pack_frames(gmid.reshape(frames, rows, cols, chans))

    def odd():
        give_ref[...] = act2
        keep_ref[...] = gmid

    def even():
        give_ref[...] = gmid
        keep_ref[...] = act2

    by_core(odd, even)


def last_kernel(
    keep_ref, give_ref, far_ref, above_ref, below_ref, keep_in, give_in, w1, w2, vec_ref,
    out_ref, gin_ref, sums_ref, ahead, behind,
):
    frames, rows, cols, chans = out_ref.shape
    own = pl.ds(1, rows)
    g1, b2 = vec_ref[1:2], vec_ref[2:3]

    def odd():
        fill_packed(ahead, 2, own, give_ref[...])
        fill_packed(behind, 0, own, keep_ref[...])

    def even():
        fill_packed(ahead, 2, own, keep_ref[...])
        fill_packed(behind, 0, own, give_ref[...])

    by_core(odd, even)
    fill_far(ahead, behind, far_ref, own)
    fill_edges(ahead, behind, above_ref, below_ref)
    feat = jnp.where(is_odd(), keep_in[...], give_in[...]).astype(f32).reshape(-1, chans)
    out = feat + conv(ahead, w2, frames, rows, False) + b2
    out_ref[...] = out.astype(bf16).reshape(out_ref.shape)
    grad = conv(behind, w1, frames, rows, True)
    d_vals, d_gain = norm_silu_back(grad, feat, g1)
    gin = d_vals + jnp.where(is_odd(), give_in[...], keep_in[...]).astype(f32).reshape(-1, chans)
    gin_ref[...] = gin.astype(bf16).reshape(gin_ref.shape)
    sums_ref[...] = jnp.concatenate([d_gain, jnp.zeros((7, chans), f32)], axis=0)


def pack_rows(chans):
    return chans + chans // 2


def chunk_rows(count, chans, planes):
    unit = 16 * planes
    return -(-count * pack_rows(chans) // unit) * unit


def put_y(plane, blocks, values, row, count, gain):
    chans = plane.shape[3]
    base = jnp.where(is_odd(), 2, 0) if blocks == 2 else 0
    for b in range(blocks):
        for f in range(2):
            part = values[b, :, :, f * chans : (f + 1) * chans]
            place = (base + 2 * b + f, pl.ds(row, count))

            def odd():
                flat = part.astype(f32).reshape(-1, chans)
                plane[place] = norm_silu(flat, gain).astype(bf16).reshape(part.shape)

            def even():
                plane[place] = part

            by_core(odd, even)


def plane_kernel(blocks, *refs):
    ys, gain, plane = refs[:4], refs[4][1:2], refs[-1]
    rows = ys[0].shape[1]
    p = lax.axis_index("height") % 4
    if blocks == 2:
        plane[pl.ds(jnp.where(is_odd(), 0, 4), 2)] = jnp.zeros((2,) + plane.shape[1:], bf16)
    for d in range(4):
        put_y(plane, blocks, ys[d][...], 1 + rows * (p ^ d), rows, gain)


def wgrad_kernel(blocks, planes, *refs):
    xs, plane_in, gain = refs[:4], refs[4], refs[5][1:2]
    out_ref, plane, xk = refs[-3:]
    _, rows, cols, _ = xs[0].shape
    rows -= 1
    chans = plane.shape[3]
    tall = 4 * rows
    cells = 4 * tall * cols
    odd = is_odd()
    p = lax.axis_index("height") % 4
    plane[:, 1 : tall + 1] = plane_in[:, 1 : tall + 1]
    if blocks == 2:
        empty = jnp.zeros((2, 1, cols, chans), bf16)
        for row in (0, tall + 1):
            plane[pl.ds(jnp.where(odd, 0, 4), 2), row : row + 1] = empty
    for d in range(4):
        at = p ^ d
        for b in range(2):
            for f in range(2):
                part = xs[d][b, :rows, :, f * chans : (f + 1) * chans]
                wide = part.astype(f32)
                place = (2 * b + f, pl.ds(rows * at, rows))
                xk[(0,) + place] = shift_cols(wide, 1).astype(bf16)
                xk[(1,) + place] = part
                xk[(2,) + place] = shift_cols(wide, -1).astype(bf16)

        @pl.when(at == 0)
        def _():
            put_y(plane, blocks, xs[d][:, rows:], 0, 1, gain)

        @pl.when(at == 3)
        def _():
            put_y(plane, blocks, xs[d][:, rows:], tall + 1, 1, gain)

    step = pack_rows(chans)
    dims = (((0,), (0,)), ((), ()))
    half = chans // 2
    offset = 0
    for first, count in chunks:
        share = chunk_rows(count, chans, planes) // planes

        def put(row, values, offset=offset, share=share):
            at = 0
            while at < values.shape[0]:
                q, r = divmod(row + at, share)
                n = min(share - r, values.shape[0] - at)
                out_ref[q, offset + r : offset + r + n] = values[at : at + n]
                at += n

        def store(row, grad, put=put):
            grad = grad.astype(bf16)
            put(row, grad[:, :128])
            put(row + chans, jnp.concatenate([grad[:half, 128:], grad[half:, 128:]], axis=1))

        for j in range(count):
            tap = jnp.minimum(p * taps_each + first + j, taps_all - 1)
            t, h, k = tap // 9, tap // 3 % 3, tap % 3

            @pl.when(odd)
            def _():
                piece = plane[pl.ds(t, 4), pl.ds(h, tall)].reshape(cells, chans)
                x = xk[k].reshape(cells, chans)
                store(j * step, lax.dot_general(piece, x, dims, preferred_element_type=f32))

            @pl.when(jnp.logical_not(odd))
            def _():
                piece = plane[pl.ds(2 - t, 4), pl.ds(2 - h, tall)].reshape(cells, chans)
                x = xk[2 - k].reshape(cells, chans)
                store(j * step, lax.dot_general(x, piece, dims, preferred_element_type=f32))

        spare = share * planes - count * step
        if spare:
            put(count * step, jnp.zeros((spare, 128), bf16))
        offset += share


def halves(total):
    high = total.astype(bf16)
    return jnp.concatenate([high, (total - high.astype(f32)).astype(bf16)])


def assemble_kernel(planes, size, *refs):
    pieces, out_ref = refs[:planes], refs[-1]
    q = lax.axis_index("height") // 4
    for d, piece in enumerate(pieces):
        start = pl.multiple_of((q - d + planes) % planes * size, 16)
        out_ref[pl.ds(start, size)] = piece[:size]
    if pieces[0].shape[0] > size:
        total = functools.reduce(lambda a, b: a + b, [piece[size:].astype(f32) for piece in pieces])
        half = total.shape[0] // 2
        out_ref[planes * size :] = halves(total[:half] + total[half:])


def unpack_kernel(taps, held, *refs):
    pieces = refs[:8]
    outs, stage, sems = refs[8 + 2 * held : 10 + 2 * held], refs[-2], refs[-1]
    more = refs[10 + 2 * held : -2]
    first, count = taps
    chans = stage.shape[1]
    half = chans // 2
    step = pack_rows(chans)
    odd = lax.axis_index("tm") % 2 == 1
    p = lax.axis_index("height") % 4
    made = []
    for n, src in enumerate(pieces):
        for j in range(count):
            tap = (p ^ (n % 4)) * taps_each + first + j
            slot = n * count + j
            high = src[j * step + chans : (j + 1) * step]
            stage[slot, :, :128] = src[j * step : j * step + chans]
            stage[slot, :half, 128:] = high[:, : chans - 128]
            stage[slot, half:, 128:] = high[:, chans - 128 :]
            real = tap < taps_all
            tap = jnp.minimum(tap, taps_all - 1)
            for which in range(2):
                good = odd if (which == 0) == (n < 4) else jnp.logical_not(odd)
                good = jnp.logical_and(good, real)
                copy = pltpu.make_async_copy(stage.at[slot], outs[which].at[tap], sems.at[slot])
                pl.when(good)(copy.start)
                made.append((good, copy))
    if more:
        sums = functools.reduce(lambda a, b: a + b, [src[src.shape[0] - 16 :].astype(f32) for src in pieces])
        sums = sums[:8] + sums[8:]
        for i in range(4):
            row = jnp.concatenate([sums[2 * i : 2 * i + 1], sums[2 * i + 1 : 2 * i + 2, : chans - 128]], axis=1)
            more[0][i : i + 1] = row.astype(bf16)
    for good, copy in made:
        pl.when(good)(copy.wait)


vmem = pl.BlockSpec(memory_space=pltpu.VMEM)
anywhere = pl.BlockSpec(memory_space=pl.ANY)
in_hbm = pl.BlockSpec(memory_space=pltpu.HBM)


def call(kernel, outs, args, us, mib, scratch=(), free=(), hbm=(), out_specs=None, **kw):
    return pl.pallas_call(
        kernel,
        out_shape=outs,
        in_specs=[in_hbm if i in hbm else anywhere if i in free else vmem for i in range(len(args))],
        out_specs=out_specs or [vmem] * len(outs),
        scratch_shapes=list(scratch),
        compiler_params=pltpu.CompilerParams(vmem_limit_bytes=mib * 2**20),
        cost_estimate=pl.CostEstimate(flops=int(us * 1.1e9), bytes_accessed=1024, transcendentals=0),
        **kw,
    )(*args)


def moved(value, axis, by):
    size = lax.axis_size(axis)
    return lax.ppermute(value, axis, [(i, i + by) for i in range(size) if 0 <= i + by < size])


def total_of(pieces):
    return functools.reduce(lambda a, b: a + b, [p.astype(f32) for p in pieces])


def piece_at(value, index):
    return lax.dynamic_index_in_dim(value, index, 0, keepdims=False)


def body(features, weight_one, bias_one, gain_one, weight_two, bias_two, gain_two, cotangent):
    frames, rows, cols, chans = features.shape
    tm, height = lax.axis_size("tm"), lax.axis_size("height")
    planes = height // 4
    c, me = lax.axis_index("tm"), lax.axis_index("height")
    odd = c % 2 == 1
    p, q = me % 4, me // 4
    swap = [(i, i ^ 1) for i in range(tm)]
    line = lambda v: v.reshape(1, chans)
    local = jax.ShapeDtypeStruct(features.shape, bf16)
    sums = jax.ShapeDtypeStruct((8, chans), f32)
    window = pltpu.VMEM((frames + 2, rows + 2, cols, chans), bf16)
    packed_shape = jax.ShapeDtypeStruct((rows, cols, 2 * chans), bf16)

    def plane_move(value, d):
        return lax.ppermute(value, "height", [(i, i ^ d) for i in range(height)])

    def column_move(value, d):
        pairs = [(z * 4 + j, (z + d) % planes * 4 + j) for z in range(planes) for j in range(4)]
        return lax.ppermute(value, "height", pairs)

    pair = tm == 2
    blocks = 2 if pair else 3
    messages = (jax.ShapeDtypeStruct((3 if pair else 4, cols, 2 * chans), bf16),) * 2
    y_shape = jax.ShapeDtypeStruct((blocks, rows, cols, 2 * chans), bf16)
    x_shape = jax.ShapeDtypeStruct((blocks, rows + 1, cols, 2 * chans), bf16)
    raw_give, raw_keep = jnp.where(odd, cotangent, features), jnp.where(odd, features, cotangent)
    if pair:
        far = (lax.ppermute(raw_give, "tm", swap),)
        extra = ()
    else:
        far = (moved(features, "tm", 1), moved(cotangent, "tm", -1))
        extra = (lax.ppermute(jnp.where(odd, far[1], far[0]), "tm", swap),)
    held = jax.ShapeDtypeStruct(weight_one.shape, bf16)
    w1, w2, vec = call(
        fetch_kernel,
        (held, held, jax.ShapeDtypeStruct((8, chans), f32)),
        (weight_one, weight_two, line(bias_one), line(gain_one), line(bias_two), line(gain_two)),
        3,
        8,
        [pltpu.SemaphoreType.DMA((6,))],
        hbm=range(6),
    )
    y_own, up, down = call(join_first_kernel, (y_shape, *messages), (raw_keep, raw_give, *far, *extra), 1, 8)
    above, below = moved(up, "height", 1), moved(down, "height", -1)
    ys = [y_own] + [plane_move(y_own, d) for d in (1, 2, 3)]

    give, keep, sums_one = call(
        first_kernel,
        (packed_shape, packed_shape, sums),
        (*ys[1:], raw_keep, raw_give, jnp.stack(far), above, below, w1, w2, vec),
        5,
        20,
        [window, window],
        free=(0, 1, 2),
    )
    other = lax.ppermute(give, "tm", swap)
    if pair:
        (x_own,) = call(join_edge_kernel, (x_shape,), (keep, other, above, below), 1, 6)
        far = lax.ppermute(keep, "tm", swap)[None]
    else:
        edge = jnp.where(p == 0, above, below)
        extra = lax.ppermute(jnp.where(odd, edge[3], edge[0]), "tm", swap)
        edge = jnp.where(odd, jnp.stack([extra, edge[0], edge[1]]), jnp.stack([edge[2], edge[3], extra]))
        x_own = jnp.where(odd, jnp.stack([other, keep, keep]), jnp.stack([keep, other, other]))
        x_own = jnp.concatenate([x_own, edge[:, None]], axis=1)
        act2, gmid = jnp.where(odd, give, keep), jnp.where(odd, keep, give)
        far = jnp.stack([moved(act2, "tm", 1), moved(gmid, "tm", -1)])
    xs = [x_own] + [plane_move(x_own, d) for d in (1, 2, 3)]
    up, down = call(gate_kernel, messages, (keep, give, far, xs[1]), 1, 6, free=(3,))
    above, below = moved(up, "height", 1), moved(down, "height", -1)

    (plane,) = call(
        functools.partial(plane_kernel, blocks),
        (jax.ShapeDtypeStruct((2 * frames + 2, 4 * rows + 2, cols, chans), bf16),),
        (*ys, vec, x_own),
        3,
        8,
        free=(5,),
    )
    shares = [chunk_rows(count, chans, planes) // planes for _, count in chunks]
    (flat,) = call(
        functools.partial(wgrad_kernel, blocks, planes),
        (jax.ShapeDtypeStruct((planes, sum(shares), 128), bf16),),
        (*xs, plane, vec),
        6,
        24,
        [
            pltpu.VMEM((2 * frames + 2, 4 * rows + 2, cols, chans), bf16),
            pltpu.VMEM((3, 2 * frames, 4 * rows, cols, chans), bf16),
        ],
    )
    arrived = [column_move(piece_at(flat, (q + d) % planes), d) for d in range(1, planes)]
    part = total_of([piece_at(flat, q), *arrived])
    hop = 2
    while hop < tm:
        part = part + lax.ppermute(part, "tm", [(i, i ^ hop) for i in range(tm)])
        hop *= 2
    part = part.astype(bf16)
    parts = jnp.split(part, [sum(shares[:n]) for n in range(1, len(shares))])

    block_out, grad_input, sums_two = call(
        last_kernel,
        (local, local, sums),
        (keep, give, far, above, below, raw_keep, raw_give, w1, w2, vec),
        6,
        20,
        [window, window],
    )

    small = jnp.concatenate([sums_one[:3], sums_two[:1]])
    small = jnp.pad(small, ((0, 0), (0, -chans % 128))).reshape(-1, 128)

    hop = 2
    while hop < tm:
        small = small + lax.ppermute(small, "tm", [(i, i ^ hop) for i in range(tm)])
        hop *= 2

    gradient = jax.ShapeDtypeStruct((taps_all, chans, chans), bf16)
    grads, gate = (), ()
    for n, (part, taps) in enumerate(zip(parts, chunks)):
        last = n == len(parts) - 1
        size = part.shape[0]
        send = jnp.concatenate([part, halves(small)]) if last else part
        got = [send] + [column_move(send, d) for d in range(1, planes)]
        (send,) = call(
            functools.partial(assemble_kernel, planes, size),
            (jax.ShapeDtypeStruct((planes * size + send.shape[0] - size, 128), bf16),),
            got,
            1,
            6,
        )
        one, two = plane_move(send, 1), plane_move(send, 2)
        cut = send.shape[0] // 32 * 16
        if False:
            three = jnp.concatenate([plane_move(two[:cut], 1), plane_move(one[cut:], 2)])
        else:
            three = plane_move(send, 3)
        got = [send, one, two, three]
        others = [lax.ppermute(g, "tm", swap) for g in got]
        held = len(grads) > 0
        grads = call(
            functools.partial(unpack_kernel, taps, held),
            (gradient, gradient) + (jax.ShapeDtypeStruct((4, chans), bf16),) * last,
            (*got, *others, *grads),
            2,
            12,
            [pltpu.VMEM((8 * taps[1], chans, chans), bf16), pltpu.SemaphoreType.DMA((8 * taps[1],))],
            free=(8, 9) if held else (),
            out_specs=[anywhere, anywhere] + [vmem] * last,
            input_output_aliases={8: 0, 9: 1} if held else {},
        )
    grad_one, grad_two, small = grads
    shape = weight_one.shape
    return (
        block_out,
        grad_input,
        grad_one.reshape(shape),
        grad_two.reshape(shape),
        small[1],
        small[2],
        small[3],
        small[0],
    )


def solution(mesh):
    split = P("tm", "height", None, None)
    return jax.shard_map(
        body,
        mesh=mesh,
        in_specs=(split, P(), P(), P(), P(), P(), P(), split),
        out_specs=(split, split, P(), P(), P(), P(), P(), P()),
        check_vma=False,
    )
```

```python
import functools

import jax
import jax.numpy as jnp
from jax import lax
from jax.experimental import pallas as pl
from jax.experimental.pallas import tpu as pltpu
from jax.sharding import PartitionSpec as P

epsilon = 1e-06
bf16 = jnp.bfloat16
f32 = jnp.float32
chunks = ((0, 3), (3, 4))
taps_each = 7
taps_all = 27


def shift_cols(value, by):
    zero = jnp.zeros_like(value[:, :1])
    if by == 1:
        return jnp.concatenate([value[:, 1:], zero], axis=1)
    return jnp.concatenate([zero, value[:, :-1]], axis=1)


def norm_parts(vals, gain):
    scale = lax.rsqrt(jnp.mean(vals * vals, axis=-1, keepdims=True) + epsilon)
    normed = vals * scale
    lifted = normed * gain
    return scale, normed, lifted, jax.nn.sigmoid(lifted)


def norm_silu(vals, gain):
    _, _, lifted, sig = norm_parts(vals, gain)
    return lifted * sig


def norm_silu_back(grad, vals, gain):
    scale, normed, lifted, sig = norm_parts(vals, gain)
    d_lift = grad * sig * (1.0 + lifted * (1.0 - sig))
    d_gain = jnp.sum(d_lift * normed, axis=0, keepdims=True)
    d_norm = d_lift * gain
    d_vals = scale * (d_norm - normed * jnp.mean(d_norm * normed, axis=-1, keepdims=True))
    return d_vals, d_gain


def conv(window, weight, frames, rows, back):
    cols, chans = window.shape[2], window.shape[3]
    parts = [None] * 3
    for t in range(3):
        for h in range(3):
            t0, h0 = (2 - t, 2 - h) if back else (t, h)
            piece = window[t0 : t0 + frames, h0 : h0 + rows].reshape(frames * rows * cols, chans)
            for k in range(3):
                dims = (((1,), (1 if back else 0,)), ((), ()))
                prod = lax.dot_general(piece, weight[t, h, k], dims, preferred_element_type=f32)
                parts[k] = prod if parts[k] is None else parts[k] + prod
    parts = [part.reshape(frames * rows, cols, chans) for part in parts]
    sign = -1 if back else 1
    total = parts[1] + shift_cols(parts[0], -sign) + shift_cols(parts[2], sign)
    return total.reshape(frames * rows * cols, chans)


def is_odd():
    return lax.axis_index("tm") % 2 == 1


def by_core(odd_fn, even_fn):
    pl.when(is_odd())(odd_fn)
    pl.when(jnp.logical_not(is_odd()))(even_fn)


def fill_packed(window, at, rows, packed):
    chans = window.shape[3]
    for f in range(2):
        window[at + f, rows] = packed[..., f * chans : (f + 1) * chans]


def fill_far(ahead, behind, far, rows):
    def put(window, at, value):
        if value.shape[-1] == window.shape[3]:
            window[pl.ds(at, 2), rows] = value
        else:
            fill_packed(window, at, rows, value)

    if far.shape[0] == 2:
        put(ahead, 0, far[0])
        put(behind, 2, far[1])
        return
    zero = jnp.zeros(far.shape[1:], bf16)

    def odd():
        put(ahead, 0, far[0])
        put(behind, 2, zero)

    def even():
        put(ahead, 0, zero)
        put(behind, 2, far[0])

    by_core(odd, even)


def fill_edges(ahead, behind, above, below):
    last = ahead.shape[1] - 1
    places = ((ahead, 0), (ahead, 2), (behind, 0), (behind, 2))
    for row, edges in ((0, above), (last, below)):
        rows = pl.ds(row, 1)
        if edges.shape[0] == 4:
            for i, (window, at) in enumerate(places):
                fill_packed(window, at, rows, edges[i : i + 1])
            continue
        zero = jnp.zeros((1,) + edges.shape[1:], bf16)

        def odd():
            for i, (window, at) in enumerate(places):
                fill_packed(window, at, rows, edges[i : i + 1] if i < 3 else zero)

        def even():
            for i, (window, at) in enumerate(places):
                fill_packed(window, at, rows, edges[i - 1 : i] if i > 0 else zero)

        by_core(odd, even)


def started(copies, sems):
    made = [pltpu.make_async_copy(src, dst, sems.at[i]) for i, (src, dst) in enumerate(copies)]
    for copy in made:
        copy.start()
    return made


def pack_frames(values):
    return jnp.concatenate([values[0], values[1]], axis=-1)


def put_messages(groups, up_ref, down_ref):
    for i, value in enumerate(groups):
        up_ref[i] = value[value.shape[0] - 1]
        down_ref[i] = value[0]


def join_first_kernel(*refs):
    refs, (y_ref, up_ref, down_ref) = refs[:-3], refs[-3:]
    keep, give, *far = [pack_frames(ref) for ref in refs]
    if len(far) == 1:

        def odd():
            y_ref[0], y_ref[1] = far[0], keep
            put_messages((far[0], keep, give), up_ref, down_ref)

        def even():
            y_ref[0], y_ref[1] = keep, far[0]
            put_messages((give, keep, far[0]), up_ref, down_ref)

    else:

        def odd():
            y_ref[0], y_ref[1], y_ref[2] = far[2], far[0], keep
            put_messages((far[0], keep, give, far[1]), up_ref, down_ref)

        def even():
            y_ref[0], y_ref[1], y_ref[2] = keep, far[1], far[2]
            put_messages((far[0], give, keep, far[1]), up_ref, down_ref)

    by_core(odd, even)


def gate_kernel(keep_ref, give_ref, far_ref, _, up_ref, down_ref):
    keep, give, far = keep_ref[...], give_ref[...], far_ref[...]

    def odd():
        put_messages((far[0], give, keep, far[-1])[: up_ref.shape[0]], up_ref, down_ref)

    def even():
        put_messages((far[0], keep, give, far[-1])[4 - up_ref.shape[0] :], up_ref, down_ref)

    by_core(odd, even)


def join_edge_kernel(keep_ref, other_ref, above_ref, below_ref, out_ref):
    rows = keep_ref.shape[0]
    top = lax.axis_index("height") % 4 == 0
    edge = jnp.where(top, above_ref[...], below_ref[...])

    def odd():
        out_ref[0, :rows], out_ref[1, :rows] = other_ref[...], keep_ref[...]
        out_ref[0, rows], out_ref[1, rows] = edge[0], edge[1]

    def even():
        out_ref[0, :rows], out_ref[1, :rows] = keep_ref[...], other_ref[...]
        out_ref[0, rows], out_ref[1, rows] = edge[1], edge[2]

    by_core(odd, even)


def fetch_kernel(w1_any, w2_any, b1_any, g1_any, b2_any, g2_any, w1_ref, w2_ref, vec_ref, sems):
    vectors = [(ref, vec_ref.at[pl.ds(i, 1)]) for i, ref in enumerate((b1_any, g1_any, b2_any, g2_any))]
    for copy in started([(w1_any, w1_ref), (w2_any, w2_ref), *vectors], sems):
        copy.wait()


def first_kernel(
    _, __, ___, keep_in, give_in, far_ref, above_ref, below_ref, w1, w2, vec_ref,
    give_ref, keep_ref, sums_ref, ahead, behind,
):
    frames, rows, cols, chans = keep_in.shape
    own = pl.ds(1, rows)
    b1, g1, g2 = vec_ref[0:1], vec_ref[1:2], vec_ref[3:4]

    def odd_in():
        ahead[pl.ds(2, 2), own] = keep_in[...]
        behind[pl.ds(0, 2), own] = give_in[...]

    def even_in():
        ahead[pl.ds(2, 2), own] = give_in[...]
        behind[pl.ds(0, 2), own] = keep_in[...]

    by_core(odd_in, even_in)
    fill_far(ahead, behind, far_ref, own)
    fill_edges(ahead, behind, above_ref, below_ref)
    for f in range(frames + 2):
        vals = ahead[f].astype(f32).reshape(-1, chans)
        ahead[f] = norm_silu(vals, g1).astype(bf16).reshape(rows + 2, cols, chans)
    mid = (conv(ahead, w1, frames, rows, False) + b1).astype(bf16).astype(f32)
    act2 = norm_silu(mid, g2).astype(bf16).reshape(frames, rows, cols, chans)
    act2 = pack_frames(act2)
    grad = conv(behind, w2, frames, rows, True)
    gmid, d_gain = norm_silu_back(grad, mid, g2)
    gmid = gmid.astype(bf16)
    cot = behind[:2, 1 : rows + 1].astype(f32).reshape(-1, chans)
    sums_ref[...] = jnp.concatenate(
        [
            d_gain,
            jnp.sum(gmid.astype(f32), axis=0, keepdims=True),
            jnp.sum(cot, axis=0, keepdims=True),
            jnp.zeros((5, chans), f32),
        ],
        axis=0,
    )
    gmid = pack_frames(gmid.reshape(frames, rows, cols, chans))

    def odd():
        give_ref[...] = act2
        keep_ref[...] = gmid

    def even():
        give_ref[...] = gmid
        keep_ref[...] = act2

    by_core(odd, even)


def last_kernel(
    keep_ref, give_ref, far_ref, above_ref, below_ref, keep_in, give_in, w1, w2, vec_ref,
    out_ref, gin_ref, sums_ref, ahead, behind,
):
    frames, rows, cols, chans = out_ref.shape
    own = pl.ds(1, rows)
    g1, b2 = vec_ref[1:2], vec_ref[2:3]

    def odd():
        fill_packed(ahead, 2, own, give_ref[...])
        fill_packed(behind, 0, own, keep_ref[...])

    def even():
        fill_packed(ahead, 2, own, keep_ref[...])
        fill_packed(behind, 0, own, give_ref[...])

    by_core(odd, even)
    fill_far(ahead, behind, far_ref, own)
    fill_edges(ahead, behind, above_ref, below_ref)
    feat = jnp.where(is_odd(), keep_in[...], give_in[...]).astype(f32).reshape(-1, chans)
    out = feat + conv(ahead, w2, frames, rows, False) + b2
    out_ref[...] = out.astype(bf16).reshape(out_ref.shape)
    grad = conv(behind, w1, frames, rows, True)
    d_vals, d_gain = norm_silu_back(grad, feat, g1)
    gin = d_vals + jnp.where(is_odd(), give_in[...], keep_in[...]).astype(f32).reshape(-1, chans)
    gin_ref[...] = gin.astype(bf16).reshape(gin_ref.shape)
    sums_ref[...] = jnp.concatenate([d_gain, jnp.zeros((7, chans), f32)], axis=0)


def pack_rows(chans):
    return chans + chans // 2


def chunk_rows(count, chans, planes):
    unit = 16 * planes
    return -(-count * pack_rows(chans) // unit) * unit


def put_y(plane, blocks, values, row, count, gain):
    chans = plane.shape[3]
    base = jnp.where(is_odd(), 2, 0) if blocks == 2 else 0
    for b in range(blocks):
        for f in range(2):
            part = values[b, :, :, f * chans : (f + 1) * chans]
            place = (base + 2 * b + f, pl.ds(row, count))

            def odd():
                flat = part.astype(f32).reshape(-1, chans)
                plane[place] = norm_silu(flat, gain).astype(bf16).reshape(part.shape)

            def even():
                plane[place] = part

            by_core(odd, even)


def plane_kernel(blocks, *refs):
    ys, gain, plane = refs[:4], refs[4][1:2], refs[-1]
    rows = ys[0].shape[1]
    p = lax.axis_index("height") % 4
    if blocks == 2:
        plane[pl.ds(jnp.where(is_odd(), 0, 4), 2)] = jnp.zeros((2,) + plane.shape[1:], bf16)
    for d in range(4):
        put_y(plane, blocks, ys[d][...], 1 + rows * (p ^ d), rows, gain)


def wgrad_kernel(blocks, planes, *refs):
    xs, plane_in, gain = refs[:4], refs[4], refs[5][1:2]
    out_ref, plane, xk = refs[-3:]
    _, rows, cols, _ = xs[0].shape
    rows -= 1
    chans = plane.shape[3]
    tall = 4 * rows
    cells = 4 * tall * cols
    odd = is_odd()
    p = lax.axis_index("height") % 4
    plane[:, 1 : tall + 1] = plane_in[:, 1 : tall + 1]
    if blocks == 2:
        empty = jnp.zeros((2, 1, cols, chans), bf16)
        for row in (0, tall + 1):
            plane[pl.ds(jnp.where(odd, 0, 4), 2), row : row + 1] = empty
    for d in range(4):
        at = p ^ d
        for b in range(2):
            for f in range(2):
                part = xs[d][b, :rows, :, f * chans : (f + 1) * chans]
                wide = part.astype(f32)
                place = (2 * b + f, pl.ds(rows * at, rows))
                xk[(0,) + place] = shift_cols(wide, 1).astype(bf16)
                xk[(1,) + place] = part
                xk[(2,) + place] = shift_cols(wide, -1).astype(bf16)

        @pl.when(at == 0)
        def _():
            put_y(plane, blocks, xs[d][:, rows:], 0, 1, gain)

        @pl.when(at == 3)
        def _():
            put_y(plane, blocks, xs[d][:, rows:], tall + 1, 1, gain)

    step = pack_rows(chans)
    dims = (((0,), (0,)), ((), ()))
    half = chans // 2
    offset = 0
    for first, count in chunks:
        share = chunk_rows(count, chans, planes) // planes

        def put(row, values, offset=offset, share=share):
            at = 0
            while at < values.shape[0]:
                q, r = divmod(row + at, share)
                n = min(share - r, values.shape[0] - at)
                out_ref[q, offset + r : offset + r + n] = values[at : at + n]
                at += n

        def store(row, grad, put=put):
            grad = grad.astype(bf16)
            put(row, grad[:, :128])
            put(row + chans, jnp.concatenate([grad[:half, 128:], grad[half:, 128:]], axis=1))

        for j in range(count):
            tap = jnp.minimum(p * taps_each + first + j, taps_all - 1)
            t, h, k = tap // 9, tap // 3 % 3, tap % 3

            @pl.when(odd)
            def _():
                piece = plane[pl.ds(t, 4), pl.ds(h, tall)].reshape(cells, chans)
                x = xk[k].reshape(cells, chans)
                store(j * step, lax.dot_general(piece, x, dims, preferred_element_type=f32))

            @pl.when(jnp.logical_not(odd))
            def _():
                piece = plane[pl.ds(2 - t, 4), pl.ds(2 - h, tall)].reshape(cells, chans)
                x = xk[2 - k].reshape(cells, chans)
                store(j * step, lax.dot_general(x, piece, dims, preferred_element_type=f32))

        spare = share * planes - count * step
        if spare:
            put(count * step, jnp.zeros((spare, 128), bf16))
        offset += share


def halves(total):
    high = total.astype(bf16)
    return jnp.concatenate([high, (total - high.astype(f32)).astype(bf16)])


def assemble_kernel(planes, size, *refs):
    pieces, out_ref = refs[:planes], refs[-1]
    q = lax.axis_index("height") // 4
    for d, piece in enumerate(pieces):
        start = pl.multiple_of((q - d + planes) % planes * size, 16)
        out_ref[pl.ds(start, size)] = piece[:size]
    if pieces[0].shape[0] > size:
        total = functools.reduce(lambda a, b: a + b, [piece[size:].astype(f32) for piece in pieces])
        half = total.shape[0] // 2
        out_ref[planes * size :] = halves(total[:half] + total[half:])


def unpack_kernel(taps, held, *refs):
    pieces = refs[:8]
    outs, stage, sems = refs[8 + 2 * held : 10 + 2 * held], refs[-2], refs[-1]
    more = refs[10 + 2 * held : -2]
    first, count = taps
    chans = stage.shape[1]
    half = chans // 2
    step = pack_rows(chans)
    odd = lax.axis_index("tm") % 2 == 1
    p = lax.axis_index("height") % 4
    made = []
    for n, src in enumerate(pieces):
        for j in range(count):
            tap = (p ^ (n % 4)) * taps_each + first + j
            slot = n * count + j
            high = src[j * step + chans : (j + 1) * step]
            stage[slot, :, :128] = src[j * step : j * step + chans]
            stage[slot, :half, 128:] = high[:, : chans - 128]
            stage[slot, half:, 128:] = high[:, chans - 128 :]
            real = tap < taps_all
            tap = jnp.minimum(tap, taps_all - 1)
            for which in range(2):
                good = odd if (which == 0) == (n < 4) else jnp.logical_not(odd)
                good = jnp.logical_and(good, real)
                copy = pltpu.make_async_copy(stage.at[slot], outs[which].at[tap], sems.at[slot])
                pl.when(good)(copy.start)
                made.append((good, copy))
    if more:
        sums = functools.reduce(lambda a, b: a + b, [src[src.shape[0] - 16 :].astype(f32) for src in pieces])
        sums = sums[:8] + sums[8:]
        for i in range(4):
            row = jnp.concatenate([sums[2 * i : 2 * i + 1], sums[2 * i + 1 : 2 * i + 2, : chans - 128]], axis=1)
            more[0][i : i + 1] = row.astype(bf16)
    for good, copy in made:
        pl.when(good)(copy.wait)


vmem = pl.BlockSpec(memory_space=pltpu.VMEM)
anywhere = pl.BlockSpec(memory_space=pl.ANY)
in_hbm = pl.BlockSpec(memory_space=pltpu.HBM)


def call(kernel, outs, args, us, mib, scratch=(), free=(), hbm=(), out_specs=None, **kw):
    return pl.pallas_call(
        kernel,
        out_shape=outs,
        in_specs=[in_hbm if i in hbm else anywhere if i in free else vmem for i in range(len(args))],
        out_specs=out_specs or [vmem] * len(outs),
        scratch_shapes=list(scratch),
        compiler_params=pltpu.CompilerParams(vmem_limit_bytes=mib * 2**20),
        cost_estimate=pl.CostEstimate(flops=int(us * 1.1e9), bytes_accessed=1024, transcendentals=0),
        **kw,
    )(*args)


def moved(value, axis, by):
    size = lax.axis_size(axis)
    return lax.ppermute(value, axis, [(i, i + by) for i in range(size) if 0 <= i + by < size])


def total_of(pieces):
    return functools.reduce(lambda a, b: a + b, [p.astype(f32) for p in pieces])


def piece_at(value, index):
    return lax.dynamic_index_in_dim(value, index, 0, keepdims=False)


def body(features, weight_one, bias_one, gain_one, weight_two, bias_two, gain_two, cotangent):
    frames, rows, cols, chans = features.shape
    tm, height = lax.axis_size("tm"), lax.axis_size("height")
    planes = height // 4
    c, me = lax.axis_index("tm"), lax.axis_index("height")
    odd = c % 2 == 1
    p, q = me % 4, me // 4
    swap = [(i, i ^ 1) for i in range(tm)]
    line = lambda v: v.reshape(1, chans)
    local = jax.ShapeDtypeStruct(features.shape, bf16)
    sums = jax.ShapeDtypeStruct((8, chans), f32)
    window = pltpu.VMEM((frames + 2, rows + 2, cols, chans), bf16)
    packed_shape = jax.ShapeDtypeStruct((rows, cols, 2 * chans), bf16)

    def plane_move(value, d):
        return lax.ppermute(value, "height", [(i, i ^ d) for i in range(height)])

    def column_move(value, d):
        pairs = [(z * 4 + j, (z + d) % planes * 4 + j) for z in range(planes) for j in range(4)]
        return lax.ppermute(value, "height", pairs)

    pair = tm == 2
    blocks = 2 if pair else 3
    messages = (jax.ShapeDtypeStruct((3 if pair else 4, cols, 2 * chans), bf16),) * 2
    y_shape = jax.ShapeDtypeStruct((blocks, rows, cols, 2 * chans), bf16)
    x_shape = jax.ShapeDtypeStruct((blocks, rows + 1, cols, 2 * chans), bf16)
    raw_give, raw_keep = jnp.where(odd, cotangent, features), jnp.where(odd, features, cotangent)
    if pair:
        far = (lax.ppermute(raw_give, "tm", swap),)
        extra = ()
    else:
        far = (moved(features, "tm", 1), moved(cotangent, "tm", -1))
        extra = (lax.ppermute(jnp.where(odd, far[1], far[0]), "tm", swap),)
    held = jax.ShapeDtypeStruct(weight_one.shape, bf16)
    w1, w2, vec = call(
        fetch_kernel,
        (held, held, jax.ShapeDtypeStruct((8, chans), f32)),
        (weight_one, weight_two, line(bias_one), line(gain_one), line(bias_two), line(gain_two)),
        3,
        8,
        [pltpu.SemaphoreType.DMA((6,))],
        hbm=range(6),
    )
    y_own, up, down = call(join_first_kernel, (y_shape, *messages), (raw_keep, raw_give, *far, *extra), 1, 8)
    above, below = moved(up, "height", 1), moved(down, "height", -1)
    ys = [y_own] + [plane_move(y_own, d) for d in (1, 2, 3)]

    give, keep, sums_one = call(
        first_kernel,
        (packed_shape, packed_shape, sums),
        (*ys[1:], raw_keep, raw_give, jnp.stack(far), above, below, w1, w2, vec),
        5,
        20,
        [window, window],
        free=(0, 1, 2),
    )
    other = lax.ppermute(give, "tm", swap)
    if pair:
        (x_own,) = call(join_edge_kernel, (x_shape,), (keep, other, above, below), 1, 6)
        far = lax.ppermute(keep, "tm", swap)[None]
    else:
        edge = jnp.where(p == 0, above, below)
        extra = lax.ppermute(jnp.where(odd, edge[3], edge[0]), "tm", swap)
        edge = jnp.where(odd, jnp.stack([extra, edge[0], edge[1]]), jnp.stack([edge[2], edge[3], extra]))
        x_own = jnp.where(odd, jnp.stack([other, keep, keep]), jnp.stack([keep, other, other]))
        x_own = jnp.concatenate([x_own, edge[:, None]], axis=1)
        act2, gmid = jnp.where(odd, give, keep), jnp.where(odd, keep, give)
        far = jnp.stack([moved(act2, "tm", 1), moved(gmid, "tm", -1)])
    xs = [x_own] + [plane_move(x_own, d) for d in (1, 2, 3)]
    up, down = call(gate_kernel, messages, (keep, give, far, xs[1]), 1, 6, free=(3,))
    above, below = moved(up, "height", 1), moved(down, "height", -1)

    (plane,) = call(
        functools.partial(plane_kernel, blocks),
        (jax.ShapeDtypeStruct((2 * frames + 2, 4 * rows + 2, cols, chans), bf16),),
        (*ys, vec, x_own),
        0.1,
        8,
        free=(5,),
    )
    shares = [chunk_rows(count, chans, planes) // planes for _, count in chunks]
    (flat,) = call(
        functools.partial(wgrad_kernel, blocks, planes),
        (jax.ShapeDtypeStruct((planes, sum(shares), 128), bf16),),
        (*xs, plane, vec),
        6,
        24,
        [
            pltpu.VMEM((2 * frames + 2, 4 * rows + 2, cols, chans), bf16),
            pltpu.VMEM((3, 2 * frames, 4 * rows, cols, chans), bf16),
        ],
    )
    arrived = [column_move(piece_at(flat, (q + d) % planes), d) for d in range(1, planes)]
    part = total_of([piece_at(flat, q), *arrived])
    hop = 2
    while hop < tm:
        part = part + lax.ppermute(part, "tm", [(i, i ^ hop) for i in range(tm)])
        hop *= 2
    part = part.astype(bf16)
    parts = jnp.split(part, [sum(shares[:n]) for n in range(1, len(shares))])

    block_out, grad_input, sums_two = call(
        last_kernel,
        (local, local, sums),
        (keep, give, far, above, below, raw_keep, raw_give, w1, w2, vec),
        6,
        20,
        [window, window],
    )

    small = jnp.concatenate([sums_one[:3], sums_two[:1]])
    small = jnp.pad(small, ((0, 0), (0, -chans % 128))).reshape(-1, 128)

    hop = 2
    while hop < tm:
        small = small + lax.ppermute(small, "tm", [(i, i ^ hop) for i in range(tm)])
        hop *= 2

    gradient = jax.ShapeDtypeStruct((taps_all, chans, chans), bf16)
    grads, gate = (), ()
    for n, (part, taps) in enumerate(zip(parts, chunks)):
        last = n == len(parts) - 1
        size = part.shape[0]
        send = jnp.concatenate([part, halves(small)]) if last else part
        got = [send] + [column_move(send, d) for d in range(1, planes)]
        (send,) = call(
            functools.partial(assemble_kernel, planes, size),
            (jax.ShapeDtypeStruct((planes * size + send.shape[0] - size, 128), bf16),),
            got,
            1,
            6,
        )
        one, two = plane_move(send, 1), plane_move(send, 2)
        cut = send.shape[0] // 32 * 16
        if False:
            three = jnp.concatenate([plane_move(two[:cut], 1), plane_move(one[cut:], 2)])
        else:
            three = plane_move(send, 3)
        got = [send, one, two, three]
        others = [lax.ppermute(g, "tm", swap) for g in got]
        held = len(grads) > 0
        grads = call(
            functools.partial(unpack_kernel, taps, held),
            (gradient, gradient) + (jax.ShapeDtypeStruct((4, chans), bf16),) * last,
            (*got, *others, *grads),
            2,
            12,
            [pltpu.VMEM((8 * taps[1], chans, chans), bf16), pltpu.SemaphoreType.DMA((8 * taps[1],))],
            free=(8, 9) if held else (),
            out_specs=[anywhere, anywhere] + [vmem] * last,
            input_output_aliases={8: 0, 9: 1} if held else {},
        )
    grad_one, grad_two, small = grads
    shape = weight_one.shape
    return (
        block_out,
        grad_input,
        grad_one.reshape(shape),
        grad_two.reshape(shape),
        small[1],
        small[2],
        small[3],
        small[0],
    )


def solution(mesh):
    split = P("tm", "height", None, None)
    return jax.shard_map(
        body,
        mesh=mesh,
        in_specs=(split, P(), P(), P(), P(), P(), P(), split),
        out_specs=(split, split, P(), P(), P(), P(), P(), P()),
        check_vma=False,
    )
```

```python
import functools

import jax
import jax.numpy as jnp
from jax import lax
from jax.experimental import pallas as pl
from jax.experimental.pallas import tpu as pltpu
from jax.sharding import PartitionSpec as P

epsilon = 1e-06
bf16 = jnp.bfloat16
f32 = jnp.float32
chunks = ((0, 3), (3, 4))
taps_each = 7
taps_all = 27


def shift_cols(value, by):
    zero = jnp.zeros_like(value[:, :1])
    if by == 1:
        return jnp.concatenate([value[:, 1:], zero], axis=1)
    return jnp.concatenate([zero, value[:, :-1]], axis=1)


def norm_parts(vals, gain):
    scale = lax.rsqrt(jnp.mean(vals * vals, axis=-1, keepdims=True) + epsilon)
    normed = vals * scale
    lifted = normed * gain
    return scale, normed, lifted, jax.nn.sigmoid(lifted)


def norm_silu(vals, gain):
    _, _, lifted, sig = norm_parts(vals, gain)
    return lifted * sig


def norm_silu_back(grad, vals, gain):
    scale, normed, lifted, sig = norm_parts(vals, gain)
    d_lift = grad * sig * (1.0 + lifted * (1.0 - sig))
    d_gain = jnp.sum(d_lift * normed, axis=0, keepdims=True)
    d_norm = d_lift * gain
    d_vals = scale * (d_norm - normed * jnp.mean(d_norm * normed, axis=-1, keepdims=True))
    return d_vals, d_gain


def conv(window, weight, frames, rows, back):
    cols, chans = window.shape[2], window.shape[3]
    parts = [None] * 3
    for t in range(3):
        for h in range(3):
            t0, h0 = (2 - t, 2 - h) if back else (t, h)
            piece = window[t0 : t0 + frames, h0 : h0 + rows].reshape(frames * rows * cols, chans)
            for k in range(3):
                dims = (((1,), (1 if back else 0,)), ((), ()))
                prod = lax.dot_general(piece, weight[t, h, k], dims, preferred_element_type=f32)
                parts[k] = prod if parts[k] is None else parts[k] + prod
    parts = [part.reshape(frames * rows, cols, chans) for part in parts]
    sign = -1 if back else 1
    total = parts[1] + shift_cols(parts[0], -sign) + shift_cols(parts[2], sign)
    return total.reshape(frames * rows * cols, chans)


def is_odd():
    return lax.axis_index("tm") % 2 == 1


def by_core(odd_fn, even_fn):
    pl.when(is_odd())(odd_fn)
    pl.when(jnp.logical_not(is_odd()))(even_fn)


def fill_packed(window, at, rows, packed):
    chans = window.shape[3]
    for f in range(2):
        window[at + f, rows] = packed[..., f * chans : (f + 1) * chans]


def fill_far(ahead, behind, far, rows):
    def put(window, at, value):
        if value.shape[-1] == window.shape[3]:
            window[pl.ds(at, 2), rows] = value
        else:
            fill_packed(window, at, rows, value)

    if far.shape[0] == 2:
        put(ahead, 0, far[0])
        put(behind, 2, far[1])
        return
    zero = jnp.zeros(far.shape[1:], bf16)

    def odd():
        put(ahead, 0, far[0])
        put(behind, 2, zero)

    def even():
        put(ahead, 0, zero)
        put(behind, 2, far[0])

    by_core(odd, even)


def fill_edges(ahead, behind, above, below):
    last = ahead.shape[1] - 1
    places = ((ahead, 0), (ahead, 2), (behind, 0), (behind, 2))
    for row, edges in ((0, above), (last, below)):
        rows = pl.ds(row, 1)
        if edges.shape[0] == 4:
            for i, (window, at) in enumerate(places):
                fill_packed(window, at, rows, edges[i : i + 1])
            continue
        zero = jnp.zeros((1,) + edges.shape[1:], bf16)

        def odd():
            for i, (window, at) in enumerate(places):
                fill_packed(window, at, rows, edges[i : i + 1] if i < 3 else zero)

        def even():
            for i, (window, at) in enumerate(places):
                fill_packed(window, at, rows, edges[i - 1 : i] if i > 0 else zero)

        by_core(odd, even)


def started(copies, sems):
    made = [pltpu.make_async_copy(src, dst, sems.at[i]) for i, (src, dst) in enumerate(copies)]
    for copy in made:
        copy.start()
    return made


def pack_frames(values):
    return jnp.concatenate([values[0], values[1]], axis=-1)


def put_messages(groups, up_ref, down_ref):
    for i, value in enumerate(groups):
        up_ref[i] = value[value.shape[0] - 1]
        down_ref[i] = value[0]


def join_first_kernel(*refs):
    refs, (y_ref, up_ref, down_ref) = refs[:-3], refs[-3:]
    keep, give, *far = [pack_frames(ref) for ref in refs]
    if len(far) == 1:

        def odd():
            y_ref[0], y_ref[1] = far[0], keep
            put_messages((far[0], keep, give), up_ref, down_ref)

        def even():
            y_ref[0], y_ref[1] = keep, far[0]
            put_messages((give, keep, far[0]), up_ref, down_ref)

    else:

        def odd():
            y_ref[0], y_ref[1], y_ref[2] = far[2], far[0], keep
            put_messages((far[0], keep, give, far[1]), up_ref, down_ref)

        def even():
            y_ref[0], y_ref[1], y_ref[2] = keep, far[1], far[2]
            put_messages((far[0], give, keep, far[1]), up_ref, down_ref)

    by_core(odd, even)


def gate_kernel(keep_ref, give_ref, far_ref, _, up_ref, down_ref):
    keep, give, far = keep_ref[...], give_ref[...], far_ref[...]

    def odd():
        put_messages((far[0], give, keep, far[-1])[: up_ref.shape[0]], up_ref, down_ref)

    def even():
        put_messages((far[0], keep, give, far[-1])[4 - up_ref.shape[0] :], up_ref, down_ref)

    by_core(odd, even)


def join_edge_kernel(keep_ref, other_ref, above_ref, below_ref, out_ref):
    rows = keep_ref.shape[0]
    top = lax.axis_index("height") % 4 == 0
    edge = jnp.where(top, above_ref[...], below_ref[...])

    def odd():
        out_ref[0, :rows], out_ref[1, :rows] = other_ref[...], keep_ref[...]
        out_ref[0, rows], out_ref[1, rows] = edge[0], edge[1]

    def even():
        out_ref[0, :rows], out_ref[1, :rows] = keep_ref[...], other_ref[...]
        out_ref[0, rows], out_ref[1, rows] = edge[1], edge[2]

    by_core(odd, even)


def fetch_kernel(w1_any, w2_any, b1_any, g1_any, b2_any, g2_any, w1_ref, w2_ref, vec_ref, sems):
    vectors = [(ref, vec_ref.at[pl.ds(i, 1)]) for i, ref in enumerate((b1_any, g1_any, b2_any, g2_any))]
    for copy in started([(w1_any, w1_ref), (w2_any, w2_ref), *vectors], sems):
        copy.wait()


def first_kernel(
    _, keep_in, give_in, far_ref, above_ref, below_ref, w1, w2, vec_ref,
    give_ref, keep_ref, sums_ref, ahead, behind,
):
    frames, rows, cols, chans = keep_in.shape
    own = pl.ds(1, rows)
    b1, g1, g2 = vec_ref[0:1], vec_ref[1:2], vec_ref[3:4]

    def odd_in():
        ahead[pl.ds(2, 2), own] = keep_in[...]
        behind[pl.ds(0, 2), own] = give_in[...]

    def even_in():
        ahead[pl.ds(2, 2), own] = give_in[...]
        behind[pl.ds(0, 2), own] = keep_in[...]

    by_core(odd_in, even_in)
    fill_far(ahead, behind, far_ref, own)
    fill_edges(ahead, behind, above_ref, below_ref)
    for f in range(frames + 2):
        vals = ahead[f].astype(f32).reshape(-1, chans)
        ahead[f] = norm_silu(vals, g1).astype(bf16).reshape(rows + 2, cols, chans)
    mid = (conv(ahead, w1, frames, rows, False) + b1).astype(bf16).astype(f32)
    act2 = norm_silu(mid, g2).astype(bf16).reshape(frames, rows, cols, chans)
    act2 = pack_frames(act2)
    grad = conv(behind, w2, frames, rows, True)
    gmid, d_gain = norm_silu_back(grad, mid, g2)
    gmid = gmid.astype(bf16)
    cot = behind[:2, 1 : rows + 1].astype(f32).reshape(-1, chans)
    sums_ref[...] = jnp.concatenate(
        [
            d_gain,
            jnp.sum(gmid.astype(f32), axis=0, keepdims=True),
            jnp.sum(cot, axis=0, keepdims=True),
            jnp.zeros((5, chans), f32),
        ],
        axis=0,
    )
    gmid = pack_frames(gmid.reshape(frames, rows, cols, chans))

    def odd():
        give_ref[...] = act2
        keep_ref[...] = gmid

    def even():
        give_ref[...] = gmid
        keep_ref[...] = act2

    by_core(odd, even)


def last_kernel(
    keep_ref, give_ref, far_ref, above_ref, below_ref, keep_in, give_in, w1, w2, vec_ref,
    out_ref, gin_ref, sums_ref, ahead, behind,
):
    frames, rows, cols, chans = out_ref.shape
    own = pl.ds(1, rows)
    g1, b2 = vec_ref[1:2], vec_ref[2:3]

    def odd():
        fill_packed(ahead, 2, own, give_ref[...])
        fill_packed(behind, 0, own, keep_ref[...])

    def even():
        fill_packed(ahead, 2, own, keep_ref[...])
        fill_packed(behind, 0, own, give_ref[...])

    by_core(odd, even)
    fill_far(ahead, behind, far_ref, own)
    fill_edges(ahead, behind, above_ref, below_ref)
    feat = jnp.where(is_odd(), keep_in[...], give_in[...]).astype(f32).reshape(-1, chans)
    out = feat + conv(ahead, w2, frames, rows, False) + b2
    out_ref[...] = out.astype(bf16).reshape(out_ref.shape)
    grad = conv(behind, w1, frames, rows, True)
    d_vals, d_gain = norm_silu_back(grad, feat, g1)
    gin = d_vals + jnp.where(is_odd(), give_in[...], keep_in[...]).astype(f32).reshape(-1, chans)
    gin_ref[...] = gin.astype(bf16).reshape(gin_ref.shape)
    sums_ref[...] = jnp.concatenate([d_gain, jnp.zeros((7, chans), f32)], axis=0)


def pack_rows(chans):
    return chans + chans // 2


def chunk_rows(count, chans, planes):
    unit = 16 * planes
    return -(-count * pack_rows(chans) // unit) * unit


def put_y(plane, blocks, values, row, count, gain):
    chans = plane.shape[3]
    base = jnp.where(is_odd(), 2, 0) if blocks == 2 else 0
    for b in range(blocks):
        for f in range(2):
            part = values[b, :, :, f * chans : (f + 1) * chans]
            place = (base + 2 * b + f, pl.ds(row, count))

            def odd():
                flat = part.astype(f32).reshape(-1, chans)
                plane[place] = norm_silu(flat, gain).astype(bf16).reshape(part.shape)

            def even():
                plane[place] = part

            by_core(odd, even)


def plane_kernel(blocks, *refs):
    ys, gain, plane = refs[:4], refs[4][1:2], refs[-1]
    rows = ys[0].shape[1]
    p = lax.axis_index("height") % 4
    if blocks == 2:
        plane[pl.ds(jnp.where(is_odd(), 0, 4), 2)] = jnp.zeros((2,) + plane.shape[1:], bf16)
    for d in range(4):
        put_y(plane, blocks, ys[d][...], 1 + rows * (p ^ d), rows, gain)


def wgrad_kernel(blocks, planes, *refs):
    xs, plane_in, gain = refs[:4], refs[4], refs[5][1:2]
    out_ref, plane, xk = refs[-3:]
    _, rows, cols, _ = xs[0].shape
    rows -= 1
    chans = plane.shape[3]
    tall = 4 * rows
    cells = 4 * tall * cols
    odd = is_odd()
    p = lax.axis_index("height") % 4
    plane[:, 1 : tall + 1] = plane_in[:, 1 : tall + 1]
    if blocks == 2:
        empty = jnp.zeros((2, 1, cols, chans), bf16)
        for row in (0, tall + 1):
            plane[pl.ds(jnp.where(odd, 0, 4), 2), row : row + 1] = empty
    for d in range(4):
        at = p ^ d
        for b in range(2):
            for f in range(2):
                part = xs[d][b, :rows, :, f * chans : (f + 1) * chans]
                wide = part.astype(f32)
                place = (2 * b + f, pl.ds(rows * at, rows))
                xk[(0,) + place] = shift_cols(wide, 1).astype(bf16)
                xk[(1,) + place] = part
                xk[(2,) + place] = shift_cols(wide, -1).astype(bf16)

        @pl.when(at == 0)
        def _():
            put_y(plane, blocks, xs[d][:, rows:], 0, 1, gain)

        @pl.when(at == 3)
        def _():
            put_y(plane, blocks, xs[d][:, rows:], tall + 1, 1, gain)

    step = pack_rows(chans)
    dims = (((0,), (0,)), ((), ()))
    half = chans // 2
    offset = 0
    for first, count in chunks:
        share = chunk_rows(count, chans, planes) // planes

        def put(row, values, offset=offset, share=share):
            at = 0
            while at < values.shape[0]:
                q, r = divmod(row + at, share)
                n = min(share - r, values.shape[0] - at)
                out_ref[q, offset + r : offset + r + n] = values[at : at + n]
                at += n

        def store(row, grad, put=put):
            grad = grad.astype(bf16)
            put(row, grad[:, :128])
            put(row + chans, jnp.concatenate([grad[:half, 128:], grad[half:, 128:]], axis=1))

        for j in range(count):
            tap = jnp.minimum(p * taps_each + first + j, taps_all - 1)
            t, h, k = tap // 9, tap // 3 % 3, tap % 3

            @pl.when(odd)
            def _():
                piece = plane[pl.ds(t, 4), pl.ds(h, tall)].reshape(cells, chans)
                x = xk[k].reshape(cells, chans)
                store(j * step, lax.dot_general(piece, x, dims, preferred_element_type=f32))

            @pl.when(jnp.logical_not(odd))
            def _():
                piece = plane[pl.ds(2 - t, 4), pl.ds(2 - h, tall)].reshape(cells, chans)
                x = xk[2 - k].reshape(cells, chans)
                store(j * step, lax.dot_general(x, piece, dims, preferred_element_type=f32))

        spare = share * planes - count * step
        if spare:
            put(count * step, jnp.zeros((spare, 128), bf16))
        offset += share


def halves(total):
    high = total.astype(bf16)
    return jnp.concatenate([high, (total - high.astype(f32)).astype(bf16)])


def assemble_kernel(planes, size, *refs):
    pieces, out_ref = refs[:planes], refs[-1]
    q = lax.axis_index("height") // 4
    for d, piece in enumerate(pieces):
        start = pl.multiple_of((q - d + planes) % planes * size, 16)
        out_ref[pl.ds(start, size)] = piece[:size]
    if pieces[0].shape[0] > size:
        total = functools.reduce(lambda a, b: a + b, [piece[size:].astype(f32) for piece in pieces])
        half = total.shape[0] // 2
        out_ref[planes * size :] = halves(total[:half] + total[half:])


def unpack_kernel(taps, held, *refs):
    pieces = refs[:8]
    outs, stage, sems = refs[8 + 2 * held : 10 + 2 * held], refs[-2], refs[-1]
    more = refs[10 + 2 * held : -2]
    first, count = taps
    chans = stage.shape[1]
    half = chans // 2
    step = pack_rows(chans)
    odd = lax.axis_index("tm") % 2 == 1
    p = lax.axis_index("height") % 4
    made = []
    for n, src in enumerate(pieces):
        for j in range(count):
            tap = (p ^ (n % 4)) * taps_each + first + j
            slot = n * count + j
            high = src[j * step + chans : (j + 1) * step]
            stage[slot, :, :128] = src[j * step : j * step + chans]
            stage[slot, :half, 128:] = high[:, : chans - 128]
            stage[slot, half:, 128:] = high[:, chans - 128 :]
            real = tap < taps_all
            tap = jnp.minimum(tap, taps_all - 1)
            for which in range(2):
                good = odd if (which == 0) == (n < 4) else jnp.logical_not(odd)
                good = jnp.logical_and(good, real)
                copy = pltpu.make_async_copy(stage.at[slot], outs[which].at[tap], sems.at[slot])
                pl.when(good)(copy.start)
                made.append((good, copy))
    if more:
        sums = functools.reduce(lambda a, b: a + b, [src[src.shape[0] - 16 :].astype(f32) for src in pieces])
        sums = sums[:8] + sums[8:]
        for i in range(4):
            row = jnp.concatenate([sums[2 * i : 2 * i + 1], sums[2 * i + 1 : 2 * i + 2, : chans - 128]], axis=1)
            more[0][i : i + 1] = row.astype(bf16)
    for good, copy in made:
        pl.when(good)(copy.wait)


vmem = pl.BlockSpec(memory_space=pltpu.VMEM)
anywhere = pl.BlockSpec(memory_space=pl.ANY)
in_hbm = pl.BlockSpec(memory_space=pltpu.HBM)


def call(kernel, outs, args, us, mib, scratch=(), free=(), hbm=(), out_specs=None, **kw):
    return pl.pallas_call(
        kernel,
        out_shape=outs,
        in_specs=[in_hbm if i in hbm else anywhere if i in free else vmem for i in range(len(args))],
        out_specs=out_specs or [vmem] * len(outs),
        scratch_shapes=list(scratch),
        compiler_params=pltpu.CompilerParams(vmem_limit_bytes=mib * 2**20),
        cost_estimate=pl.CostEstimate(flops=int(us * 1.1e9), bytes_accessed=1024, transcendentals=0),
        **kw,
    )(*args)


def moved(value, axis, by):
    size = lax.axis_size(axis)
    return lax.ppermute(value, axis, [(i, i + by) for i in range(size) if 0 <= i + by < size])


def total_of(pieces):
    return functools.reduce(lambda a, b: a + b, [p.astype(f32) for p in pieces])


def piece_at(value, index):
    return lax.dynamic_index_in_dim(value, index, 0, keepdims=False)


def body(features, weight_one, bias_one, gain_one, weight_two, bias_two, gain_two, cotangent):
    frames, rows, cols, chans = features.shape
    tm, height = lax.axis_size("tm"), lax.axis_size("height")
    planes = height // 4
    c, me = lax.axis_index("tm"), lax.axis_index("height")
    odd = c % 2 == 1
    p, q = me % 4, me // 4
    swap = [(i, i ^ 1) for i in range(tm)]
    line = lambda v: v.reshape(1, chans)
    local = jax.ShapeDtypeStruct(features.shape, bf16)
    sums = jax.ShapeDtypeStruct((8, chans), f32)
    window = pltpu.VMEM((frames + 2, rows + 2, cols, chans), bf16)
    packed_shape = jax.ShapeDtypeStruct((rows, cols, 2 * chans), bf16)

    def plane_move(value, d):
        return lax.ppermute(value, "height", [(i, i ^ d) for i in range(height)])

    def column_move(value, d):
        pairs = [(z * 4 + j, (z + d) % planes * 4 + j) for z in range(planes) for j in range(4)]
        return lax.ppermute(value, "height", pairs)

    pair = tm == 2
    blocks = 2 if pair else 3
    messages = (jax.ShapeDtypeStruct((3 if pair else 4, cols, 2 * chans), bf16),) * 2
    y_shape = jax.ShapeDtypeStruct((blocks, rows, cols, 2 * chans), bf16)
    x_shape = jax.ShapeDtypeStruct((blocks, rows + 1, cols, 2 * chans), bf16)
    raw_give, raw_keep = jnp.where(odd, cotangent, features), jnp.where(odd, features, cotangent)
    if pair:
        far = (lax.ppermute(raw_give, "tm", swap),)
        extra = ()
    else:
        far = (moved(features, "tm", 1), moved(cotangent, "tm", -1))
        extra = (lax.ppermute(jnp.where(odd, far[1], far[0]), "tm", swap),)
    held = jax.ShapeDtypeStruct(weight_one.shape, bf16)
    w1, w2, vec = call(
        fetch_kernel,
        (held, held, jax.ShapeDtypeStruct((8, chans), f32)),
        (weight_one, weight_two, line(bias_one), line(gain_one), line(bias_two), line(gain_two)),
        3,
        8,
        [pltpu.SemaphoreType.DMA((6,))],
        hbm=range(6),
    )
    y_own, up, down = call(join_first_kernel, (y_shape, *messages), (raw_keep, raw_give, *far, *extra), 1, 8)
    above, below = moved(up, "height", 1), moved(down, "height", -1)
    ys = [y_own] + [plane_move(y_own, d) for d in (1, 2, 3)]

    give, keep, sums_one = call(
        first_kernel,
        (packed_shape, packed_shape, sums),
        (ys[3], raw_keep, raw_give, jnp.stack(far), above, below, w1, w2, vec),
        5,
        20,
        [window, window],
        free=(0,),
    )
    other = lax.ppermute(give, "tm", swap)
    if pair:
        (x_own,) = call(join_edge_kernel, (x_shape,), (keep, other, above, below), 1, 6)
        far = lax.ppermute(keep, "tm", swap)[None]
    else:
        edge = jnp.where(p == 0, above, below)
        extra = lax.ppermute(jnp.where(odd, edge[3], edge[0]), "tm", swap)
        edge = jnp.where(odd, jnp.stack([extra, edge[0], edge[1]]), jnp.stack([edge[2], edge[3], extra]))
        x_own = jnp.where(odd, jnp.stack([other, keep, keep]), jnp.stack([keep, other, other]))
        x_own = jnp.concatenate([x_own, edge[:, None]], axis=1)
        act2, gmid = jnp.where(odd, give, keep), jnp.where(odd, keep, give)
        far = jnp.stack([moved(act2, "tm", 1), moved(gmid, "tm", -1)])
    xs = [x_own] + [plane_move(x_own, d) for d in (1, 2, 3)]
    up, down = call(gate_kernel, messages, (keep, give, far, xs[1]), 1, 6, free=(3,))
    above, below = moved(up, "height", 1), moved(down, "height", -1)

    (plane,) = call(
        functools.partial(plane_kernel, blocks),
        (jax.ShapeDtypeStruct((2 * frames + 2, 4 * rows + 2, cols, chans), bf16),),
        (*ys, vec, x_own),
        0.1,
        8,
        free=(5,),
    )
    shares = [chunk_rows(count, chans, planes) // planes for _, count in chunks]
    (flat,) = call(
        functools.partial(wgrad_kernel, blocks, planes),
        (jax.ShapeDtypeStruct((planes, sum(shares), 128), bf16),),
        (*xs, plane, vec),
        6,
        24,
        [
            pltpu.VMEM((2 * frames + 2, 4 * rows + 2, cols, chans), bf16),
            pltpu.VMEM((3, 2 * frames, 4 * rows, cols, chans), bf16),
        ],
    )
    arrived = [column_move(piece_at(flat, (q + d) % planes), d) for d in range(1, planes)]
    part = total_of([piece_at(flat, q), *arrived])
    hop = 2
    while hop < tm:
        part = part + lax.ppermute(part, "tm", [(i, i ^ hop) for i in range(tm)])
        hop *= 2
    part = part.astype(bf16)
    parts = jnp.split(part, [sum(shares[:n]) for n in range(1, len(shares))])

    block_out, grad_input, sums_two = call(
        last_kernel,
        (local, local, sums),
        (keep, give, far, above, below, raw_keep, raw_give, w1, w2, vec),
        6,
        20,
        [window, window],
    )

    small = jnp.concatenate([sums_one[:3], sums_two[:1]])
    small = jnp.pad(small, ((0, 0), (0, -chans % 128))).reshape(-1, 128)

    hop = 2
    while hop < tm:
        small = small + lax.ppermute(small, "tm", [(i, i ^ hop) for i in range(tm)])
        hop *= 2

    gradient = jax.ShapeDtypeStruct((taps_all, chans, chans), bf16)
    grads, gate = (), ()
    for n, (part, taps) in enumerate(zip(parts, chunks)):
        last = n == len(parts) - 1
        size = part.shape[0]
        send = jnp.concatenate([part, halves(small)]) if last else part
        got = [send] + [column_move(send, d) for d in range(1, planes)]
        (send,) = call(
            functools.partial(assemble_kernel, planes, size),
            (jax.ShapeDtypeStruct((planes * size + send.shape[0] - size, 128), bf16),),
            got,
            1,
            6,
        )
        one, two = plane_move(send, 1), plane_move(send, 2)
        cut = send.shape[0] // 32 * 16
        if False:
            three = jnp.concatenate([plane_move(two[:cut], 1), plane_move(one[cut:], 2)])
        else:
            three = plane_move(send, 3)
        got = [send, one, two, three]
        others = [lax.ppermute(g, "tm", swap) for g in got]
        held = len(grads) > 0
        grads = call(
            functools.partial(unpack_kernel, taps, held),
            (gradient, gradient) + (jax.ShapeDtypeStruct((4, chans), bf16),) * last,
            (*got, *others, *grads),
            2,
            12,
            [pltpu.VMEM((8 * taps[1], chans, chans), bf16), pltpu.SemaphoreType.DMA((8 * taps[1],))],
            free=(8, 9) if held else (),
            out_specs=[anywhere, anywhere] + [vmem] * last,
            input_output_aliases={8: 0, 9: 1} if held else {},
        )
    grad_one, grad_two, small = grads
    shape = weight_one.shape
    return (
        block_out,
        grad_input,
        grad_one.reshape(shape),
        grad_two.reshape(shape),
        small[1],
        small[2],
        small[3],
        small[0],
    )


def solution(mesh):
    split = P("tm", "height", None, None)
    return jax.shard_map(
        body,
        mesh=mesh,
        in_specs=(split, P(), P(), P(), P(), P(), P(), split),
        out_specs=(split, split, P(), P(), P(), P(), P(), P()),
        check_vma=False,
    )
```

```python
import functools

import jax
import jax.numpy as jnp
from jax import lax
from jax.experimental import pallas as pl
from jax.experimental.pallas import tpu as pltpu
from jax.sharding import PartitionSpec as P

epsilon = 1e-06
bf16 = jnp.bfloat16
f32 = jnp.float32
chunks = ((0, 3), (3, 4))
taps_each = 7
taps_all = 27


def shift_cols(value, by):
    zero = jnp.zeros_like(value[:, :1])
    if by == 1:
        return jnp.concatenate([value[:, 1:], zero], axis=1)
    return jnp.concatenate([zero, value[:, :-1]], axis=1)


def norm_parts(vals, gain):
    scale = lax.rsqrt(jnp.mean(vals * vals, axis=-1, keepdims=True) + epsilon)
    normed = vals * scale
    lifted = normed * gain
    return scale, normed, lifted, jax.nn.sigmoid(lifted)


def norm_silu(vals, gain):
    _, _, lifted, sig = norm_parts(vals, gain)
    return lifted * sig


def norm_silu_back(grad, vals, gain):
    scale, normed, lifted, sig = norm_parts(vals, gain)
    d_lift = grad * sig * (1.0 + lifted * (1.0 - sig))
    d_gain = jnp.sum(d_lift * normed, axis=0, keepdims=True)
    d_norm = d_lift * gain
    d_vals = scale * (d_norm - normed * jnp.mean(d_norm * normed, axis=-1, keepdims=True))
    return d_vals, d_gain


def conv(window, weight, frames, rows, back):
    cols, chans = window.shape[2], window.shape[3]
    parts = [None] * 3
    for t in range(3):
        for h in range(3):
            t0, h0 = (2 - t, 2 - h) if back else (t, h)
            piece = window[t0 : t0 + frames, h0 : h0 + rows].reshape(frames * rows * cols, chans)
            for k in range(3):
                dims = (((1,), (1 if back else 0,)), ((), ()))
                prod = lax.dot_general(piece, weight[t, h, k], dims, preferred_element_type=f32)
                parts[k] = prod if parts[k] is None else parts[k] + prod
    parts = [part.reshape(frames * rows, cols, chans) for part in parts]
    sign = -1 if back else 1
    total = parts[1] + shift_cols(parts[0], -sign) + shift_cols(parts[2], sign)
    return total.reshape(frames * rows * cols, chans)


def is_odd():
    return lax.axis_index("tm") % 2 == 1


def by_core(odd_fn, even_fn):
    pl.when(is_odd())(odd_fn)
    pl.when(jnp.logical_not(is_odd()))(even_fn)


def fill_packed(window, at, rows, packed):
    chans = window.shape[3]
    for f in range(2):
        window[at + f, rows] = packed[..., f * chans : (f + 1) * chans]


def fill_far(ahead, behind, far, rows):
    def put(window, at, value):
        if value.shape[-1] == window.shape[3]:
            window[pl.ds(at, 2), rows] = value
        else:
            fill_packed(window, at, rows, value)

    if far.shape[0] == 2:
        put(ahead, 0, far[0])
        put(behind, 2, far[1])
        return
    zero = jnp.zeros(far.shape[1:], bf16)

    def odd():
        put(ahead, 0, far[0])
        put(behind, 2, zero)

    def even():
        put(ahead, 0, zero)
        put(behind, 2, far[0])

    by_core(odd, even)


def fill_edges(ahead, behind, above, below):
    last = ahead.shape[1] - 1
    places = ((ahead, 0), (ahead, 2), (behind, 0), (behind, 2))
    for row, edges in ((0, above), (last, below)):
        rows = pl.ds(row, 1)
        if edges.shape[0] == 4:
            for i, (window, at) in enumerate(places):
                fill_packed(window, at, rows, edges[i : i + 1])
            continue
        zero = jnp.zeros((1,) + edges.shape[1:], bf16)

        def odd():
            for i, (window, at) in enumerate(places):
                fill_packed(window, at, rows, edges[i : i + 1] if i < 3 else zero)

        def even():
            for i, (window, at) in enumerate(places):
                fill_packed(window, at, rows, edges[i - 1 : i] if i > 0 else zero)

        by_core(odd, even)


def started(copies, sems):
    made = [pltpu.make_async_copy(src, dst, sems.at[i]) for i, (src, dst) in enumerate(copies)]
    for copy in made:
        copy.start()
    return made


def pack_frames(values):
    return jnp.concatenate([values[0], values[1]], axis=-1)


def put_messages(groups, up_ref, down_ref):
    for i, value in enumerate(groups):
        up_ref[i] = value[value.shape[0] - 1]
        down_ref[i] = value[0]


def join_first_kernel(*refs):
    refs, (y_ref, up_ref, down_ref) = refs[:-3], refs[-3:]
    keep, give, *far = [pack_frames(ref) for ref in refs]
    if len(far) == 1:

        def odd():
            y_ref[0], y_ref[1] = far[0], keep
            put_messages((far[0], keep, give), up_ref, down_ref)

        def even():
            y_ref[0], y_ref[1] = keep, far[0]
            put_messages((give, keep, far[0]), up_ref, down_ref)

    else:

        def odd():
            y_ref[0], y_ref[1], y_ref[2] = far[2], far[0], keep
            put_messages((far[0], keep, give, far[1]), up_ref, down_ref)

        def even():
            y_ref[0], y_ref[1], y_ref[2] = keep, far[1], far[2]
            put_messages((far[0], give, keep, far[1]), up_ref, down_ref)

    by_core(odd, even)


def gate_kernel(keep_ref, give_ref, far_ref, _, up_ref, down_ref):
    keep, give, far = keep_ref[...], give_ref[...], far_ref[...]

    def odd():
        put_messages((far[0], give, keep, far[-1])[: up_ref.shape[0]], up_ref, down_ref)

    def even():
        put_messages((far[0], keep, give, far[-1])[4 - up_ref.shape[0] :], up_ref, down_ref)

    by_core(odd, even)


def join_edge_kernel(keep_ref, other_ref, above_ref, below_ref, out_ref):
    rows = keep_ref.shape[0]
    top = lax.axis_index("height") % 4 == 0
    edge = jnp.where(top, above_ref[...], below_ref[...])

    def odd():
        out_ref[0, :rows], out_ref[1, :rows] = other_ref[...], keep_ref[...]
        out_ref[0, rows], out_ref[1, rows] = edge[0], edge[1]

    def even():
        out_ref[0, :rows], out_ref[1, :rows] = keep_ref[...], other_ref[...]
        out_ref[0, rows], out_ref[1, rows] = edge[1], edge[2]

    by_core(odd, even)


def fetch_kernel(w1_any, w2_any, b1_any, g1_any, b2_any, g2_any, w1_ref, w2_ref, vec_ref, sems):
    vectors = [(ref, vec_ref.at[pl.ds(i, 1)]) for i, ref in enumerate((b1_any, g1_any, b2_any, g2_any))]
    for copy in started([(w1_any, w1_ref), (w2_any, w2_ref), *vectors], sems):
        copy.wait()


def first_kernel(
    _, __, ___, keep_in, give_in, far_ref, above_ref, below_ref, w1, w2, vec_ref,
    give_ref, keep_ref, sums_ref, ahead, behind,
):
    frames, rows, cols, chans = keep_in.shape
    own = pl.ds(1, rows)
    b1, g1, g2 = vec_ref[0:1], vec_ref[1:2], vec_ref[3:4]

    def odd_in():
        ahead[pl.ds(2, 2), own] = keep_in[...]
        behind[pl.ds(0, 2), own] = give_in[...]

    def even_in():
        ahead[pl.ds(2, 2), own] = give_in[...]
        behind[pl.ds(0, 2), own] = keep_in[...]

    by_core(odd_in, even_in)
    fill_far(ahead, behind, far_ref, own)
    fill_edges(ahead, behind, above_ref, below_ref)
    for f in range(frames + 2):
        vals = ahead[f].astype(f32).reshape(-1, chans)
        ahead[f] = norm_silu(vals, g1).astype(bf16).reshape(rows + 2, cols, chans)
    mid = (conv(ahead, w1, frames, rows, False) + b1).astype(bf16).astype(f32)
    act2 = norm_silu(mid, g2).astype(bf16).reshape(frames, rows, cols, chans)
    act2 = pack_frames(act2)
    grad = conv(behind, w2, frames, rows, True)
    gmid, d_gain = norm_silu_back(grad, mid, g2)
    gmid = gmid.astype(bf16)
    cot = behind[:2, 1 : rows + 1].astype(f32).reshape(-1, chans)
    sums_ref[...] = jnp.concatenate(
        [
            d_gain,
            jnp.sum(gmid.astype(f32), axis=0, keepdims=True),
            jnp.sum(cot, axis=0, keepdims=True),
            jnp.zeros((5, chans), f32),
        ],
        axis=0,
    )
    gmid = pack_frames(gmid.reshape(frames, rows, cols, chans))

    def odd():
        give_ref[...] = act2
        keep_ref[...] = gmid

    def even():
        give_ref[...] = gmid
        keep_ref[...] = act2

    by_core(odd, even)


def last_kernel(
    keep_ref, give_ref, far_ref, above_ref, below_ref, keep_in, give_in, w1, w2, vec_ref,
    out_ref, gin_ref, sums_ref, ahead, behind,
):
    frames, rows, cols, chans = out_ref.shape
    own = pl.ds(1, rows)
    g1, b2 = vec_ref[1:2], vec_ref[2:3]

    def odd():
        fill_packed(ahead, 2, own, give_ref[...])
        fill_packed(behind, 0, own, keep_ref[...])

    def even():
        fill_packed(ahead, 2, own, keep_ref[...])
        fill_packed(behind, 0, own, give_ref[...])

    by_core(odd, even)
    fill_far(ahead, behind, far_ref, own)
    fill_edges(ahead, behind, above_ref, below_ref)
    feat = jnp.where(is_odd(), keep_in[...], give_in[...]).astype(f32).reshape(-1, chans)
    out = feat + conv(ahead, w2, frames, rows, False) + b2
    out_ref[...] = out.astype(bf16).reshape(out_ref.shape)
    grad = conv(behind, w1, frames, rows, True)
    d_vals, d_gain = norm_silu_back(grad, feat, g1)
    gin = d_vals + jnp.where(is_odd(), give_in[...], keep_in[...]).astype(f32).reshape(-1, chans)
    gin_ref[...] = gin.astype(bf16).reshape(gin_ref.shape)
    sums_ref[...] = jnp.concatenate([d_gain, jnp.zeros((7, chans), f32)], axis=0)


def pack_rows(chans):
    return chans + chans // 2


def chunk_rows(count, chans, planes):
    unit = 16 * planes
    return -(-count * pack_rows(chans) // unit) * unit


def put_y(plane, blocks, values, row, count, gain):
    chans = plane.shape[3]
    base = jnp.where(is_odd(), 2, 0) if blocks == 2 else 0
    for b in range(blocks):
        for f in range(2):
            part = values[b, :, :, f * chans : (f + 1) * chans]
            place = (base + 2 * b + f, pl.ds(row, count))

            def odd():
                flat = part.astype(f32).reshape(-1, chans)
                plane[place] = norm_silu(flat, gain).astype(bf16).reshape(part.shape)

            def even():
                plane[place] = part

            by_core(odd, even)


def plane_kernel(blocks, *refs):
    ys, gain, plane = refs[:4], refs[4][1:2], refs[-1]
    rows = ys[0].shape[1]
    p = lax.axis_index("height") % 4
    if blocks == 2:
        plane[pl.ds(jnp.where(is_odd(), 0, 4), 2)] = jnp.zeros((2,) + plane.shape[1:], bf16)
    for d in range(4):
        put_y(plane, blocks, ys[d][...], 1 + rows * (p ^ d), rows, gain)


def wgrad_kernel(blocks, planes, *refs):
    xs, plane_in, gain = refs[:4], refs[4], refs[5][1:2]
    out_ref, plane, xk = refs[-3:]
    _, rows, cols, _ = xs[0].shape
    rows -= 1
    chans = plane.shape[3]
    tall = 4 * rows
    cells = 4 * tall * cols
    odd = is_odd()
    p = lax.axis_index("height") % 4
    plane[:, 1 : tall + 1] = plane_in[:, 1 : tall + 1]
    if blocks == 2:
        empty = jnp.zeros((2, 1, cols, chans), bf16)
        for row in (0, tall + 1):
            plane[pl.ds(jnp.where(odd, 0, 4), 2), row : row + 1] = empty
    for d in range(4):
        at = p ^ d
        for b in range(2):
            for f in range(2):
                part = xs[d][b, :rows, :, f * chans : (f + 1) * chans]
                wide = part.astype(f32)
                place = (2 * b + f, pl.ds(rows * at, rows))
                xk[(0,) + place] = shift_cols(wide, 1).astype(bf16)
                xk[(1,) + place] = part
                xk[(2,) + place] = shift_cols(wide, -1).astype(bf16)

        @pl.when(at == 0)
        def _():
            put_y(plane, blocks, xs[d][:, rows:], 0, 1, gain)

        @pl.when(at == 3)
        def _():
            put_y(plane, blocks, xs[d][:, rows:], tall + 1, 1, gain)

    step = pack_rows(chans)
    dims = (((0,), (0,)), ((), ()))
    half = chans // 2
    offset = 0
    for first, count in chunks:
        share = chunk_rows(count, chans, planes) // planes

        def put(row, values, offset=offset, share=share):
            at = 0
            while at < values.shape[0]:
                q, r = divmod(row + at, share)
                n = min(share - r, values.shape[0] - at)
                out_ref[q, offset + r : offset + r + n] = values[at : at + n]
                at += n

        def store(row, grad, put=put):
            grad = grad.astype(bf16)
            put(row, grad[:, :128])
            put(row + chans, jnp.concatenate([grad[:half, 128:], grad[half:, 128:]], axis=1))

        for j in range(count):
            tap = jnp.minimum(p * taps_each + first + j, taps_all - 1)
            t, h, k = tap // 9, tap // 3 % 3, tap % 3

            @pl.when(odd)
            def _():
                piece = plane[pl.ds(t, 4), pl.ds(h, tall)].reshape(cells, chans)
                x = xk[k].reshape(cells, chans)
                store(j * step, lax.dot_general(piece, x, dims, preferred_element_type=f32))

            @pl.when(jnp.logical_not(odd))
            def _():
                piece = plane[pl.ds(2 - t, 4), pl.ds(2 - h, tall)].reshape(cells, chans)
                x = xk[2 - k].reshape(cells, chans)
                store(j * step, lax.dot_general(x, piece, dims, preferred_element_type=f32))

        spare = share * planes - count * step
        if spare:
            put(count * step, jnp.zeros((spare, 128), bf16))
        offset += share


def halves(total):
    high = total.astype(bf16)
    return jnp.concatenate([high, (total - high.astype(f32)).astype(bf16)])


def assemble_kernel(planes, size, *refs):
    pieces, out_ref = refs[:planes], refs[-1]
    q = lax.axis_index("height") // 4
    for d, piece in enumerate(pieces):
        start = pl.multiple_of((q - d + planes) % planes * size, 16)
        out_ref[pl.ds(start, size)] = piece[:size]
    if pieces[0].shape[0] > size:
        total = functools.reduce(lambda a, b: a + b, [piece[size:].astype(f32) for piece in pieces])
        half = total.shape[0] // 2
        out_ref[planes * size :] = halves(total[:half] + total[half:])


def unpack_kernel(*refs):
    pieces, outs, more, stage, sems = refs[:-8], refs[-8:-6], refs[-6:-2], refs[-2], refs[-1]
    chans = stage.shape[1]
    half = chans // 2
    step = pack_rows(chans)
    odd = lax.axis_index("tm") % 2 == 1
    p = lax.axis_index("height") % 4
    made = []
    for n, src in enumerate(pieces):
        first, count = chunks[n // 8]
        for j in range(count):
            tap = (p ^ (n % 4)) * taps_each + first + j
            slot = len(made) // 2
            high = src[j * step + chans : (j + 1) * step]
            stage[slot, :, :128] = src[j * step : j * step + chans]
            stage[slot, :half, 128:] = high[:, : chans - 128]
            stage[slot, half:, 128:] = high[:, chans - 128 :]
            real = tap < taps_all
            tap = jnp.minimum(tap, taps_all - 1)
            for which in range(2):
                good = odd if (which == 0) == (n % 8 < 4) else jnp.logical_not(odd)
                good = jnp.logical_and(good, real)
                copy = pltpu.make_async_copy(stage.at[slot], outs[which].at[tap], sems.at[slot])
                pl.when(good)(copy.start)
                made.append((good, copy))
    if more:
        sums = functools.reduce(lambda a, b: a + b, [src[src.shape[0] - 16 :].astype(f32) for src in pieces[-8:]])
        sums = sums[:8] + sums[8:]
        for i in range(4):
            row = jnp.concatenate([sums[2 * i : 2 * i + 1], sums[2 * i + 1 : 2 * i + 2, : chans - 128]], axis=1)
            more[i][...] = row.astype(bf16)
    for good, copy in made:
        pl.when(good)(copy.wait)


vmem = pl.BlockSpec(memory_space=pltpu.VMEM)
anywhere = pl.BlockSpec(memory_space=pl.ANY)
in_hbm = pl.BlockSpec(memory_space=pltpu.HBM)


def call(kernel, outs, args, us, mib, scratch=(), free=(), hbm=(), out_specs=None, **kw):
    return pl.pallas_call(
        kernel,
        out_shape=outs,
        in_specs=[in_hbm if i in hbm else anywhere if i in free else vmem for i in range(len(args))],
        out_specs=out_specs or [vmem] * len(outs),
        scratch_shapes=list(scratch),
        compiler_params=pltpu.CompilerParams(vmem_limit_bytes=mib * 2**20),
        cost_estimate=pl.CostEstimate(flops=int(us * 1.1e9), bytes_accessed=1024, transcendentals=0),
        **kw,
    )(*args)


def moved(value, axis, by):
    size = lax.axis_size(axis)
    return lax.ppermute(value, axis, [(i, i + by) for i in range(size) if 0 <= i + by < size])


def total_of(pieces):
    return functools.reduce(lambda a, b: a + b, [p.astype(f32) for p in pieces])


def piece_at(value, index):
    return lax.dynamic_index_in_dim(value, index, 0, keepdims=False)


def body(features, weight_one, bias_one, gain_one, weight_two, bias_two, gain_two, cotangent):
    frames, rows, cols, chans = features.shape
    tm, height = lax.axis_size("tm"), lax.axis_size("height")
    planes = height // 4
    c, me = lax.axis_index("tm"), lax.axis_index("height")
    odd = c % 2 == 1
    p, q = me % 4, me // 4
    swap = [(i, i ^ 1) for i in range(tm)]
    line = lambda v: v.reshape(1, chans)
    local = jax.ShapeDtypeStruct(features.shape, bf16)
    sums = jax.ShapeDtypeStruct((8, chans), f32)
    window = pltpu.VMEM((frames + 2, rows + 2, cols, chans), bf16)
    packed_shape = jax.ShapeDtypeStruct((rows, cols, 2 * chans), bf16)

    def plane_move(value, d):
        return lax.ppermute(value, "height", [(i, i ^ d) for i in range(height)])

    def column_move(value, d):
        pairs = [(z * 4 + j, (z + d) % planes * 4 + j) for z in range(planes) for j in range(4)]
        return lax.ppermute(value, "height", pairs)

    pair = tm == 2
    blocks = 2 if pair else 3
    messages = (jax.ShapeDtypeStruct((3 if pair else 4, cols, 2 * chans), bf16),) * 2
    y_shape = jax.ShapeDtypeStruct((blocks, rows, cols, 2 * chans), bf16)
    x_shape = jax.ShapeDtypeStruct((blocks, rows + 1, cols, 2 * chans), bf16)
    raw_give, raw_keep = jnp.where(odd, cotangent, features), jnp.where(odd, features, cotangent)
    if pair:
        far = (lax.ppermute(raw_give, "tm", swap),)
        extra = ()
    else:
        far = (moved(features, "tm", 1), moved(cotangent, "tm", -1))
        extra = (lax.ppermute(jnp.where(odd, far[1], far[0]), "tm", swap),)
    held = jax.ShapeDtypeStruct(weight_one.shape, bf16)
    w1, w2, vec = call(
        fetch_kernel,
        (held, held, jax.ShapeDtypeStruct((8, chans), f32)),
        (weight_one, weight_two, line(bias_one), line(gain_one), line(bias_two), line(gain_two)),
        3,
        8,
        [pltpu.SemaphoreType.DMA((6,))],
        hbm=range(6),
    )
    y_own, up, down = call(join_first_kernel, (y_shape, *messages), (raw_keep, raw_give, *far, *extra), 1, 8)
    above, below = moved(up, "height", 1), moved(down, "height", -1)
    ys = [y_own] + [plane_move(y_own, d) for d in (1, 2, 3)]

    give, keep, sums_one = call(
        first_kernel,
        (packed_shape, packed_shape, sums),
        (*ys[1:], raw_keep, raw_give, jnp.stack(far), above, below, w1, w2, vec),
        5,
        20,
        [window, window],
        free=(0, 1, 2),
    )
    other = lax.ppermute(give, "tm", swap)
    if pair:
        (x_own,) = call(join_edge_kernel, (x_shape,), (keep, other, above, below), 1, 6)
        far = lax.ppermute(keep, "tm", swap)[None]
    else:
        edge = jnp.where(p == 0, above, below)
        extra = lax.ppermute(jnp.where(odd, edge[3], edge[0]), "tm", swap)
        edge = jnp.where(odd, jnp.stack([extra, edge[0], edge[1]]), jnp.stack([edge[2], edge[3], extra]))
        x_own = jnp.where(odd, jnp.stack([other, keep, keep]), jnp.stack([keep, other, other]))
        x_own = jnp.concatenate([x_own, edge[:, None]], axis=1)
        act2, gmid = jnp.where(odd, give, keep), jnp.where(odd, keep, give)
        far = jnp.stack([moved(act2, "tm", 1), moved(gmid, "tm", -1)])
    xs = [x_own] + [plane_move(x_own, d) for d in (1, 2, 3)]
    up, down = call(gate_kernel, messages, (keep, give, far, xs[1]), 1, 6, free=(3,))
    above, below = moved(up, "height", 1), moved(down, "height", -1)

    (plane,) = call(
        functools.partial(plane_kernel, blocks),
        (jax.ShapeDtypeStruct((2 * frames + 2, 4 * rows + 2, cols, chans), bf16),),
        (*ys, vec, x_own),
        0.1,
        8,
        free=(5,),
    )
    shares = [chunk_rows(count, chans, planes) // planes for _, count in chunks]
    (flat,) = call(
        functools.partial(wgrad_kernel, blocks, planes),
        (jax.ShapeDtypeStruct((planes, sum(shares), 128), bf16),),
        (*xs, plane, vec),
        6,
        24,
        [
            pltpu.VMEM((2 * frames + 2, 4 * rows + 2, cols, chans), bf16),
            pltpu.VMEM((3, 2 * frames, 4 * rows, cols, chans), bf16),
        ],
    )
    arrived = [column_move(piece_at(flat, (q + d) % planes), d) for d in range(1, planes)]
    part = total_of([piece_at(flat, q), *arrived])
    hop = 2
    while hop < tm:
        part = part + lax.ppermute(part, "tm", [(i, i ^ hop) for i in range(tm)])
        hop *= 2
    part = part.astype(bf16)
    parts = jnp.split(part, [sum(shares[:n]) for n in range(1, len(shares))])

    block_out, grad_input, sums_two = call(
        last_kernel,
        (local, local, sums),
        (keep, give, far, above, below, raw_keep, raw_give, w1, w2, vec),
        6,
        20,
        [window, window],
    )

    small = jnp.concatenate([sums_one[:3], sums_two[:1]])
    small = jnp.pad(small, ((0, 0), (0, -chans % 128))).reshape(-1, 128)

    hop = 2
    while hop < tm:
        small = small + lax.ppermute(small, "tm", [(i, i ^ hop) for i in range(tm)])
        hop *= 2

    gradient = jax.ShapeDtypeStruct((taps_all, chans, chans), bf16)
    final = []
    for n, (part, taps) in enumerate(zip(parts, chunks)):
        last = n == len(parts) - 1
        size = part.shape[0]
        send = jnp.concatenate([part, halves(small)]) if last else part
        got = [send] + [column_move(send, d) for d in range(1, planes)]
        (send,) = call(
            functools.partial(assemble_kernel, planes, size),
            (jax.ShapeDtypeStruct((planes * size + send.shape[0] - size, 128), bf16),),
            got,
            1,
            6,
        )
        one, two = plane_move(send, 1), plane_move(send, 2)
        cut = send.shape[0] // 32 * 16
        if False:
            three = jnp.concatenate([plane_move(two[:cut], 1), plane_move(one[cut:], 2)])
        else:
            three = plane_move(send, 3)
        got = [send, one, two, three]
        others = [lax.ppermute(g, "tm", swap) for g in got]
        final += [*got, *others]
    slots = 8 * taps_each
    grads = call(
        unpack_kernel,
        (gradient, gradient) + (jax.ShapeDtypeStruct((1, chans), bf16),) * 4,
        final,
        3,
        16,
        [pltpu.VMEM((slots, chans, chans), bf16), pltpu.SemaphoreType.DMA((slots,))],
        out_specs=[anywhere, anywhere] + [vmem] * 4,
    )
    grad_one, grad_two, *small = grads
    small = [v.reshape(chans) for v in small]
    shape = weight_one.shape
    return (
        block_out,
        grad_input,
        grad_one.reshape(shape),
        grad_two.reshape(shape),
        small[1],
        small[2],
        small[3],
        small[0],
    )


def solution(mesh):
    split = P("tm", "height", None, None)
    return jax.shard_map(
        body,
        mesh=mesh,
        in_specs=(split, P(), P(), P(), P(), P(), P(), split),
        out_specs=(split, split, P(), P(), P(), P(), P(), P()),
        check_vma=False,
    )
```

```python
import functools

import jax
import jax.numpy as jnp
from jax import lax
from jax.experimental import pallas as pl
from jax.experimental.pallas import tpu as pltpu
from jax.sharding import PartitionSpec as P

epsilon = 1e-06
bf16 = jnp.bfloat16
f32 = jnp.float32
chunks = ((0, 3), (3, 4))
taps_each = 7
taps_all = 27


def shift_cols(value, by):
    zero = jnp.zeros_like(value[:, :1])
    if by == 1:
        return jnp.concatenate([value[:, 1:], zero], axis=1)
    return jnp.concatenate([zero, value[:, :-1]], axis=1)


def norm_parts(vals, gain):
    scale = lax.rsqrt(jnp.mean(vals * vals, axis=-1, keepdims=True) + epsilon)
    normed = vals * scale
    lifted = normed * gain
    return scale, normed, lifted, jax.nn.sigmoid(lifted)


def norm_silu(vals, gain):
    _, _, lifted, sig = norm_parts(vals, gain)
    return lifted * sig


def norm_silu_back(grad, vals, gain):
    scale, normed, lifted, sig = norm_parts(vals, gain)
    d_lift = grad * sig * (1.0 + lifted * (1.0 - sig))
    d_gain = jnp.sum(d_lift * normed, axis=0, keepdims=True)
    d_norm = d_lift * gain
    d_vals = scale * (d_norm - normed * jnp.mean(d_norm * normed, axis=-1, keepdims=True))
    return d_vals, d_gain


def conv(window, weight, frames, rows, back):
    cols, chans = window.shape[2], window.shape[3]
    parts = [None] * 3
    for t in range(3):
        for h in range(3):
            t0, h0 = (2 - t, 2 - h) if back else (t, h)
            piece = window[t0 : t0 + frames, h0 : h0 + rows].reshape(frames * rows * cols, chans)
            for k in range(3):
                dims = (((1,), (1 if back else 0,)), ((), ()))
                prod = lax.dot_general(piece, weight[t, h, k], dims, preferred_element_type=f32)
                parts[k] = prod if parts[k] is None else parts[k] + prod
    parts = [part.reshape(frames * rows, cols, chans) for part in parts]
    sign = -1 if back else 1
    total = parts[1] + shift_cols(parts[0], -sign) + shift_cols(parts[2], sign)
    return total.reshape(frames * rows * cols, chans)


def is_odd():
    return lax.axis_index("tm") % 2 == 1


def by_core(odd_fn, even_fn):
    pl.when(is_odd())(odd_fn)
    pl.when(jnp.logical_not(is_odd()))(even_fn)


def fill_packed(window, at, rows, packed):
    chans = window.shape[3]
    for f in range(2):
        window[at + f, rows] = packed[..., f * chans : (f + 1) * chans]


def fill_far(ahead, behind, far, rows):
    def put(window, at, value):
        if value.shape[-1] == window.shape[3]:
            window[pl.ds(at, 2), rows] = value
        else:
            fill_packed(window, at, rows, value)

    if far.shape[0] == 2:
        put(ahead, 0, far[0])
        put(behind, 2, far[1])
        return
    zero = jnp.zeros(far.shape[1:], bf16)

    def odd():
        put(ahead, 0, far[0])
        put(behind, 2, zero)

    def even():
        put(ahead, 0, zero)
        put(behind, 2, far[0])

    by_core(odd, even)


def fill_edges(ahead, behind, above, below):
    last = ahead.shape[1] - 1
    places = ((ahead, 0), (ahead, 2), (behind, 0), (behind, 2))
    for row, edges in ((0, above), (last, below)):
        rows = pl.ds(row, 1)
        if edges.shape[0] == 4:
            for i, (window, at) in enumerate(places):
                fill_packed(window, at, rows, edges[i : i + 1])
            continue
        zero = jnp.zeros((1,) + edges.shape[1:], bf16)

        def odd():
            for i, (window, at) in enumerate(places):
                fill_packed(window, at, rows, edges[i : i + 1] if i < 3 else zero)

        def even():
            for i, (window, at) in enumerate(places):
                fill_packed(window, at, rows, edges[i - 1 : i] if i > 0 else zero)

        by_core(odd, even)


def started(copies, sems):
    made = [pltpu.make_async_copy(src, dst, sems.at[i]) for i, (src, dst) in enumerate(copies)]
    for copy in made:
        copy.start()
    return made


def pack_frames(values):
    return jnp.concatenate([values[0], values[1]], axis=-1)


def put_messages(groups, up_ref, down_ref):
    for i, value in enumerate(groups):
        up_ref[i] = value[value.shape[0] - 1]
        down_ref[i] = value[0]


def join_first_kernel(*refs):
    refs, (y_ref, up_ref, down_ref) = refs[:-3], refs[-3:]
    keep, give, *far = [pack_frames(ref) for ref in refs]
    if len(far) == 1:

        def odd():
            y_ref[0], y_ref[1] = far[0], keep
            put_messages((far[0], keep, give), up_ref, down_ref)

        def even():
            y_ref[0], y_ref[1] = keep, far[0]
            put_messages((give, keep, far[0]), up_ref, down_ref)

    else:

        def odd():
            y_ref[0], y_ref[1], y_ref[2] = far[2], far[0], keep
            put_messages((far[0], keep, give, far[1]), up_ref, down_ref)

        def even():
            y_ref[0], y_ref[1], y_ref[2] = keep, far[1], far[2]
            put_messages((far[0], give, keep, far[1]), up_ref, down_ref)

    by_core(odd, even)


def gate_kernel(keep_ref, give_ref, far_ref, _, up_ref, down_ref):
    keep, give, far = keep_ref[...], give_ref[...], far_ref[...]

    def odd():
        put_messages((far[0], give, keep, far[-1])[: up_ref.shape[0]], up_ref, down_ref)

    def even():
        put_messages((far[0], keep, give, far[-1])[4 - up_ref.shape[0] :], up_ref, down_ref)

    by_core(odd, even)


def join_edge_kernel(keep_ref, other_ref, above_ref, below_ref, out_ref):
    rows = keep_ref.shape[0]
    top = lax.axis_index("height") % 4 == 0
    edge = jnp.where(top, above_ref[...], below_ref[...])

    def odd():
        out_ref[0, :rows], out_ref[1, :rows] = other_ref[...], keep_ref[...]
        out_ref[0, rows], out_ref[1, rows] = edge[0], edge[1]

    def even():
        out_ref[0, :rows], out_ref[1, :rows] = keep_ref[...], other_ref[...]
        out_ref[0, rows], out_ref[1, rows] = edge[1], edge[2]

    by_core(odd, even)


def fetch_kernel(w1_any, w2_any, b1_any, g1_any, b2_any, g2_any, w1_ref, w2_ref, vec_ref, sems):
    vectors = [(ref, vec_ref.at[pl.ds(i, 1)]) for i, ref in enumerate((b1_any, g1_any, b2_any, g2_any))]
    for copy in started([(w1_any, w1_ref), (w2_any, w2_ref), *vectors], sems):
        copy.wait()


def first_kernel(
    _, __, ___, keep_in, give_in, far_ref, above_ref, below_ref, w1, w2, vec_ref,
    give_ref, keep_ref, sums_ref, ahead, behind,
):
    frames, rows, cols, chans = keep_in.shape
    own = pl.ds(1, rows)
    b1, g1, g2 = vec_ref[0:1], vec_ref[1:2], vec_ref[3:4]

    def odd_in():
        ahead[pl.ds(2, 2), own] = keep_in[...]
        behind[pl.ds(0, 2), own] = give_in[...]

    def even_in():
        ahead[pl.ds(2, 2), own] = give_in[...]
        behind[pl.ds(0, 2), own] = keep_in[...]

    by_core(odd_in, even_in)
    fill_far(ahead, behind, far_ref, own)
    fill_edges(ahead, behind, above_ref, below_ref)
    for f in range(frames + 2):
        vals = ahead[f].astype(f32).reshape(-1, chans)
        ahead[f] = norm_silu(vals, g1).astype(bf16).reshape(rows + 2, cols, chans)
    mid = (conv(ahead, w1, frames, rows, False) + b1).astype(bf16).astype(f32)
    act2 = norm_silu(mid, g2).astype(bf16).reshape(frames, rows, cols, chans)
    act2 = pack_frames(act2)
    grad = conv(behind, w2, frames, rows, True)
    gmid, d_gain = norm_silu_back(grad, mid, g2)
    gmid = gmid.astype(bf16)
    cot = behind[:2, 1 : rows + 1].astype(f32).reshape(-1, chans)
    sums_ref[...] = jnp.concatenate(
        [
            d_gain,
            jnp.sum(gmid.astype(f32), axis=0, keepdims=True),
            jnp.sum(cot, axis=0, keepdims=True),
            jnp.zeros((5, chans), f32),
        ],
        axis=0,
    )
    gmid = pack_frames(gmid.reshape(frames, rows, cols, chans))

    def odd():
        give_ref[...] = act2
        keep_ref[...] = gmid

    def even():
        give_ref[...] = gmid
        keep_ref[...] = act2

    by_core(odd, even)


def last_kernel(
    keep_ref, give_ref, far_ref, above_ref, below_ref, keep_in, give_in, w1, w2, vec_ref,
    out_ref, gin_ref, sums_ref, ahead, behind,
):
    frames, rows, cols, chans = out_ref.shape
    own = pl.ds(1, rows)
    g1, b2 = vec_ref[1:2], vec_ref[2:3]

    def odd():
        fill_packed(ahead, 2, own, give_ref[...])
        fill_packed(behind, 0, own, keep_ref[...])

    def even():
        fill_packed(ahead, 2, own, keep_ref[...])
        fill_packed(behind, 0, own, give_ref[...])

    by_core(odd, even)
    fill_far(ahead, behind, far_ref, own)
    fill_edges(ahead, behind, above_ref, below_ref)
    feat = jnp.where(is_odd(), keep_in[...], give_in[...]).astype(f32).reshape(-1, chans)
    out = feat + conv(ahead, w2, frames, rows, False) + b2
    out_ref[...] = out.astype(bf16).reshape(out_ref.shape)
    grad = conv(behind, w1, frames, rows, True)
    d_vals, d_gain = norm_silu_back(grad, feat, g1)
    gin = d_vals + jnp.where(is_odd(), give_in[...], keep_in[...]).astype(f32).reshape(-1, chans)
    gin_ref[...] = gin.astype(bf16).reshape(gin_ref.shape)
    sums_ref[...] = jnp.concatenate([d_gain, jnp.zeros((7, chans), f32)], axis=0)


def pack_rows(chans):
    return chans + chans // 2


def chunk_rows(count, chans, planes):
    unit = 16 * planes
    return -(-count * pack_rows(chans) // unit) * unit


def put_y(plane, blocks, values, row, count, gain):
    chans = plane.shape[3]
    base = jnp.where(is_odd(), 2, 0) if blocks == 2 else 0
    for b in range(blocks):
        for f in range(2):
            part = values[b, :, :, f * chans : (f + 1) * chans]
            place = (base + 2 * b + f, pl.ds(row, count))

            def odd():
                flat = part.astype(f32).reshape(-1, chans)
                plane[place] = norm_silu(flat, gain).astype(bf16).reshape(part.shape)

            def even():
                plane[place] = part

            by_core(odd, even)


def plane_kernel(blocks, *refs):
    ys, gain, plane = refs[:4], refs[4][1:2], refs[-1]
    rows = ys[0].shape[1]
    p = lax.axis_index("height") % 4
    if blocks == 2:
        plane[pl.ds(jnp.where(is_odd(), 0, 4), 2)] = jnp.zeros((2,) + plane.shape[1:], bf16)
    for d in range(4):
        put_y(plane, blocks, ys[d][...], 1 + rows * (p ^ d), rows, gain)


def wgrad_kernel(blocks, planes, *refs):
    xs, plane_in, gain = refs[:4], refs[4], refs[5][1:2]
    out_ref, plane, xk = refs[-3:]
    _, rows, cols, _ = xs[0].shape
    rows -= 1
    chans = plane.shape[3]
    tall = 4 * rows
    cells = 4 * tall * cols
    odd = is_odd()
    p = lax.axis_index("height") % 4
    plane[:, 1 : tall + 1] = plane_in[:, 1 : tall + 1]
    if blocks == 2:
        empty = jnp.zeros((2, 1, cols, chans), bf16)
        for row in (0, tall + 1):
            plane[pl.ds(jnp.where(odd, 0, 4), 2), row : row + 1] = empty
    for d in range(4):
        at = p ^ d
        for b in range(2):
            for f in range(2):
                part = xs[d][b, :rows, :, f * chans : (f + 1) * chans]
                wide = part.astype(f32)
                place = (2 * b + f, pl.ds(rows * at, rows))
                xk[(0,) + place] = shift_cols(wide, 1).astype(bf16)
                xk[(1,) + place] = part
                xk[(2,) + place] = shift_cols(wide, -1).astype(bf16)

        @pl.when(at == 0)
        def _():
            put_y(plane, blocks, xs[d][:, rows:], 0, 1, gain)

        @pl.when(at == 3)
        def _():
            put_y(plane, blocks, xs[d][:, rows:], tall + 1, 1, gain)

    step = pack_rows(chans)
    dims = (((0,), (0,)), ((), ()))
    half = chans // 2
    offset = 0
    for first, count in chunks:
        share = chunk_rows(count, chans, planes) // planes

        def put(row, values, offset=offset, share=share):
            at = 0
            while at < values.shape[0]:
                q, r = divmod(row + at, share)
                n = min(share - r, values.shape[0] - at)
                out_ref[q, offset + r : offset + r + n] = values[at : at + n]
                at += n

        def store(row, grad, put=put):
            grad = grad.astype(bf16)
            put(row, grad[:, :128])
            put(row + chans, jnp.concatenate([grad[:half, 128:], grad[half:, 128:]], axis=1))

        for j in range(count):
            tap = jnp.minimum(p * taps_each + first + j, taps_all - 1)
            t, h, k = tap // 9, tap // 3 % 3, tap % 3

            @pl.when(odd)
            def _():
                piece = plane[pl.ds(t, 4), pl.ds(h, tall)].reshape(cells, chans)
                x = xk[k].reshape(cells, chans)
                store(j * step, lax.dot_general(piece, x, dims, preferred_element_type=f32))

            @pl.when(jnp.logical_not(odd))
            def _():
                piece = plane[pl.ds(2 - t, 4), pl.ds(2 - h, tall)].reshape(cells, chans)
                x = xk[2 - k].reshape(cells, chans)
                store(j * step, lax.dot_general(x, piece, dims, preferred_element_type=f32))

        spare = share * planes - count * step
        if spare:
            put(count * step, jnp.zeros((spare, 128), bf16))
        offset += share


def halves(total):
    high = total.astype(bf16)
    return jnp.concatenate([high, (total - high.astype(f32)).astype(bf16)])


def assemble_kernel(planes, size, *refs):
    pieces, out_ref = refs[:planes], refs[-1]
    q = lax.axis_index("height") // 4
    for d, piece in enumerate(pieces):
        start = pl.multiple_of((q - d + planes) % planes * size, 16)
        out_ref[pl.ds(start, size)] = piece[:size]
    if pieces[0].shape[0] > size:
        total = functools.reduce(lambda a, b: a + b, [piece[size:].astype(f32) for piece in pieces])
        half = total.shape[0] // 2
        out_ref[planes * size :] = halves(total[:half] + total[half:])


def unpack_kernel(taps, held, *refs):
    pieces = refs[:8]
    outs, stage, sems = refs[8 + 2 * held : 10 + 2 * held], refs[-2], refs[-1]
    first, count = taps
    chans = stage.shape[1]
    half = chans // 2
    step = pack_rows(chans)
    odd = lax.axis_index("tm") % 2 == 1
    p = lax.axis_index("height") % 4
    made = []
    for n, src in enumerate(pieces):
        for j in range(count):
            tap = (p ^ (n % 4)) * taps_each + first + j
            slot = n * count + j
            high = src[j * step + chans : (j + 1) * step]
            stage[slot, :, :128] = src[j * step : j * step + chans]
            stage[slot, :half, 128:] = high[:, : chans - 128]
            stage[slot, half:, 128:] = high[:, chans - 128 :]
            real = tap < taps_all
            tap = jnp.minimum(tap, taps_all - 1)
            for which in range(2):
                good = odd if (which == 0) == (n < 4) else jnp.logical_not(odd)
                good = jnp.logical_and(good, real)
                copy = pltpu.make_async_copy(stage.at[slot], outs[which].at[tap], sems.at[slot])
                pl.when(good)(copy.start)
                made.append((good, copy))
    for good, copy in made:
        pl.when(good)(copy.wait)


vmem = pl.BlockSpec(memory_space=pltpu.VMEM)
anywhere = pl.BlockSpec(memory_space=pl.ANY)
in_hbm = pl.BlockSpec(memory_space=pltpu.HBM)


def call(kernel, outs, args, us, mib, scratch=(), free=(), hbm=(), out_spec=vmem, **kw):
    return pl.pallas_call(
        kernel,
        out_shape=outs,
        in_specs=[in_hbm if i in hbm else anywhere if i in free else vmem for i in range(len(args))],
        out_specs=[out_spec] * len(outs),
        scratch_shapes=list(scratch),
        compiler_params=pltpu.CompilerParams(vmem_limit_bytes=mib * 2**20),
        cost_estimate=pl.CostEstimate(flops=int(us * 1.1e9), bytes_accessed=1024, transcendentals=0),
        **kw,
    )(*args)


def moved(value, axis, by):
    size = lax.axis_size(axis)
    return lax.ppermute(value, axis, [(i, i + by) for i in range(size) if 0 <= i + by < size])


def total_of(pieces):
    return functools.reduce(lambda a, b: a + b, [p.astype(f32) for p in pieces])


def piece_at(value, index):
    return lax.dynamic_index_in_dim(value, index, 0, keepdims=False)


def body(features, weight_one, bias_one, gain_one, weight_two, bias_two, gain_two, cotangent):
    frames, rows, cols, chans = features.shape
    tm, height = lax.axis_size("tm"), lax.axis_size("height")
    planes = height // 4
    c, me = lax.axis_index("tm"), lax.axis_index("height")
    odd = c % 2 == 1
    p, q = me % 4, me // 4
    swap = [(i, i ^ 1) for i in range(tm)]
    line = lambda v: v.reshape(1, chans)
    local = jax.ShapeDtypeStruct(features.shape, bf16)
    sums = jax.ShapeDtypeStruct((8, chans), f32)
    window = pltpu.VMEM((frames + 2, rows + 2, cols, chans), bf16)
    packed_shape = jax.ShapeDtypeStruct((rows, cols, 2 * chans), bf16)

    def plane_move(value, d):
        return lax.ppermute(value, "height", [(i, i ^ d) for i in range(height)])

    def column_move(value, d):
        pairs = [(z * 4 + j, (z + d) % planes * 4 + j) for z in range(planes) for j in range(4)]
        return lax.ppermute(value, "height", pairs)

    pair = tm == 2
    blocks = 2 if pair else 3
    messages = (jax.ShapeDtypeStruct((3 if pair else 4, cols, 2 * chans), bf16),) * 2
    y_shape = jax.ShapeDtypeStruct((blocks, rows, cols, 2 * chans), bf16)
    x_shape = jax.ShapeDtypeStruct((blocks, rows + 1, cols, 2 * chans), bf16)
    raw_give, raw_keep = jnp.where(odd, cotangent, features), jnp.where(odd, features, cotangent)
    if pair:
        far = (lax.ppermute(raw_give, "tm", swap),)
        extra = ()
    else:
        far = (moved(features, "tm", 1), moved(cotangent, "tm", -1))
        extra = (lax.ppermute(jnp.where(odd, far[1], far[0]), "tm", swap),)
    held = jax.ShapeDtypeStruct(weight_one.shape, bf16)
    w1, w2, vec = call(
        fetch_kernel,
        (held, held, jax.ShapeDtypeStruct((8, chans), f32)),
        (weight_one, weight_two, line(bias_one), line(gain_one), line(bias_two), line(gain_two)),
        3,
        8,
        [pltpu.SemaphoreType.DMA((6,))],
        hbm=range(6),
    )
    y_own, up, down = call(join_first_kernel, (y_shape, *messages), (raw_keep, raw_give, *far, *extra), 1, 8)
    above, below = moved(up, "height", 1), moved(down, "height", -1)
    ys = [y_own] + [plane_move(y_own, d) for d in (1, 2, 3)]

    give, keep, sums_one = call(
        first_kernel,
        (packed_shape, packed_shape, sums),
        (*ys[1:], raw_keep, raw_give, jnp.stack(far), above, below, w1, w2, vec),
        5,
        20,
        [window, window],
        free=(0, 1, 2),
    )
    other = lax.ppermute(give, "tm", swap)
    if pair:
        (x_own,) = call(join_edge_kernel, (x_shape,), (keep, other, above, below), 1, 6)
        far = lax.ppermute(keep, "tm", swap)[None]
    else:
        edge = jnp.where(p == 0, above, below)
        extra = lax.ppermute(jnp.where(odd, edge[3], edge[0]), "tm", swap)
        edge = jnp.where(odd, jnp.stack([extra, edge[0], edge[1]]), jnp.stack([edge[2], edge[3], extra]))
        x_own = jnp.where(odd, jnp.stack([other, keep, keep]), jnp.stack([keep, other, other]))
        x_own = jnp.concatenate([x_own, edge[:, None]], axis=1)
        act2, gmid = jnp.where(odd, give, keep), jnp.where(odd, keep, give)
        far = jnp.stack([moved(act2, "tm", 1), moved(gmid, "tm", -1)])
    xs = [x_own] + [plane_move(x_own, d) for d in (1, 2, 3)]
    up, down = call(gate_kernel, messages, (keep, give, far, xs[1]), 1, 6, free=(3,))
    above, below = moved(up, "height", 1), moved(down, "height", -1)

    (plane,) = call(
        functools.partial(plane_kernel, blocks),
        (jax.ShapeDtypeStruct((2 * frames + 2, 4 * rows + 2, cols, chans), bf16),),
        (*ys, vec, x_own),
        0.1,
        8,
        free=(5,),
    )
    shares = [chunk_rows(count, chans, planes) // planes for _, count in chunks]
    (flat,) = call(
        functools.partial(wgrad_kernel, blocks, planes),
        (jax.ShapeDtypeStruct((planes, sum(shares), 128), bf16),),
        (*xs, plane, vec),
        6,
        24,
        [
            pltpu.VMEM((2 * frames + 2, 4 * rows + 2, cols, chans), bf16),
            pltpu.VMEM((3, 2 * frames, 4 * rows, cols, chans), bf16),
        ],
    )
    arrived = [column_move(piece_at(flat, (q + d) % planes), d) for d in range(1, planes)]
    part = total_of([piece_at(flat, q), *arrived])
    hop = 2
    while hop < tm:
        part = part + lax.ppermute(part, "tm", [(i, i ^ hop) for i in range(tm)])
        hop *= 2
    part = part.astype(bf16)
    parts = jnp.split(part, [sum(shares[:n]) for n in range(1, len(shares))])

    block_out, grad_input, sums_two = call(
        last_kernel,
        (local, local, sums),
        (keep, give, far, above, below, raw_keep, raw_give, w1, w2, vec),
        6,
        20,
        [window, window],
    )

    small = jnp.concatenate([sums_one[:3], sums_two[:1]]).reshape(-1, 128)
    used = small.shape[0]
    count = -(-used // 8) * 8
    small = jnp.pad(small, ((0, count - used), (0, 0)))

    hop = 2
    while hop < tm:
        small = small + lax.ppermute(small, "tm", [(i, i ^ hop) for i in range(tm)])
        hop *= 2

    gradient = jax.ShapeDtypeStruct((taps_all, chans, chans), bf16)
    grads, gate = (), ()
    for n, (part, taps) in enumerate(zip(parts, chunks)):
        last = n == len(parts) - 1
        size = part.shape[0]
        send = jnp.concatenate([part, halves(small)]) if last else part
        got = [send] + [column_move(send, d) for d in range(1, planes)]
        (send,) = call(
            functools.partial(assemble_kernel, planes, size),
            (jax.ShapeDtypeStruct((planes * size + send.shape[0] - size, 128), bf16),),
            got,
            1,
            6,
        )
        one, two = plane_move(send, 1), plane_move(send, 2)
        cut = send.shape[0] // 32 * 16
        if False:
            three = jnp.concatenate([plane_move(two[:cut], 1), plane_move(one[cut:], 2)])
        else:
            three = plane_move(send, 3)
        got = [send, one, two, three]
        others = [lax.ppermute(g, "tm", swap) for g in got]
        if last:
            small = total_of([v[planes * size :] for v in got + others])
            small = (small[:count] + small[count:])[:used]
        held = len(grads) > 0
        grads = call(
            functools.partial(unpack_kernel, taps, held),
            (gradient, gradient),
            (*got, *others, *grads),
            2,
            12,
            [pltpu.VMEM((8 * taps[1], chans, chans), bf16), pltpu.SemaphoreType.DMA((8 * taps[1],))],
            free=(8, 9) if held else (),
            out_spec=anywhere,
            input_output_aliases={8: 0, 9: 1} if held else {},
        )
    grad_one, grad_two = grads
    shape = weight_one.shape
    small = small.reshape(4, chans).astype(bf16)
    return (
        block_out,
        grad_input,
        grad_one.reshape(shape),
        grad_two.reshape(shape),
        small[1],
        small[2],
        small[3],
        small[0],
    )


def solution(mesh):
    split = P("tm", "height", None, None)
    return jax.shard_map(
        body,
        mesh=mesh,
        in_specs=(split, P(), P(), P(), P(), P(), P(), split),
        out_specs=(split, split, P(), P(), P(), P(), P(), P()),
        check_vma=False,
    )
```
